32 devices in a mesh: section: 2 (over core), fsdp: 4 (over y, x), dp: 4 (over z).
Axes of the slice: x: 2, y: 2, z: 4, core: 2. Of those that a mesh axis runs over, the one named last changes fastest.
Arguments:
- tokens: bfloat16 [16, 2, 512, 576], P(('fsdp', 'dp')), may hold values from -6 to 6
- cotangent: bfloat16 [16, 2, 512, 576], P(('fsdp', 'dp')), may hold values from -6 to 6
- doc_lengths: int32 [16, 2, 3], P(('fsdp', 'dp')), may hold values from 1 to 384, 512 in all within a row
- w_query: bfloat16 [2, 576, 576], P('section', 'fsdp'), may hold values from -0.25 to 0.25
- w_key: bfloat16 [2, 576, 192], P('section', 'fsdp'), may hold values from -0.25 to 0.25
- w_value: bfloat16 [2, 576, 192], P('section', 'fsdp'), may hold values from -0.25 to 0.25
- w_out: bfloat16 [2, 576, 576], P('section', 'fsdp'), may hold values from -1 to 1
- w_gate: bfloat16 [2, 576, 1536], P('section', 'fsdp'), may hold values from -0.25 to 0.25
- w_up: bfloat16 [2, 576, 1536], P('section', 'fsdp'), may hold values from -0.25 to 0.25
- w_down: bfloat16 [2, 1536, 576], P('section', 'fsdp'), may hold values from -0.15625 to 0.15625
- gain_attn: bfloat16 [2, 576], P('section', 'fsdp'), may hold values from 0.5 to 1.5
- gain_ffn: bfloat16 [2, 576], P('section', 'fsdp'), may hold values from 0.5 to 1.5
Outputs:
- section_out: bfloat16 [2, 16, 2, 512, 576], P('section', ('fsdp', 'dp'))
- in_grad: float32 [2, 16, 2, 512, 576], P('section', ('fsdp', 'dp'))
- grad_query: float32 [2, 576, 576], P('section', 'fsdp')
- grad_key: float32 [2, 576, 192], P('section', 'fsdp')
- grad_value: float32 [2, 576, 192], P('section', 'fsdp')
- grad_out: float32 [2, 576, 576], P('section', 'fsdp')
- grad_gate: float32 [2, 576, 1536], P('section', 'fsdp')
- grad_up: float32 [2, 576, 1536], P('section', 'fsdp')
- grad_down: float32 [2, 1536, 576], P('section', 'fsdp')
- grad_gain_attn: float32 [2, 576], P('section', 'fsdp')
- grad_gain_ffn: float32 [2, 576], P('section', 'fsdp')
The draws below stay inside these ranges and needn't reach their ends.
Inputs may be any that keep to these rules, and one draw needn't show every extreme that they name: `doc_lengths`: each row of 3 lengths sums to 512, and its largest is 384.
All inputs are finite; a program needn't handle non-finite values.
Results may differ from the reference program's by a relative error of at most 0.025.
Values may be sent and summed in bfloat16 or wider, within the bound.
No kernel may reach another device: no remote copies, remote signals or barrier semaphores. Data moves between devices by JAX's collectives and lax.ppermute only.
A program may use at most 256 MiB of HBM per device.

```python
import math
import jax
import jax.numpy as jnp
import numpy as np
from jax import lax

D = 576
FF = 1536
HEADS = 9
KV_HEADS = 3
HEAD = 64
MICRO = 2
ROW = 512
LONGEST = 384
NDOC = 3
KVW = 192
SAMPLES = 16


def block_levels(key, dims, cuts, low, high):
    def one(dim, parts):
        heights = jax.random.uniform(jax.random.fold_in(jax.random.fold_in(key, 6), dim), (parts,), jnp.float32, low / len(cuts), high / len(cuts))
        return jnp.repeat(jnp.exp(heights), dims[dim] // parts).reshape((-1,) + (1,) * (len(dims) - dim - 1))

    gain = one(*cuts[0])
    for cut in cuts[1:]:
        gain = gain * one(*cut)
    return gain


def profile(count, total, most, slope):
    portions = [(1 << 20) // math.isqrt(grade ** slope) + 1 for grade in range(2, count + 1)]
    rest, holding = total - most - (count - 1), [1] * (count - 1)
    while rest > 0:
        candidates = [i for i in range(count - 1) if holding[i] < most]
        pool, left = sum([portions[i] for i in candidates]), rest
        for i in candidates:
            more = min(most - holding[i], max(1, left * portions[i] // pool), rest)
            holding[i] = holding[i] + more
            rest = rest - more
    return np.array([most] + holding)


def uneven_parts(rng, amount, total, bound, lean):
    if amount == 2:
        one = jax.random.randint(rng, (), max(1, total - bound), min(bound, total - 1) + 1)
        return jnp.stack([one, total - one])
    sizes = jnp.asarray(profile(amount, total, bound, lean), jnp.int32)
    twos = (amount - 1) // 2
    giver, taker = sizes[1:1 + 2 * twos:2], sizes[2:2 + 2 * twos:2]
    slack = jnp.minimum(giver - 1, bound - taker)
    passed = jax.random.randint(jax.random.fold_in(rng, 1), (twos,), 0, 1 << 20) % (slack + 1)
    sizes = sizes.at[1:1 + 2 * twos:2].set(giver - passed).at[2:2 + 2 * twos:2].set(taker + passed)
    return sizes[jax.random.permutation(jax.random.fold_in(rng, 2), amount)]


def noise(stream_key, dims, deviation, reach, cuts=(), kind=jnp.bfloat16):
    gain = block_levels(stream_key, dims, cuts, -0.22, 0.18) if cuts else 1.0
    values = jax.random.normal(stream_key, dims, jnp.float32) * deviation * gain
    return jnp.minimum(jnp.maximum(values, -reach), reach).astype(kind)


def setup_inputs(seed: int = 0) -> dict:
    arg_keys = jax.random.split(jax.random.key(seed), 13)
    return {
        "tokens": noise(arg_keys[0], (SAMPLES, MICRO, ROW, D), 1.0, 6.0, ((0, 16),)),
        "cotangent": noise(arg_keys[1], (SAMPLES, MICRO, ROW, D), 1.0, 6.0, ((0, 16),)),
        "doc_lengths": jax.vmap(lambda own: uneven_parts(own, NDOC, ROW, LONGEST, 2))(jax.random.split(arg_keys[2], SAMPLES * MICRO)).reshape((SAMPLES, MICRO, NDOC)).astype(jnp.int32),
        "w_query": noise(arg_keys[3], (2, D, D), D ** -0.5, 0.25, ((0, 2), (1, 4))),
        "w_key": noise(arg_keys[4], (2, D, KVW), D ** -0.5, 0.25, ((0, 2), (1, 4))),
        "w_value": noise(arg_keys[5], (2, D, KVW), D ** -0.5, 0.25, ((0, 2), (1, 4))),
        "w_out": noise(arg_keys[6], (2, D, D), (D // 16) ** -0.5, 1.0, ((0, 2), (1, 4))),
        "w_gate": noise(arg_keys[7], (2, D, FF), D ** -0.5, 0.25, ((0, 2), (1, 4))),
        "w_up": noise(arg_keys[8], (2, D, FF), D ** -0.5, 0.25, ((0, 2), (1, 4))),
        "w_down": noise(arg_keys[9], (2, FF, D), FF ** -0.5, 0.15625, ((0, 2), (1, 4))),
        "gain_attn": jnp.clip(1.0 + 0.1 * jax.random.normal(arg_keys[10], (2, D), jnp.float32), 0.5, 1.5).astype(jnp.bfloat16),
        "gain_ffn": jnp.clip(1.0 + 0.1 * jax.random.normal(arg_keys[11], (2, D), jnp.float32), 0.5, 1.5).astype(jnp.bfloat16),
    }


@jax.custom_vjp
def low(v):
    return lax.optimization_barrier(v.astype(jnp.bfloat16)).astype(jnp.float32)

@jax.custom_vjp
def low_back(v):
    return v

def low_keep(v):
    return (low(v), None)

def low_pass(kept, grad):
    return (grad,)

def back_keep(v):
    return (v, None)

def back_low(kept, grad):
    return (low(grad),)
low.defvjp(low_keep, low_pass)
low_back.defvjp(back_keep, back_low)
epsilon = 1e-05
rope_base = 100000.0
masked_score = -1e+30

def matmul(left_side, right_side):
    return jnp.dot(left_side, right_side, precision=lax.Precision.HIGHEST, preferred_element_type=jnp.float32)

def normalize(values, gain_vector):
    mean_square = lax.optimization_barrier(jnp.mean(values * values, axis=-1, keepdims=True))
    return values * lax.rsqrt(mean_square + epsilon) * gain_vector

def tables(lengths, row_count, head_size):
    lengths = lengths.astype(jnp.int32)
    doc_ends = jnp.cumsum(lengths).astype(jnp.int32)
    doc_starts = (doc_ends - lengths).astype(jnp.int32)
    places = jnp.arange(row_count, dtype=jnp.int32)
    document = lax.optimization_barrier(jnp.sum((places[:, None] >= doc_ends[None, :]).astype(jnp.int32), axis=1)).astype(jnp.int32)
    inside = document[:, None] == jnp.arange(lengths.shape[0], dtype=jnp.int32)[None, :]
    opening = lax.optimization_barrier(jnp.sum(jnp.where(inside, doc_starts[None, :], 0), axis=1)).astype(jnp.int32)
    position = (places - opening).astype(jnp.float32)
    half_size = head_size // 2
    frequency = rope_base ** (-(jnp.arange(half_size, dtype=jnp.float32) * 2.0 / head_size))
    angles = position[:, None] * frequency[None, :]
    cos_table = jnp.concatenate([jnp.cos(angles), jnp.cos(angles)], axis=1)
    sin_table = jnp.concatenate([jnp.sin(angles), jnp.sin(angles)], axis=1)
    return (document, cos_table, sin_table)

def rotate(values, cos_table, sin_table):
    half_size = values.shape[-1] // 2
    turned = jnp.concatenate([-values[..., half_size:], values[..., :half_size]], axis=-1)
    return values * cos_table[:, None, :] + turned * sin_table[:, None, :]

def attend(queries, keys, values, document):
    row_count = queries.shape[0]
    block_rows = min(512, row_count)
    groups = HEADS // KV_HEADS
    scale = HEAD ** (-0.5)
    places = jnp.arange(row_count, dtype=jnp.int32)
    outputs = []
    for offset in range(0, row_count, block_rows):
        finish = offset + block_rows
        allowed = (document[offset:finish, None] == document[None, :finish]) & (places[offset:finish, None] >= places[None, :finish])

        def block_attend(query_block, key_block, value_block):
            query_groups = query_block.reshape(block_rows, KV_HEADS, groups, HEAD)
            scores = jnp.einsum('qkgd,tkd->kgqt', query_groups, key_block, precision=lax.Precision.HIGHEST) * scale
            scores = low_back(scores)
            scores = jnp.where(allowed[None, None], scores, masked_score)
            row_max = lax.optimization_barrier(jnp.max(scores, axis=-1, keepdims=True))
            exponent = jnp.exp(scores - row_max)
            probability = exponent / lax.optimization_barrier(jnp.sum(exponent, axis=-1, keepdims=True))
            mixed = jnp.einsum('kgqt,tkd->qkgd', low(probability), value_block, precision=lax.Precision.HIGHEST)
            return mixed.reshape(block_rows, HEADS * HEAD)
        outputs.append(jax.checkpoint(block_attend)(queries[offset:finish], keys[:finish], values[:finish]))
    return jnp.concatenate(outputs, axis=0)

def layer(inputs, layer_weights, document, cos_table, sin_table):
    query_weight, key_weight, value_weight, out_weight, gate_weight, up_weight, down_weight, attn_gain, ffn_gain = layer_weights
    row_count = inputs.shape[0]
    first_in = low(normalize(inputs, attn_gain))
    queries = low_back(matmul(first_in, query_weight)).reshape(row_count, HEADS, HEAD)
    keys = low_back(matmul(first_in, key_weight)).reshape(row_count, KV_HEADS, HEAD)
    values = low(low_back(matmul(first_in, value_weight))).reshape(row_count, KV_HEADS, HEAD)
    queries = low(rotate(queries, cos_table, sin_table))
    keys = low(rotate(keys, cos_table, sin_table))
    attended = low_back(low(attend(queries, keys, values, document)))
    middle = inputs + low_back(matmul(attended, out_weight))
    second_in = low(normalize(middle, ffn_gain))
    gate = low_back(matmul(second_in, gate_weight))
    upward = low_back(matmul(second_in, up_weight))
    hidden = low(gate * jax.nn.sigmoid(gate) * upward)
    return middle + low_back(matmul(hidden, down_weight))

def reference(tokens, cotangent, doc_lengths, w_query, w_key, w_value, w_out, w_gate, w_up, w_down, gain_attn, gain_ffn):
    weights = tuple((array.astype(jnp.float32) for array in (w_query, w_key, w_value, w_out, w_gate, w_up, w_down, gain_attn, gain_ffn)))
    token_rows = tokens.astype(jnp.float32).reshape(SAMPLES * MICRO, ROW, D)
    cot_rows = cotangent.astype(jnp.float32).reshape(SAMPLES * MICRO, ROW, D)
    length_rows = doc_lengths.reshape(SAMPLES * MICRO, NDOC).astype(jnp.int32)

    def step(totals, inputs):
        block_in, block_cot, lengths = inputs
        document, cos_table, sin_table = tables(lengths, ROW, HEAD)

        def whole(first_in, shift_in, all_weights):
            first_weights = tuple((array[0] for array in all_weights))
            second_weights = tuple((array[1] for array in all_weights))
            middle = low_back(low(layer(first_in, first_weights, document, cos_table, sin_table))) + shift_in
            final = layer(middle, second_weights, document, cos_table, sin_table)
            return (middle, final)
        (middle, final), pullback = jax.vjp(whole, block_in, jnp.zeros_like(block_in), weights)
        grad_first, grad_middle, grad_weights = pullback((jnp.zeros_like(middle), block_cot))
        totals = tuple((held + added for held, added in zip(totals, grad_weights)))
        return (totals, (middle.astype(jnp.bfloat16), final.astype(jnp.bfloat16), grad_first, grad_middle))
    initial = tuple((jnp.zeros_like(array) for array in weights))
    totals, (middles, finals, grads_first, grads_middle) = lax.scan(step, initial, (token_rows, cot_rows, length_rows))
    section_out = jnp.stack([middles, finals]).reshape(2, SAMPLES, MICRO, ROW, D)
    in_grad = jnp.stack([grads_first, grads_middle]).reshape(2, SAMPLES, MICRO, ROW, D)
    return (section_out, in_grad, totals[0], totals[1], totals[2], totals[3], totals[4], totals[5], totals[6], totals[7], totals[8])
```

```python
import functools
import jax
import jax.numpy as jnp
from jax import lax
from jax.experimental import pallas as pl
from jax.experimental.pallas import tpu as pltpu
from jax.sharding import PartitionSpec as P

HEADS = 9
KV_HEADS = 3
GROUP = HEADS // KV_HEADS
HEAD = 64
HALF = HEAD // 2

epsilon = 1e-05
rope_base = 100000.0
masked_score = -1e30
SCALE = HEAD ** (-0.5)
F32 = jnp.float32
BF16 = jnp.bfloat16


def nn(left, right):
    return lax.dot_general(left, right, (((1,), (0,)), ((), ())), preferred_element_type=F32)


def nt(left, right):
    return lax.dot_general(left, right, (((1,), (1,)), ((), ())), preferred_element_type=F32)


def tn(left, right):
    return lax.dot_general(left, right, (((0,), (0,)), ((), ())), preferred_element_type=F32)


def inverse_root(values):
    return lax.rsqrt(jnp.mean(values * values, axis=-1, keepdims=True) + epsilon)


def norm_back(values, inv_root, gain, upstream):
    gain_grad = jnp.sum(upstream * values * inv_root, axis=0, keepdims=True)
    scaled = upstream * gain
    dot = jnp.mean(scaled * values, axis=-1, keepdims=True)
    return inv_root * scaled - values * (inv_root * inv_root * inv_root * dot), gain_grad


def sigmoid(values):
    return 0.5 * jnp.tanh(0.5 * values) + 0.5


def copies(plan, sems):
    started = []
    for number, (source, target) in enumerate(plan):
        one = pltpu.make_async_copy(source, target, sems.at[number])
        one.start()
        started.append(one)
    return started


def spread(place, mine, theirs, buffer, rows):
    sec = place[0]
    plan = []
    for side, pieces in ((sec, mine), (1 - sec, theirs)):
        for slot, piece in enumerate(pieces):
            offset = pl.multiple_of(place[1 + slot] * rows, 16)
            plan.append((piece, buffer.at[side, pl.ds(offset, rows), :]))
    return plan


def spread_rows(place, mine, theirs, buffer, rows):
    sec = place[0]
    plan = []
    for side, pieces in ((sec, mine), (1 - sec, theirs)):
        for slot, piece in enumerate(pieces):
            offset = pl.multiple_of((2 * place[1 + slot] + side) * rows, 16)
            plan.append((piece, buffer.at[pl.ds(offset, rows), :]))
    return plan


def fill_bias(first_ref, bias):
    count = bias.shape[0]
    key = lax.broadcasted_iota(jnp.int32, (count, count), 0)
    query = lax.broadcasted_iota(jnp.int32, (count, count), 1)
    allowed = (key >= first_ref[...]) & (key <= query)
    bias[...] = jnp.where(allowed, 0.0, masked_score).astype(F32)


def attention_forward(place, first, cos, sin, x, gain, *rest, tile):
    owners = place.shape[0] - 1
    mine, theirs = rest[:owners], rest[owners:2 * owners]
    mid, q_out, k_out, v_out, o_out, lse_out, weights, bias, sems = rest[2 * owners:]
    rows = mine[0].shape[0]
    started = copies(spread(place, mine, theirs, weights, rows), sems)
    values = x[...].astype(F32)
    normed = (values * inverse_root(values) * gain[...]).astype(BF16)
    fill_bias(first, bias)
    for one in started:
        one.wait()
    kvw = KV_HEADS * HEAD
    width = HEADS * HEAD
    count = x.shape[0]
    qk = nt(weights[0].T, normed)
    v_out[...] = nt(weights[1, :, :kvw].T, normed).astype(BF16)
    c, s = cos[...], sin[...]

    def turned(part):
        low, high = part[:HALF], part[HALF:]
        return jnp.concatenate([low * c - high * s, high * c + low * s], axis=0)

    for head in range(HEADS):
        q_out[head * HEAD:(head + 1) * HEAD, :] = (
            turned(qk[head * HEAD:(head + 1) * HEAD]) * SCALE
        ).astype(BF16)
    for j in range(KV_HEADS):
        at = width + j * HEAD
        k_out[j * HEAD:(j + 1) * HEAD, :] = turned(qk[at:at + HEAD]).astype(BF16)
    for j in range(KV_HEADS):
        keys = k_out[j * HEAD:(j + 1) * HEAD, :].T
        vals = v_out[j * HEAD:(j + 1) * HEAD, :]
        for g in range(GROUP):
            head = j * GROUP + g
            span = slice(head * HEAD, (head + 1) * HEAD)
            for at in range(0, count, tile):
                end = at + tile
                scores = nn(keys[:end], q_out[span, at:end]) + bias[:end, at:end]
                top = jnp.max(scores, axis=0, keepdims=True)
                power = jnp.exp(scores - top)
                total = jnp.sum(power, axis=0, keepdims=True)
                mixed = nn(vals[:, :end], power.astype(BF16))
                o_out[span, at:end] = (mixed / total).astype(BF16)
                lse_out[head:head + 1, at:end] = top + jnp.log(total)
    mid[...] = values + nn(o_out[...].T, weights[1, :, kvw:])


def attention_backward(place, first, cos, sin, x, gain, d_mid, g_ffn, q, k, v, o, lse, *rest, tile):
    owners = place.shape[0] - 1
    mine, theirs = rest[:owners], rest[owners:2 * owners]
    dx, keep, send, weights, grads, bias, g_out, d_q, d_k, d_v, sems, sems_out = rest[2 * owners:]
    rows = mine[0].shape[0]
    sec = place[0]
    started = copies(spread(place, mine, theirs, weights, rows), sems)
    kvw = KV_HEADS * HEAD
    width = HEADS * HEAD
    count = x.shape[0]
    g_mid = d_mid[...].astype(BF16)
    fill_bias(first, bias)
    for one in started:
        one.wait()
    g_out[...] = nt(weights[1, :, kvw:], g_mid).astype(BF16)

    def store(side, columns, value):
        for owner in range(owners):
            grads[side, owner, :rows, columns] = value[owner * rows:(owner + 1) * rows].astype(BF16)

    store(1, slice(kvw, None), nn(o[...], g_mid))
    c, s = cos[...], sin[...]

    def turned_back(part):
        low, high = part[:HALF], part[HALF:]
        return jnp.concatenate([low * c + high * s, high * c - low * s], axis=0)

    for j in range(KV_HEADS):
        own = slice(j * HEAD, (j + 1) * HEAD)
        keys_t = k[own, :]
        keys = keys_t.T
        vals = v[own, :].T
        k_sum = [jnp.zeros((HEAD, tile), F32) for _ in range(count // tile)]
        v_sum = [jnp.zeros((HEAD, tile), F32) for _ in range(count // tile)]
        for g in range(GROUP):
            head = j * GROUP + g
            span = slice(head * HEAD, (head + 1) * HEAD)
            for at in range(0, count, tile):
                end = at + tile
                q_part = q[span, at:end]
                g_part = g_out[span, at:end]
                power = jnp.exp(nn(keys[:end], q_part) + bias[:end, at:end] - lse[head:head + 1, at:end])
                d_prob = nn(vals[:end], g_part)
                delta = jnp.sum(power * d_prob, axis=0, keepdims=True)
                d_score = (power * (d_prob - delta)).astype(BF16)
                power = power.astype(BF16)
                v_add = nt(g_part, power)
                k_add = nt(q_part, d_score)
                for i in range(end // tile):
                    v_sum[i] = v_sum[i] + v_add[:, i * tile:(i + 1) * tile]
                    k_sum[i] = k_sum[i] + k_add[:, i * tile:(i + 1) * tile]
                d_q[span, at:end] = nn(keys_t[:, :end], d_score) * SCALE
        d_k[own, :] = jnp.concatenate(k_sum, axis=1)
        d_v[own, :] = jnp.concatenate(v_sum, axis=1).astype(BF16)
    turned = [turned_back(d_q[h * HEAD:(h + 1) * HEAD, :]).astype(BF16) for h in range(HEADS)]
    turned += [turned_back(d_k[h * HEAD:(h + 1) * HEAD, :]).astype(BF16) for h in range(KV_HEADS)]
    d_qk = jnp.concatenate(turned, axis=0)
    values = x[...].astype(F32)
    inv = inverse_root(values)
    normed = (values * inv * gain[...]).astype(BF16)
    normed_t = normed.T
    store(0, slice(None), nt(normed_t, d_qk))
    store(1, slice(0, kvw), nt(normed_t, d_v[...]))
    d_normed = (nn(weights[0], d_qk) + nn(weights[1, :, :kvw], d_v[...])).T
    back, gain_grad = norm_back(values, inv, gain[...], d_normed)
    extra = grads.shape[2] - rows
    for owner in range(owners):
        span = slice(owner * rows, (owner + 1) * rows)
        both = jnp.concatenate([gain_grad[:, span], g_ffn[:, span]], axis=0)
        grads[:, owner, rows:, :] = jnp.zeros((2, extra, grads.shape[3]), BF16)
        padded = jnp.concatenate([both, jnp.zeros((extra - 2, rows), F32)], axis=0)
        grads[0, owner, rows:, :rows] = padded.astype(BF16)
    out = copies([(grads.at[sec], keep), (grads.at[1 - sec], send)], sems_out)
    dx[...] = d_mid[...] + back
    for one in out:
        one.wait()


def feed_forward(place, mid, gain, *rest, forward, backward, block):
    owners = place.shape[0] - 1
    gu_mine, gu_theirs, down_mine, down_theirs = [rest[i * owners:(i + 1) * owners] for i in range(4)]
    rest = list(rest[4 * owners:])
    dy = rest.pop(0) if backward else None
    y = rest.pop(0) if forward else None
    if backward:
        d_mid, d_gain, gu_keep, gu_send, down_keep, down_send = rest[:6]
        rest = rest[6:]
    w_gu, w_down = rest[:2]
    sems = rest[-1]
    if backward:
        grad_gu, grad_down, sems_out = rest[2:5]
    sec = place[0]
    plan = spread(place, gu_mine, gu_theirs, w_gu, gu_mine[0].shape[0])
    half = down_mine[0].shape[0]
    plan += spread_rows(place, down_mine, down_theirs, w_down, half)
    started = copies(plan, sems)
    values = mid[...]
    inv = inverse_root(values)
    normed = (values * inv * gain[...]).astype(BF16)
    normed_t = normed.T if backward else None
    for one in started:
        one.wait()
    units = w_down.shape[0]
    result, d_normed = None, None
    for at in range(0, units, block):
        span = slice(at, at + block)
        gate = nn(normed, w_gu[0, :, span])
        up = nn(normed, w_gu[1, :, span])
        sg = sigmoid(gate)
        swish = gate * sg
        hidden = (swish * up).astype(BF16)
        if forward:
            part = nn(hidden, w_down[span, :])
            result = part if result is None else result + part
        if backward:
            d_hidden = nt(dy[...], w_down[span, :])
            g_gate = (d_hidden * up * (sg * (1.0 + gate * (1.0 - sg)))).astype(BF16)
            g_up = (d_hidden * swish).astype(BF16)
            grad_gu[0, :, span] = nn(normed_t, g_gate).astype(BF16)
            grad_gu[1, :, span] = nn(normed_t, g_up).astype(BF16)
            down = tn(hidden, dy[...]).astype(BF16)
            for i in range(block // half):
                index = at // half + i
                grad_down[index % 2, index // 2] = down[i * half:(i + 1) * half]
            part = nt(g_gate, w_gu[0, :, span]) + nt(g_up, w_gu[1, :, span])
            d_normed = part if d_normed is None else d_normed + part
    if forward:
        y[...] = (values + result).astype(BF16)
    if backward:
        out = copies(
            [
                (grad_gu.at[sec], gu_keep),
                (grad_gu.at[1 - sec], gu_send),
                (grad_down.at[sec], down_keep),
                (grad_down.at[1 - sec], down_send),
            ],
            sems_out,
        )
        back, gain_grad = norm_back(values, inv, gain[...], d_normed)
        d_gain[...] = gain_grad
        d_mid[...] = dy[...].astype(F32) + back
        for one in out:
            one.wait()


VM = pl.BlockSpec(memory_space=pltpu.VMEM)
SM = pl.BlockSpec(memory_space=pltpu.SMEM)
AN = pl.BlockSpec(memory_space=pl.ANY)
LIMIT = 56 * 1024 * 1024


def params():
    return pltpu.CompilerParams(vmem_limit_bytes=LIMIT)


def shape(dims, kind):
    return jax.ShapeDtypeStruct(dims, kind)


def run_attention_forward(place, tables, x, gain, pieces, tile=256):
    first, cos, sin = tables
    count, wide = x.shape
    cols = pieces[0].shape[1]
    kvw, width = KV_HEADS * HEAD, HEADS * HEAD
    return pl.pallas_call(
        functools.partial(attention_forward, tile=tile),
        out_shape=(
            shape((count, wide), F32),
            shape((width, count), BF16),
            shape((kvw, count), BF16),
            shape((kvw, count), BF16),
            shape((width, count), BF16),
            shape((HEADS, count), F32),
        ),
        in_specs=[SM] + [VM] * 5 + [AN] * len(pieces),
        out_specs=(VM,) * 6,
        scratch_shapes=[
            pltpu.VMEM((2, wide, cols), BF16),
            pltpu.VMEM((count, count), F32),
            pltpu.SemaphoreType.DMA((len(pieces),)),
        ],
        compiler_params=params(),
        cost_estimate=pl.CostEstimate(flops=6 * 10**9, bytes_accessed=10**7, transcendentals=10**6),
        name="attention_forward",
    )(place, first, cos, sin, x, gain, *pieces)


def run_attention_backward(place, tables, x, gain, d_mid, g_ffn, saved, pieces, tile=256):
    first, cos, sin = tables
    count, wide = x.shape
    cols = pieces[0].shape[1]
    kvw, width = KV_HEADS * HEAD, HEADS * HEAD
    q, k, v, o, lse = saved
    owners = len(pieces) // 2
    padded = wide // owners + 16
    return pl.pallas_call(
        functools.partial(attention_backward, tile=tile),
        out_shape=(
            shape((count, wide), F32),
            shape((owners, padded, cols), BF16),
            shape((owners, padded, cols), BF16),
        ),
        in_specs=[SM] + [VM] * 12 + [AN] * len(pieces),
        out_specs=(VM, AN, AN),
        scratch_shapes=[
            pltpu.VMEM((2, wide, cols), BF16),
            pltpu.VMEM((2, owners, padded, cols), BF16),
            pltpu.VMEM((count, count), F32),
            pltpu.VMEM((width, count), BF16),
            pltpu.VMEM((width, count), F32),
            pltpu.VMEM((kvw, count), F32),
            pltpu.VMEM((kvw, count), BF16),
            pltpu.SemaphoreType.DMA((len(pieces),)),
            pltpu.SemaphoreType.DMA((2,)),
        ],
        compiler_params=params(),
        cost_estimate=pl.CostEstimate(flops=12 * 10**9, bytes_accessed=10**7, transcendentals=10**6),
        name="attention_backward",
    )(place, first, cos, sin, x, gain, d_mid, g_ffn, q, k, v, o, lse, *pieces)


def run_feed_forward(place, mid, gain, gu_pieces, down_pieces, dy=None, forward=True, block=384):
    backward = dy is not None
    count, wide = mid.shape
    cols = gu_pieces[0].shape[1]
    half = down_pieces[0].shape[0]
    out_shape, out_specs = [], []
    scratch = [pltpu.VMEM((2, wide, cols), BF16), pltpu.VMEM((cols, wide), BF16)]
    if forward:
        out_shape.append(shape((count, wide), BF16))
        out_specs.append(VM)
    if backward:
        parts = cols // (2 * half)
        out_shape += [
            shape((count, wide), F32),
            shape((1, wide), F32),
            shape((wide, cols), BF16),
            shape((wide, cols), BF16),
            shape((parts, half, wide), BF16),
            shape((parts, half, wide), BF16),
        ]
        out_specs += [VM, VM, AN, AN, AN, AN]
        scratch += [
            pltpu.VMEM((2, wide, cols), BF16),
            pltpu.VMEM((2, parts, half, wide), BF16),
            pltpu.SemaphoreType.DMA((4,)),
        ]
    scratch.append(pltpu.SemaphoreType.DMA((len(gu_pieces) + len(down_pieces),)))
    flops = (7 if forward else 0) + (16 if backward else 0)
    return pl.pallas_call(
        functools.partial(feed_forward, forward=forward, backward=backward, block=block),
        out_shape=tuple(out_shape),
        in_specs=[SM, VM, VM] + [AN] * (len(gu_pieces) + len(down_pieces)) + ([VM] if backward else []),
        out_specs=tuple(out_specs),
        scratch_shapes=scratch,
        compiler_params=params(),
        cost_estimate=pl.CostEstimate(flops=flops * 10**9, bytes_accessed=10**7, transcendentals=10**6),
        name="feed_forward",
    )(place, mid, gain, *gu_pieces, *down_pieces, *([dy] if backward else []))


def make_tables(lengths, count):
    ends = jnp.cumsum(lengths)
    starts = ends - lengths
    places = jnp.arange(count, dtype=jnp.int32)
    document = jnp.sum((places[:, None] >= ends[None, :]).astype(jnp.int32), axis=1)
    inside = document[:, None] == jnp.arange(lengths.shape[0], dtype=jnp.int32)[None, :]
    first = jnp.sum(jnp.where(inside, starts[None, :], 0), axis=1)
    position = (places - first).astype(F32)
    frequency = rope_base ** (-(jnp.arange(HALF, dtype=F32) * 2.0 / HEAD))
    angles = frequency[:, None] * position[None, :]
    return first[None, :], jnp.cos(angles), jnp.sin(angles)


def swap(value):
    return lax.ppermute(value, "section", [(0, 1), (1, 0)])


def give(value, target):
    return lax.ppermute(value, "section", [(1 - target, target)])


def exchange(value, axis, bit):
    count = lax.axis_size(axis)
    return lax.ppermute(value, axis, [(i, i ^ bit) for i in range(count)])


def mixed_exchange(value, even_bit, odd_bit):
    owners, replicas = lax.axis_size("fsdp"), lax.axis_size("dp")
    pairs = []
    for i in range(owners):
        for z in range(replicas):
            partner = i ^ (odd_bit if z % 2 else even_bit)
            pairs.append((i * replicas + z, partner * replicas + z))
    return lax.ppermute(value, ("fsdp", "dp"), pairs)


def paired():
    return lax.axis_size("fsdp") == 4 and lax.axis_size("dp") % 2 == 0


def piece_places():
    own = lax.axis_index("fsdp")
    if not paired():
        return list(range(lax.axis_size("fsdp")))
    odd = lax.axis_index("dp") % 2
    near, far = jnp.where(odd == 1, own ^ 2, own ^ 1), jnp.where(odd == 1, own ^ 1, own ^ 2)
    return [own, near, own ^ 3, far]


def gather(value):
    if not paired():
        whole = lax.all_gather(value, "fsdp")
        return [whole[i] for i in range(lax.axis_size("fsdp"))]
    near = mixed_exchange(value, 1, 2)
    return [value, near, mixed_exchange(near, 2, 1), exchange(near, "dp", 1)]


def add(left, right):
    return (left.astype(F32) + right.astype(F32)).astype(BF16)


def pick(pair, index, axis):
    return lax.dynamic_index_in_dim(pair, index, axis, keepdims=False)


def scatter_sum(parts, x_first):
    own = lax.axis_index("fsdp")
    if lax.axis_size("fsdp") != 4:
        total = lax.psum_scatter(parts, "fsdp", scatter_dimension=0, tiled=False)
        return total
    y, x = own // 2, own % 2
    square = parts.reshape((2, 2) + parts.shape[1:])
    if x_first:
        row = add(pick(square, x, 1), exchange(pick(square, 1 - x, 1), "fsdp", 1))
        return add(pick(row, y, 0), exchange(pick(row, 1 - y, 0), "fsdp", 2))
    row = add(pick(square, y, 0), exchange(pick(square, 1 - y, 0), "fsdp", 2))
    return add(pick(row, x, 0), exchange(pick(row, 1 - x, 0), "fsdp", 1))


def replica_sum(value, axis, halve):
    count = lax.axis_size("dp")
    if count != 4:
        return lax.psum(value, "dp")
    if not halve:
        value = add(value, exchange(value, "dp", 1))
        return add(value, exchange(value, "dp", 2))
    index = lax.axis_index("dp")
    low, high = index % 2, index // 2

    def split(whole):
        dims = whole.shape
        return whole.reshape(dims[:axis] + (2, dims[axis] // 2) + dims[axis + 1:])

    def join(bit, mine, other):
        first = jnp.where(bit == 0, mine, other)
        second = jnp.where(bit == 0, other, mine)
        return jnp.concatenate([first, second], axis=axis)

    one = split(value)
    half = add(pick(one, low, axis), exchange(pick(one, 1 - low, axis), "dp", 1))
    two = split(half)
    part = add(pick(two, high, axis), exchange(pick(two, 1 - high, axis), "dp", 2))
    half = join(high, part, exchange(part, "dp", 2))
    return join(low, half, exchange(half, "dp", 1))


def local(
    tokens,
    cotangent,
    doc_lengths,
    w_query,
    w_key,
    w_value,
    w_out,
    w_gate,
    w_up,
    w_down,
    gain_attn,
    gain_ffn,
):
    sec = lax.axis_index("section")
    first_section = sec == 0
    owners = lax.axis_size("fsdp")
    count = tokens.shape[2]
    places = piece_places()
    place = jnp.stack([jnp.asarray(i, jnp.int32) for i in [sec] + places])

    half_rows = w_down.shape[1] // 2
    halves = (
        (jnp.concatenate([w_query[0], w_key[0]], axis=1), jnp.concatenate([w_value[0], w_out[0]], axis=1)),
        (w_gate[0], w_up[0]),
        (w_down[0, :half_rows], w_down[0, half_rows:]),
    )
    gains = jnp.concatenate([gain_attn, gain_ffn], axis=0)
    gains_other = swap(gains)
    gains_both = jnp.concatenate(
        [jnp.where(first_section, gains, gains_other), jnp.where(first_section, gains_other, gains)], axis=0
    )
    gain_pieces = gather(gains_both)
    gain_rows = []
    for owner in range(owners):
        row = gain_pieces[0]
        for spot, piece in zip(places[1:], gain_pieces[1:]):
            row = jnp.where(spot == owner, piece, row)
        gain_rows.append(row)
    gain_full = jnp.concatenate(gain_rows, axis=1).astype(F32)
    attn_gains = (gain_full[0:1], gain_full[2:3])
    ffn_gains = (gain_full[1:2], gain_full[3:4])

    carried, others = [[], []], [[], []]
    for half0, half1 in halves:
        mine = jnp.where(first_section, half0, half1)
        rest = jnp.where(first_section, half1, half0)
        mine_back, rest_back = swap(rest), swap(mine)
        carried[0].append(jnp.where(first_section, mine, mine_back))
        carried[1].append(jnp.where(first_section, mine_back, mine))
        others[0].append(jnp.where(first_section, rest, rest_back))
        others[1].append(jnp.where(first_section, rest_back, rest))
    weights = [[], []]
    for layer in range(2):
        for mine, other in zip(carried[layer], others[layer]):
            pieces = gather(mine)
            if paired():
                theirs = [other] + [swap(piece) for piece in pieces[1:]]
            else:
                theirs = [swap(piece) for piece in pieces]
            weights[layer].append(pieces + theirs)

    tables = make_tables(pick(doc_lengths[0], sec, 0), count)
    x0 = pick(tokens[0], sec, 0)
    dy1 = pick(cotangent[0], sec, 0)
    (attn0, gu0, down0), (attn1, gu1, down1) = weights

    mid0, *saved0 = run_attention_forward(place, tables, x0, attn_gains[0], attn0)
    (y0,) = run_feed_forward(place, mid0, ffn_gains[0], gu0, down0)
    mid1, *saved1 = run_attention_forward(place, tables, y0, attn_gains[1], attn1)
    y1, d_mid1, g_ffn1, gu_keep1, gu_send1, down_keep1, down_send1 = run_feed_forward(
        place, mid1, ffn_gains[1], gu1, down1, dy=dy1
    )
    dx1, at_keep1, at_send1 = run_attention_backward(
        place, tables, y0, attn_gains[1], d_mid1, g_ffn1, saved1, attn1
    )
    dy0 = dx1.astype(BF16)
    d_mid0, g_ffn0, gu_keep0, gu_send0, down_keep0, down_send0 = run_feed_forward(
        place, mid0, ffn_gains[0], gu0, down0, dy=dy0, forward=False
    )
    dx0, at_keep0, at_send0 = run_attention_backward(
        place, tables, x0, attn_gains[0], d_mid0, g_ffn0, saved0, attn0
    )

    def reduced(keep, send, x_first, axis, halve=True):
        parts = add(keep, swap(send))
        if parts.ndim == 2:
            parts = parts.reshape(owners, parts.shape[0] // owners, parts.shape[1])
        return replica_sum(scatter_sum(parts, x_first), axis, halve)

    gu_sum1 = reduced(gu_keep1, gu_send1, True, 1)
    down_sum1 = reduced(down_keep1, down_send1, False, 0)
    at_sum1 = reduced(at_keep1, at_send1, False, 1)
    gu_sum0 = reduced(gu_keep0, gu_send0, True, 1)
    down_sum0 = reduced(down_keep0, down_send0, False, 0)
    at_sum0 = reduced(at_keep0, at_send0, False, 1, halve=False)

    def final(sum0, sum1):
        back0, back1 = give(sum0, 0), give(sum1, 1)
        return (
            jnp.where(first_section, sum0, back1).astype(F32),
            jnp.where(first_section, back0, sum1).astype(F32),
        )

    gate, up = final(gu_sum0, gu_sum1)
    down = jnp.concatenate(final(down_sum0, down_sum1), axis=0)
    qk, vo = final(at_sum0, at_sum1)
    rows = w_query.shape[1]
    width, kvw = w_query.shape[2], w_key.shape[2]

    def both_rows(own0, own1):
        back = swap(jnp.where(first_section, own1, own0))
        return jnp.where(first_section, jnp.stack([own0, back]), jnp.stack([back, own1]))[None, None]

    return (
        both_rows(y0, y1),
        both_rows(dx0, dx1),
        qk[None, :rows, :width],
        qk[None, :rows, width:],
        vo[None, :rows, :kvw],
        vo[None, :rows, kvw:],
        gate[None],
        up[None],
        down[None],
        qk[None, rows, :rows],
        qk[None, rows + 1, :rows],
    )


def solution(mesh):
    whole = P(("fsdp", "dp"), None, None, None)
    weight = P("section", "fsdp", None)
    gain = P("section", "fsdp")
    rows = P("section", ("fsdp", "dp"), None, None, None)
    in_specs = (whole, whole, P(("fsdp", "dp"), None, None)) + (weight,) * 7 + (gain,) * 2
    out_specs = (rows, rows) + (weight,) * 7 + (gain,) * 2
    return jax.shard_map(local, mesh=mesh, in_specs=in_specs, out_specs=out_specs, check_vma=False)
```

```python
import functools
import jax
import jax.numpy as jnp
from jax import lax
from jax.experimental import pallas as pl
from jax.experimental.pallas import tpu as pltpu
from jax.sharding import PartitionSpec as P

HEADS = 9
KV_HEADS = 3
GROUP = HEADS // KV_HEADS
HEAD = 64
HALF = HEAD // 2
WIDTH = HEADS * HEAD
KVW = KV_HEADS * HEAD

epsilon = 1e-05
rope_base = 100000.0
masked_score = -1e30
SCALE = HEAD ** (-0.5)
EXTRA = 16
F32 = jnp.float32
BF16 = jnp.bfloat16


def nn(left, right):
    return lax.dot_general(left, right, (((1,), (0,)), ((), ())), preferred_element_type=F32)


def nt(left, right):
    return lax.dot_general(left, right, (((1,), (1,)), ((), ())), preferred_element_type=F32)


def inverse_root(values):
    return lax.rsqrt(jnp.mean(values * values, axis=-1, keepdims=True) + epsilon)


def norm_back(values, inv_root, gain, upstream):
    gain_grad = jnp.sum(upstream * values * inv_root, axis=0, keepdims=True)
    scaled = upstream * gain
    dot = jnp.mean(scaled * values, axis=-1, keepdims=True)
    return inv_root * scaled - values * (inv_root * inv_root * inv_root * dot), gain_grad


def sigmoid(values):
    return 0.5 * jnp.tanh(0.5 * values) + 0.5


def pack(place, wq, wk, wv, wo, gate, up, down, gains, own_at, rest_at, own_ff, rest_ff):
    rows, cols = wq.shape[0], own_at.shape[1]
    down_cols = down.shape[1]
    half_down = down.shape[0] // 2

    def write(at, ff, half):
        left, right = ((wq, wk), (wo, wv))[half]
        at[:rows, :] = jnp.concatenate([left[...], right[...]], axis=1)
        at[rows:, :] = jnp.zeros((EXTRA, cols), BF16)
        at[rows:, :rows] = jnp.concatenate(
            [gains[...].astype(F32), jnp.zeros((EXTRA - 2, rows), F32)], axis=0
        ).astype(BF16)
        wide = (gate, up)[half]
        ff[:rows, :] = wide[:, :cols]
        ff[rows:2 * rows, :] = wide[:, cols:]
        for i in range(2):
            top = half * half_down + i * rows
            ff[2 * rows:, i * down_cols:(i + 1) * down_cols] = down[top:top + rows, :]

    for number in range(2):

        @pl.when(place[0] == number)
        def _(number=number):
            write(own_at, own_ff, number)
            write(rest_at, rest_ff, 1 - number)


def either(condition, first, second, target, sem):
    @pl.when(condition)
    def _():
        pltpu.make_async_copy(first, target, sem).start()

    @pl.when(jnp.logical_not(condition))
    def _():
        pltpu.make_async_copy(second, target, sem).start()

    return pltpu.make_async_copy(first, target, sem)


def start(source, target, sem):
    one = pltpu.make_async_copy(source, target, sem)
    one.start()
    return one


def sides(place, layer, pieces):
    sec = place[0]
    slots = place.shape[0] - 1
    found = []
    for number, (half, rest) in enumerate(((sec, pieces[4:3 + slots]), (1 - sec, pieces[3 + slots:]))):
        found.append((half, place[1], pieces[2 * number], pieces[2 * number + 1]))
        for slot, piece in enumerate(rest):
            found.append((half, place[2 + slot], piece, None))
    return found


def load_attention(place, layer, pieces, weights, gains, sems):
    rows = pieces[0].shape[0] - EXTRA
    home = place[0] == layer
    waits = []
    slots = place.shape[0] - 1
    for number, (half, owner, source, other) in enumerate(sides(place, layer, pieces)):
        target = weights.at[half, pl.ds(pl.multiple_of(owner * rows, 16), rows), :]
        window = slice(0, rows)
        if other is None:
            waits.append(start(source.at[window], target, sems.at[number]))
        else:
            waits.append(either(home, source.at[window], other.at[window], target, sems.at[number]))
        if number < slots and gains is not None:
            window, target, sem = slice(rows, rows + EXTRA), gains.at[owner], sems.at[2 * slots + number]
            if other is None:
                waits.append(start(source.at[window], target, sem))
            else:
                waits.append(either(home, source.at[window], other.at[window], target, sem))
    return waits


def load_feed_forward(place, layer, pieces, gate_up, down, sems):
    rows, cols = pieces[0].shape[0] // 3, pieces[0].shape[1]
    narrow = cols // 2
    home = place[0] == layer
    early, late = [], []
    for number, (half, owner, source, other) in enumerate(sides(place, layer, pieces)):
        for part in range(4):
            if part < 2:
                window = (slice(part * rows, (part + 1) * rows), slice(None))
                target = gate_up.at[half, pl.ds(pl.multiple_of(owner * rows, 16), rows), part * cols:(part + 1) * cols]
            else:
                i = part - 2
                window = (slice(2 * rows, 3 * rows), slice(i * narrow, (i + 1) * narrow))
                top = pl.multiple_of(half * (2 * rows) + i * rows, 16)
                target = down.at[pl.ds(top, rows), pl.ds(pl.multiple_of(owner * narrow, 128), narrow)]
            sem = sems.at[4 * number + part]
            if other is None:
                one = start(source.at[window], target, sem)
            else:
                one = either(home, source.at[window], other.at[window], target, sem)
            (early if part < 2 else late).append(one)
    return early, late


def fill_bias(first, bias):
    count = bias.shape[0]
    key = lax.broadcasted_iota(jnp.int32, (count, count), 0)
    query = lax.broadcasted_iota(jnp.int32, (count, count), 1)
    allowed = (key >= first[...]) & (key <= query)
    bias[...] = jnp.where(allowed, 0.0, masked_score).astype(F32)


def attention_forward(place, first, cos, sin, x_t, *rest, layer, tile, count_pieces):
    pieces = rest[:count_pieces]
    mid, q_out, k_out, v_out, o_out, lse_out, gain_out, weights, gain_parts, bias, sems = rest[count_pieces:]
    owners = gain_parts.shape[0]
    rows = weights.shape[1] // owners
    waits = load_attention(place, layer, pieces, weights, gain_parts, sems)
    count = x_t.shape[1]
    values = x_t[...].T.astype(F32)
    scaled = values * inverse_root(values)
    fill_bias(first, bias)
    for one in waits:
        one.wait()
    gain = jnp.concatenate([gain_parts[f][:2, :rows].astype(F32) for f in range(owners)], axis=1)
    gain_out[...] = gain
    normed = (scaled * gain[:1]).astype(BF16)
    qk = nt(weights[0].T, normed)
    v_out[...] = nt(weights[1, :, WIDTH:].T, normed).astype(BF16)
    c, s = cos[...], sin[...]

    def turned(part):
        low, high = part[:HALF], part[HALF:]
        return jnp.concatenate([low * c - high * s, high * c + low * s], axis=0)

    for head in range(HEADS):
        span = slice(head * HEAD, (head + 1) * HEAD)
        q_out[span, :] = (turned(qk[span]) * SCALE).astype(BF16)
    for j in range(KV_HEADS):
        at = WIDTH + j * HEAD
        k_out[j * HEAD:(j + 1) * HEAD, :] = turned(qk[at:at + HEAD]).astype(BF16)
    for j in range(KV_HEADS):
        keys = k_out[j * HEAD:(j + 1) * HEAD, :].T
        vals = v_out[j * HEAD:(j + 1) * HEAD, :]
        for g in range(GROUP):
            head = j * GROUP + g
            span = slice(head * HEAD, (head + 1) * HEAD)
            for at in range(0, count, tile):
                end = at + tile
                scores = nn(keys[:end], q_out[span, at:end]) + bias[:end, at:end]
                top = jnp.max(scores, axis=0, keepdims=True)
                power = jnp.exp(scores - top)
                total = jnp.sum(power, axis=0, keepdims=True)
                mixed = nn(vals[:, :end], power.astype(BF16))
                o_out[span, at:end] = (mixed / total).astype(BF16)
                lse_out[head:head + 1, at:end] = top + jnp.log(total)
    mid[...] = values + nn(o_out[...].T, weights[1, :, :WIDTH])


def attention_backward(place, first, cos, sin, x_t, gain, d_mid, g_ffn, q, k, v, o, lse, *rest, layer, tile, count_pieces):
    pieces = rest[:count_pieces]
    dx, dx_low, keep, send, weights, grads, bias, g_out, d_q, d_k, d_v, sems, sems_out = rest[count_pieces:]
    owners = grads.shape[1]
    rows = weights.shape[1] // owners
    sec = place[0]
    waits = load_attention(place, layer, pieces, weights, None, sems)
    count = x_t.shape[1]
    g_mid = d_mid[...].astype(BF16)
    fill_bias(first, bias)
    for one in waits:
        one.wait()
    g_out[...] = nt(weights[1, :, :WIDTH], g_mid).astype(BF16)

    def store(side, columns, value):
        for owner in range(owners):
            grads[side, owner, :rows, columns] = value[owner * rows:(owner + 1) * rows].astype(BF16)

    store(1, slice(0, WIDTH), nn(o[...], g_mid))
    c, s = cos[...], sin[...]

    def turned_back(part):
        low, high = part[:HALF], part[HALF:]
        return jnp.concatenate([low * c + high * s, high * c - low * s], axis=0)

    for j in range(KV_HEADS):
        own = slice(j * HEAD, (j + 1) * HEAD)
        keys_t = k[own, :]
        keys = keys_t.T
        vals = v[own, :].T
        k_sum = [jnp.zeros((HEAD, tile), F32) for _ in range(count // tile)]
        v_sum = [jnp.zeros((HEAD, tile), F32) for _ in range(count // tile)]
        for g in range(GROUP):
            head = j * GROUP + g
            span = slice(head * HEAD, (head + 1) * HEAD)
            for at in range(0, count, tile):
                end = at + tile
                q_part = q[span, at:end]
                g_part = g_out[span, at:end]
                power = jnp.exp(nn(keys[:end], q_part) + bias[:end, at:end] - lse[head:head + 1, at:end])
                d_prob = nn(vals[:end], g_part)
                delta = jnp.sum(power * d_prob, axis=0, keepdims=True)
                d_score = (power * (d_prob - delta)).astype(BF16)
                power = power.astype(BF16)
                v_add = nt(g_part, power)
                k_add = nt(q_part, d_score)
                for i in range(end // tile):
                    v_sum[i] = v_sum[i] + v_add[:, i * tile:(i + 1) * tile]
                    k_sum[i] = k_sum[i] + k_add[:, i * tile:(i + 1) * tile]
                d_q[span, at:end] = nn(keys_t[:, :end], d_score) * SCALE
        d_k[own, :] = jnp.concatenate(k_sum, axis=1)
        d_v[own, :] = jnp.concatenate(v_sum, axis=1).astype(BF16)
    turned = [turned_back(d_q[h * HEAD:(h + 1) * HEAD, :]).astype(BF16) for h in range(HEADS)]
    turned += [turned_back(d_k[h * HEAD:(h + 1) * HEAD, :]).astype(BF16) for h in range(KV_HEADS)]
    d_qk = jnp.concatenate(turned, axis=0)
    values = x_t[...].T.astype(F32)
    inv = inverse_root(values)
    attn_gain = gain[:1, :]
    normed_t = (values * inv * attn_gain).astype(BF16).T
    store(0, slice(None), nt(normed_t, d_qk))
    store(1, slice(WIDTH, None), nt(normed_t, d_v[...]))
    d_normed = (nn(weights[0], d_qk) + nn(weights[1, :, WIDTH:], d_v[...])).T
    back, gain_grad = norm_back(values, inv, attn_gain, d_normed)
    for owner in range(owners):
        span = slice(owner * rows, (owner + 1) * rows)
        both = jnp.concatenate([gain_grad[:, span], g_ffn[:, span]], axis=0)
        grads[:, owner, rows:, :] = jnp.zeros((2, EXTRA, grads.shape[3]), BF16)
        padded = jnp.concatenate([both, jnp.zeros((EXTRA - 2, rows), F32)], axis=0)
        grads[0, owner, rows:, :rows] = padded.astype(BF16)
    out = [start(grads.at[1 - sec], send, sems_out.at[0]), start(grads.at[sec], keep, sems_out.at[1])]
    total = (d_mid[...] + back).T
    dx[...] = total
    dx_low[...] = total.astype(BF16)
    for one in out:
        one.wait()


def feed_forward(place, mid, gain, *rest, layer, forward, backward, block, count_pieces):
    pieces = rest[:count_pieces]
    rest = list(rest[count_pieces:])
    take = lambda: rest.pop(0)
    dy_t = take() if backward else None
    kept = (take(), take()) if backward and not forward else None
    y_t = take() if forward else None
    keeping = (take(), take()) if forward and not backward else None
    if backward:
        d_mid, d_gain, keep, send = take(), take(), take(), take()
    gate_up, down, sems = take(), take(), take()
    if backward:
        grads, sems_out = take(), take()
    sec = place[0]
    early, late = load_feed_forward(place, layer, pieces, gate_up, down, sems)
    values = mid[...]
    inv = inverse_root(values)
    ffn_gain = gain[1:, :]
    normed = (values * inv * ffn_gain).astype(BF16)
    if backward:
        normed_t = normed.T
        dy = dy_t[...].T
        rows = grads.shape[2] // 3
        owners = grads.shape[1]
    for one in early:
        one.wait()
    units = down.shape[1]
    result, d_normed = None, None
    out = []
    for number, at in enumerate(range(0, units, block)):
        span = slice(at, at + block)
        if kept is None:
            gate, up = nn(normed, gate_up[0, :, span]), nn(normed, gate_up[1, :, span])
        else:
            gate, up = kept[0][:, span].astype(F32), kept[1][:, span].astype(F32)
        sg = sigmoid(gate)
        swish = gate * sg
        hidden = (swish * up).astype(BF16)
        if keeping is not None:
            keeping[0][:, span] = gate.astype(BF16)
            keeping[1][:, span] = up.astype(BF16)
        if number == 0:
            for one in late:
                one.wait()
        if forward:
            part = nt(hidden, down[:, span])
            result = part if result is None else result + part
        if backward:
            d_hidden = nn(dy, down[:, span])
            g_gate = (d_hidden * up * (sg * (1.0 + gate * (1.0 - sg)))).astype(BF16)
            g_up = (d_hidden * swish).astype(BF16)
            for half, grad in ((0, g_gate), (1, g_up)):
                value = nn(normed_t, grad).astype(BF16)
                for owner in range(owners):
                    grads[half, owner, number * rows:(number + 1) * rows, :] = value[owner * rows:(owner + 1) * rows]
            value = nn(dy_t[...], hidden).astype(BF16)
            narrow = block // 2
            for i in range(2):
                for half in range(2):
                    for k in range(2):
                        top = (2 * half + k) * rows
                        grads[half, 2 * number + i, 2 * rows:, k * narrow:(k + 1) * narrow] = value[
                            top:top + rows, i * narrow:(i + 1) * narrow
                        ]
            for side, target in ((1 - sec, send), (sec, keep)):
                for window in (
                    (slice(None), slice(number * rows, (number + 1) * rows)),
                    (slice(2 * number, 2 * number + 2), slice(2 * rows, 3 * rows)),
                ):
                    out.append(start(grads.at[(side,) + window], target.at[window], sems_out.at[len(out)]))
            part = nt(g_gate, gate_up[0, :, span]) + nt(g_up, gate_up[1, :, span])
            d_normed = part if d_normed is None else d_normed + part
    if forward:
        y_t[...] = (values + result).astype(BF16).T
    if backward:
        back, gain_grad = norm_back(values, inv, ffn_gain, d_normed)
        d_gain[...] = gain_grad
        d_mid[...] = dy.astype(F32) + back
        for one in out:
            one.wait()


VM = pl.BlockSpec(memory_space=pltpu.VMEM)
SM = pl.BlockSpec(memory_space=pltpu.SMEM)
AN = pl.BlockSpec(memory_space=pl.ANY)


def params(mib):
    return pltpu.CompilerParams(vmem_limit_bytes=mib * 1024 * 1024)


def shape(dims, kind):
    return jax.ShapeDtypeStruct(dims, kind)


def cost(gigaflops):
    return pl.CostEstimate(flops=int(gigaflops * 10**9), bytes_accessed=10**7, transcendentals=10**6)


def run_pack(place, wq, wk, wv, wo, gate, up, down, gains):
    rows, cols = wq.shape[0], wq.shape[1] + wk.shape[1]
    at, ff = shape((rows + EXTRA, cols), BF16), shape((3 * rows, cols), BF16)
    return pl.pallas_call(
        pack,
        out_shape=(at, at, ff, ff),
        in_specs=[SM] + [VM] * 8,
        out_specs=(VM,) * 4,
        compiler_params=params(16),
        name="pack",
    )(place, wq, wk, wv, wo, gate, up, down, gains)


def run_attention_forward(layer, place, tables, x_t, pieces, tile=256):
    first, cos, sin = tables
    wide, count = x_t.shape
    cols = pieces[0].shape[1]
    owners = place.shape[0] - 1
    return pl.pallas_call(
        functools.partial(attention_forward, layer=layer, tile=tile, count_pieces=len(pieces)),
        out_shape=(
            shape((count, wide), F32),
            shape((WIDTH, count), BF16),
            shape((KVW, count), BF16),
            shape((KVW, count), BF16),
            shape((WIDTH, count), BF16),
            shape((HEADS, count), F32),
            shape((2, wide), F32),
        ),
        in_specs=[SM] + [VM] * 4 + [AN] * len(pieces),
        out_specs=(VM,) * 7,
        scratch_shapes=[
            pltpu.VMEM((2, wide, cols), BF16),
            pltpu.VMEM((owners, EXTRA, cols), BF16),
            pltpu.VMEM((count, count), F32),
            pltpu.SemaphoreType.DMA((3 * owners,)),
        ],
        compiler_params=params(40),
        cost_estimate=cost(6),
        name="attention_forward",
    )(place, first, cos, sin, x_t, *pieces)


def run_attention_backward(layer, place, tables, x_t, gain, d_mid, g_ffn, saved, pieces, tile=256):
    first, cos, sin = tables
    wide, count = x_t.shape
    cols = pieces[0].shape[1]
    owners = place.shape[0] - 1
    padded = wide // owners + EXTRA
    return pl.pallas_call(
        functools.partial(attention_backward, layer=layer, tile=tile, count_pieces=len(pieces)),
        out_shape=(
            shape((wide, count), F32),
            shape((wide, count), BF16),
            shape((owners, padded, cols), BF16),
            shape((owners, padded, cols), BF16),
        ),
        in_specs=[SM] + [VM] * 12 + [AN] * len(pieces),
        out_specs=(VM, VM, AN, AN),
        scratch_shapes=[
            pltpu.VMEM((2, wide, cols), BF16),
            pltpu.VMEM((2, owners, padded, cols), BF16),
            pltpu.VMEM((count, count), F32),
            pltpu.VMEM((WIDTH, count), BF16),
            pltpu.VMEM((WIDTH, count), F32),
            pltpu.VMEM((KVW, count), F32),
            pltpu.VMEM((KVW, count), BF16),
            pltpu.SemaphoreType.DMA((2 * owners,)),
            pltpu.SemaphoreType.DMA((2,)),
        ],
        compiler_params=params(40),
        cost_estimate=cost(10),
        name="attention_backward",
    )(place, first, cos, sin, x_t, gain, d_mid, g_ffn, *saved, *pieces)


def run_feed_forward(layer, place, mid, gain, pieces, dy_t=None, kept=(), block=768):
    backward = dy_t is not None
    forward = not kept
    count, wide = mid.shape
    owners = place.shape[0] - 1
    rows, cols = pieces[0].shape[0] // 3, pieces[0].shape[1]
    out_shape, out_specs = [], []
    scratch = [
        pltpu.VMEM((2, wide, 2 * cols), BF16),
        pltpu.VMEM((wide, 2 * cols), BF16),
        pltpu.SemaphoreType.DMA((8 * owners,)),
    ]
    if forward:
        out_shape.append(shape((wide, count), BF16))
        out_specs.append(VM)
        if not backward:
            out_shape += [shape((count, 2 * cols), BF16)] * 2
            out_specs += [VM] * 2
    if backward:
        out_shape += [
            shape((count, wide), F32),
            shape((1, wide), F32),
            shape((owners, 3 * rows, cols), BF16),
            shape((owners, 3 * rows, cols), BF16),
        ]
        out_specs += [VM, VM, AN, AN]
        scratch += [
            pltpu.VMEM((2, owners, 3 * rows, cols), BF16),
            pltpu.SemaphoreType.DMA((8,)),
        ]
    flops = (7 if forward else 0) + (14 if backward else 0)
    extra = ([dy_t] if backward else []) + list(kept)
    return pl.pallas_call(
        functools.partial(
            feed_forward, layer=layer, forward=forward, backward=backward, block=block, count_pieces=len(pieces)
        ),
        out_shape=tuple(out_shape),
        in_specs=[SM, VM, VM] + [AN] * len(pieces) + [VM] * len(extra),
        out_specs=tuple(out_specs),
        scratch_shapes=scratch,
        compiler_params=params(48),
        cost_estimate=cost(flops),
        name="feed_forward",
    )(place, mid, gain, *pieces, *extra)


def make_tables(lengths, count):
    ends = jnp.cumsum(lengths)
    starts = ends - lengths
    places = jnp.arange(count, dtype=jnp.int32)
    document = jnp.sum((places[:, None] >= ends[None, :]).astype(jnp.int32), axis=1)
    inside = document[:, None] == jnp.arange(lengths.shape[0], dtype=jnp.int32)[None, :]
    first = jnp.sum(jnp.where(inside, starts[None, :], 0), axis=1)
    position = (places - first).astype(F32)
    frequency = rope_base ** (-(jnp.arange(HALF, dtype=F32) * 2.0 / HEAD))
    angles = frequency[:, None] * position[None, :]
    return first[None, :], jnp.cos(angles), jnp.sin(angles)


def swap(value):
    return lax.ppermute(value, "section", [(0, 1), (1, 0)])


def give(value, target):
    return lax.ppermute(value, "section", [(1 - target, target)])


def exchange(value, axis, bit):
    count = lax.axis_size(axis)
    return lax.ppermute(value, axis, [(i, i ^ bit) for i in range(count)])


def mixed_exchange(value, even_bit, odd_bit):
    owners, replicas = lax.axis_size("fsdp"), lax.axis_size("dp")
    pairs = []
    for i in range(owners):
        for z in range(replicas):
            partner = i ^ (odd_bit if z % 2 else even_bit)
            pairs.append((i * replicas + z, partner * replicas + z))
    return lax.ppermute(value, ("fsdp", "dp"), pairs)


def paired():
    return lax.axis_size("fsdp") == 4 and lax.axis_size("dp") % 2 == 0


def piece_places():
    own = lax.axis_index("fsdp")
    if not paired():
        count = lax.axis_size("fsdp")
        return [own] + [(own + i) % count for i in range(1, count)]
    odd = lax.axis_index("dp") % 2
    near, far = jnp.where(odd == 1, own ^ 2, own ^ 1), jnp.where(odd == 1, own ^ 1, own ^ 2)
    return [own, near, own ^ 3, far]


def first_hop(value):
    if not paired():
        return lax.all_gather(value, "fsdp")
    return mixed_exchange(value, 1, 2)


def second_hop(near):
    if not paired():
        count = lax.axis_size("fsdp")
        own = lax.axis_index("fsdp")
        carried = [pick(near, (own + i) % count, 0) for i in range(1, count)]
    else:
        carried = [near, mixed_exchange(near, 2, 1), exchange(near, "dp", 1)]
    return carried + [swap(piece) for piece in carried]


def tie(*values):
    return lax.optimization_barrier(values)


def add(left, right):
    return (left.astype(F32) + right.astype(F32)).astype(BF16)


def pick(value, index, axis):
    return lax.dynamic_index_in_dim(value, index, axis, keepdims=False)


def split_first(place, keep, came, *outs, cut):
    y, x = place[1] // 2, place[1] % 2
    outs = list(outs)
    total = keep.shape[1]
    for by_x, low, high in ((True, 0, cut), (False, cut, total)):
        if low == high:
            continue
        hold, away = outs.pop(0), outs.pop(0)
        for i in range(2):
            for target, mine in ((hold, True), (away, False)):
                bit_x, bit_y = (x, y) if mine else (1 - x, 1 - y)
                block = 2 * i + bit_x if by_x else 2 * bit_y + i
                target[i] = (
                    keep[block, low:high].astype(F32) + came[block, low:high].astype(F32)
                ).astype(BF16)


def run_split_first(place, keep, came, cut):
    owners, total, cols = keep.shape
    out = []
    for low, high in ((0, cut), (cut, total)):
        if high > low:
            out += [shape((2, high - low, cols), BF16)] * 2
    return pl.pallas_call(
        functools.partial(split_first, cut=cut),
        out_shape=tuple(out),
        in_specs=[SM, VM, VM],
        out_specs=(VM,) * len(out),
        compiler_params=params(24),
        name="split_first",
    )(place, keep, came)


def split_second(place, *refs, cut, total):
    y, x = place[1] // 2, place[1] % 2
    ranges = [(True, 0, cut), (False, cut, total)]
    ranges = [r for r in ranges if r[2] > r[1]]
    ins, outs = list(refs[:2 * len(ranges)]), list(refs[2 * len(ranges):])
    for by_x, low, high in ranges:
        hold, came = ins.pop(0), ins.pop(0)
        stay, away = outs.pop(0), outs.pop(0)
        bit = y if by_x else x
        stay[...] = (hold[bit].astype(F32) + came[bit].astype(F32)).astype(BF16)
        away[...] = (hold[1 - bit].astype(F32) + came[1 - bit].astype(F32)).astype(BF16)


def run_split_second(place, parts, cut, total):
    out = []
    for hold in parts[::2]:
        out += [shape(hold.shape[1:], BF16)] * 2
    return pl.pallas_call(
        functools.partial(split_second, cut=cut, total=total),
        out_shape=tuple(out),
        in_specs=[SM] + [VM] * len(parts),
        out_specs=(VM,) * len(out),
        compiler_params=params(24),
        name="split_second",
    )(place, *parts)


class Sum:
    def __init__(self, place, keep, send, cut, layer, halve):
        self.place, self.keep, self.cut, self.layer, self.halve = place, keep, cut, layer, halve
        self.total = keep.shape[1]
        self.direct = lax.axis_size("fsdp") == 4
        self.came = [swap(send)]

    def bits(self, second):
        order = (2, 1) if second else (1, 2)
        found = [order[0]] if self.cut > 0 else []
        return found + ([order[1]] if self.cut < self.total else [])

    def fsdp_first(self):
        if not self.direct:
            whole = add(self.keep, self.came[0])
            self.came = [lax.psum_scatter(whole, "fsdp", scatter_dimension=0, tiled=False)]
            return
        parts = run_split_first(self.place, self.keep, self.came[0], self.cut)
        self.hold = parts[::2]
        self.came = [exchange(p, "fsdp", b) for p, b in zip(parts[1::2], self.bits(False))]

    def fsdp_second(self):
        if not self.direct:
            return
        parts = [p for pair in zip(self.hold, self.came) for p in pair]
        parts = run_split_second(self.place, parts, self.cut, self.total)
        self.hold = parts[::2]
        self.came = [exchange(p, "fsdp", b) for p, b in zip(parts[1::2], self.bits(True))]

    def dp_first(self):
        if self.direct:
            parts = [add(h, c) for h, c in zip(self.hold, self.came)]
            value = parts[0] if len(parts) == 1 else jnp.concatenate(parts, axis=0)
        else:
            value = self.came[0]
        if lax.axis_size("dp") != 4:
            value = lax.psum(value, "dp")
            if self.halve:
                middle = value.shape[1] // 2
                low = lax.axis_index("dp") % 2 == 0
                one, two = value[:, :middle], value[:, middle:]
                self.result = [jnp.where(low, one, two), jnp.where(low, two, one)]
            else:
                self.result = [value]
            return
        self.result = None
        if self.halve:
            middle = value.shape[1] // 2
            low = lax.axis_index("dp") % 2 == 0
            one, two = value[:, :middle], value[:, middle:]
            self.value = jnp.where(low, one, two)
            self.came = [exchange(jnp.where(low, two, one), "dp", 1)]
        else:
            self.value = value
            self.came = [exchange(value, "dp", 1)]

    def dp_second(self):
        if self.result is None:
            self.value = add(self.value, self.came[0])
            self.came = [exchange(self.value, "dp", 2)]

    def dp_third(self):
        if self.result is None:
            self.value = add(self.value, self.came[0])
            self.result = [self.value]
            if self.halve:
                self.result.append(exchange(self.value, "dp", 1))
        self.given = [give(value, self.layer) for value in self.result]


def unpack_feed_forward(place, *refs):
    gate, up, down = refs[8:]
    rows = gate.shape[0]
    narrow = down.shape[1]

    def emit(half, left, right):
        wide = (gate, up)[half]
        for i in range(2):
            wide[:, 2 * i * narrow:(2 * i + 1) * narrow] = left[i * rows:(i + 1) * rows, :].astype(F32)
            wide[:, (2 * i + 1) * narrow:(2 * i + 2) * narrow] = right[i * rows:(i + 1) * rows, :].astype(F32)
        top = 2 * half * rows
        down[top:top + rows, :] = left[2 * rows:, :].astype(F32)
        down[top + rows:top + 2 * rows, :] = right[2 * rows:, :].astype(F32)

    for sec in range(2):
        for low in range(2):

            @pl.when((place[0] == sec) & (place[place.shape[0] - 1] == low))
            def _(sec=sec, low=low):
                own, given = refs[4 * sec:4 * sec + 2], refs[4 * sec + 2:4 * sec + 4]
                emit(sec, own[low], own[1 - low])
                emit(1 - sec, given[low], given[1 - low])


def run_unpack_feed_forward(place, low, zero, one):
    rows, narrow = zero.result[0].shape[0] // 3, zero.result[0].shape[1]
    return pl.pallas_call(
        unpack_feed_forward,
        out_shape=(
            shape((rows, 4 * narrow), F32),
            shape((rows, 4 * narrow), F32),
            shape((4 * rows, narrow), F32),
        ),
        in_specs=[SM] + [VM] * 8,
        out_specs=(VM,) * 3,
        compiler_params=params(16),
        name="unpack_feed_forward",
    )(jnp.concatenate([place, low]), *zero.result, *zero.given, *one.result, *one.given)


def unpack_attention(place, own0, given0, own1, given1, wq, wk, wv, wo, gains):
    rows = wq.shape[0]

    def emit(half, value):
        left, right = ((wq, wk), (wo, wv))[half]
        left[...] = value[:rows, :WIDTH].astype(F32)
        right[...] = value[:rows, WIDTH:].astype(F32)
        if half == 0:
            gains[...] = value[rows:, :rows].astype(F32)[:2]

    for sec in range(2):

        @pl.when(place[0] == sec)
        def _(sec=sec):
            own, given = ((own0, given0), (own1, given1))[sec]
            emit(sec, own)
            emit(1 - sec, given)


def run_unpack_attention(place, zero, one):
    rows = zero.result[0].shape[0] - EXTRA
    return pl.pallas_call(
        unpack_attention,
        out_shape=(
            shape((rows, WIDTH), F32),
            shape((rows, KVW), F32),
            shape((rows, KVW), F32),
            shape((rows, WIDTH), F32),
            shape((2, rows), F32),
        ),
        in_specs=[SM] + [VM] * 4,
        out_specs=(VM,) * 5,
        compiler_params=params(16),
        name="unpack_attention",
    )(place, zero.result[0], zero.given[0], one.result[0], one.given[0])


def local(
    tokens,
    cotangent,
    doc_lengths,
    w_query,
    w_key,
    w_value,
    w_out,
    w_gate,
    w_up,
    w_down,
    gain_attn,
    gain_ffn,
):
    sec = lax.axis_index("section")
    first_section = sec == 0
    count = tokens.shape[2]
    place = jnp.stack([jnp.asarray(i, jnp.int32) for i in [sec] + piece_places()])
    gains = jnp.concatenate([gain_attn, gain_ffn], axis=0)
    own_at, rest_at, own_ff, rest_ff = run_pack(
        place, w_query[0], w_key[0], w_value[0], w_out[0], w_gate[0], w_up[0], w_down[0].T, gains
    )

    def own_pieces(own, rest):
        came_own, came_rest = swap(rest), swap(own)
        home = [own, came_own, rest, came_rest]
        return home, jnp.where(first_section, own, came_own), jnp.where(first_section, came_own, own)

    at_home, at_zero, at_one = own_pieces(own_at, rest_at)
    ff_home, ff_zero, ff_one = own_pieces(own_ff, rest_ff)
    tables = make_tables(pick(doc_lengths[0], sec, 0), count)
    x0 = jnp.swapaxes(pick(tokens[0], sec, 0), 0, 1)
    dy1 = jnp.swapaxes(pick(cotangent[0], sec, 0), 0, 1)

    near_at0 = first_hop(at_zero)
    near_at0, ff_zero = tie(near_at0, ff_zero)
    at0 = second_hop(near_at0)
    near_ff0 = first_hop(ff_zero)
    mid0, *saved0, gains0 = run_attention_forward(0, place, tables, x0, at_home + at0)
    mid0, near_ff0, at_one, ff_one = tie(mid0, near_ff0, at_one, ff_one)
    ff0 = second_hop(near_ff0)
    near_at1 = first_hop(at_one)
    near_ff1 = first_hop(ff_one)
    y0, gate0, up0 = run_feed_forward(0, place, mid0, gains0, ff_home + ff0)
    y0, near_at1, near_ff1 = tie(y0, near_at1, near_ff1)
    at1 = second_hop(near_at1)
    ff1 = second_hop(near_ff1)
    mid1, *saved1, gains1 = run_attention_forward(1, place, tables, y0, at_home + at1)
    mid1, *ff1 = tie(mid1, *ff1)
    y1, d_mid1, g_ffn1, ff_keep1, ff_send1 = run_feed_forward(1, place, mid1, gains1, ff_home + ff1, dy_t=dy1)

    ff_cut, at_rows = ff_keep1.shape[1] // 32 * 16, w_query.shape[1] + EXTRA
    ff_sum1 = Sum(place, ff_keep1, ff_send1, ff_cut, 1, True)
    dx1, dy0, at_keep1, at_send1 = run_attention_backward(
        1, place, tables, y0, gains1, d_mid1, g_ffn1, saved1, at_home + at1
    )
    dy0, *ff_sum1.came = tie(dy0, *ff_sum1.came)
    ff_sum1.fsdp_first()
    at_sum1 = Sum(place, at_keep1, at_send1, 0, 1, False)
    d_mid0, g_ffn0, ff_keep0, ff_send0 = run_feed_forward(
        0, place, mid0, gains0, ff_home + ff0, dy_t=dy0, kept=(gate0, up0)
    )
    d_mid0, ff_send0, *came = tie(d_mid0, ff_send0, *ff_sum1.came, *at_sum1.came)
    ff_sum1.came, at_sum1.came = came[:-1], came[-1:]
    ff_sum1.fsdp_second()
    at_sum1.fsdp_first()
    ff_sum0 = Sum(place, ff_keep0, ff_send0, ff_cut, 0, True)
    dx0, _, at_keep0, at_send0 = run_attention_backward(
        0, place, tables, x0, gains0, d_mid0, g_ffn0, saved0, at_home + at0
    )
    at_keep0, at_send0, *came = tie(at_keep0, at_send0, *ff_sum1.came, *at_sum1.came, *ff_sum0.came)
    ff_sum1.came, at_sum1.came, ff_sum0.came = came[:-2], came[-2:-1], came[-1:]
    at_sum0 = Sum(place, at_keep0, at_send0, at_rows, 0, False)
    ff_sum0.fsdp_first()
    ff_sum1.dp_first()
    at_sum1.fsdp_second()
    at_sum0.fsdp_first()
    ff_sum0.fsdp_second()
    ff_sum1.dp_second()
    at_sum1.dp_first()
    at_sum0.fsdp_second()
    ff_sum0.dp_first()
    at_sum1.dp_second()
    ff_sum1.dp_third()
    at_sum0.dp_first()
    ff_sum0.dp_second()
    at_sum1.dp_third()
    at_sum0.dp_second()
    ff_sum0.dp_third()
    at_sum0.dp_third()

    low = (lax.axis_index("dp") % 2).astype(jnp.int32)[None]
    gate, up, down = run_unpack_feed_forward(place, low, ff_sum0, ff_sum1)
    wq, wk, wv, wo, gain_grads = run_unpack_attention(place, at_sum0, at_sum1)

    def both_rows(own0, own1):
        back = swap(jnp.where(first_section, own1, own0))
        both = jnp.where(first_section, jnp.stack([own0, back]), jnp.stack([back, own1]))
        return jnp.swapaxes(both, 1, 2)[None, None]

    return (
        both_rows(y0, y1),
        both_rows(dx0, dx1),
        wq[None],
        wk[None],
        wv[None],
        wo[None],
        gate[None],
        up[None],
        down.T[None],
        gain_grads[:1],
        gain_grads[1:],
    )


def solution(mesh):
    whole = P(("fsdp", "dp"), None, None, None)
    weight = P("section", "fsdp", None)
    gain = P("section", "fsdp")
    rows = P("section", ("fsdp", "dp"), None, None, None)
    in_specs = (whole, whole, P(("fsdp", "dp"), None, None)) + (weight,) * 7 + (gain,) * 2
    out_specs = (rows, rows) + (weight,) * 7 + (gain,) * 2
    return jax.shard_map(local, mesh=mesh, in_specs=in_specs, out_specs=out_specs, check_vma=False)
```

```python
import functools
import jax
import jax.numpy as jnp
from jax import lax
from jax.experimental import pallas as pl
from jax.experimental.pallas import tpu as pltpu
from jax.sharding import PartitionSpec as P

HEADS = 9
KV_HEADS = 3
GROUP = HEADS // KV_HEADS
HEAD = 64
HALF = HEAD // 2
WIDTH = HEADS * HEAD
KVW = KV_HEADS * HEAD

epsilon = 1e-05
rope_base = 100000.0
masked_score = -1e30
SCALE = HEAD ** (-0.5)
EXTRA = 16
F32 = jnp.float32
BF16 = jnp.bfloat16


def nn(left, right):
    return lax.dot_general(left, right, (((1,), (0,)), ((), ())), preferred_element_type=F32)


def nt(left, right):
    return lax.dot_general(left, right, (((1,), (1,)), ((), ())), preferred_element_type=F32)


def inverse_root(values):
    return lax.rsqrt(jnp.mean(values * values, axis=-1, keepdims=True) + epsilon)


def norm_back(values, inv_root, gain, upstream):
    gain_grad = jnp.sum(upstream * values * inv_root, axis=0, keepdims=True)
    scaled = upstream * gain
    dot = jnp.mean(scaled * values, axis=-1, keepdims=True)
    return inv_root * scaled - values * (inv_root * inv_root * inv_root * dot), gain_grad


def sigmoid(values):
    return 0.5 * jnp.tanh(0.5 * values) + 0.5


def pack_attention(place, wq, wk, wv, wo, gains, own, rest):
    rows, cols = wq.shape[0], own.shape[1]

    def write(target, half):
        left, right = ((wq, wk), (wo, wv))[half]
        target[:rows, :] = jnp.concatenate([left[...], right[...]], axis=1)
        target[rows:, :] = jnp.zeros((EXTRA, cols), BF16)
        target[rows:, :rows] = jnp.concatenate(
            [gains[...].astype(F32), jnp.zeros((EXTRA - 2, rows), F32)], axis=0
        ).astype(BF16)

    for number in range(2):

        @pl.when(place[0] == number)
        def _(number=number):
            write(own, number)
            write(rest, 1 - number)


def pack_feed_forward(place, gate, up, down, own, rest):
    rows, cols = gate.shape[0], own.shape[1]
    down_cols = down.shape[1]
    half_down = down.shape[0] // 2

    def write(target, half):
        wide = (gate, up)[half]
        target[:rows, :] = wide[:, :cols]
        target[rows:2 * rows, :] = wide[:, cols:]
        for i in range(2):
            top = half * half_down + i * rows
            target[2 * rows:, i * down_cols:(i + 1) * down_cols] = down[top:top + rows, :]

    for number in range(2):

        @pl.when(place[0] == number)
        def _(number=number):
            write(own, number)
            write(rest, 1 - number)


def either(condition, first, second, target, sem):
    @pl.when(condition)
    def _():
        pltpu.make_async_copy(first, target, sem).start()

    @pl.when(jnp.logical_not(condition))
    def _():
        pltpu.make_async_copy(second, target, sem).start()

    return pltpu.make_async_copy(first, target, sem)


def start(source, target, sem):
    one = pltpu.make_async_copy(source, target, sem)
    one.start()
    return one


def sides(place, layer, pieces):
    sec = place[0]
    slots = place.shape[0] - 1
    found = []
    for number, (half, rest) in enumerate(((sec, pieces[4:3 + slots]), (1 - sec, pieces[3 + slots:]))):
        found.append((half, place[1], pieces[2 * number], pieces[2 * number + 1]))
        for slot, piece in enumerate(rest):
            found.append((half, place[2 + slot], piece, None))
    return found


def load_attention(place, layer, pieces, weights, gains, sems):
    rows = pieces[0].shape[0] - EXTRA
    home = place[0] == layer
    waits = []
    slots = place.shape[0] - 1
    for number, (half, owner, source, other) in enumerate(sides(place, layer, pieces)):
        target = weights.at[half, pl.ds(pl.multiple_of(owner * rows, 16), rows), :]
        window = slice(0, rows)
        if other is None:
            waits.append(start(source.at[window], target, sems.at[number]))
        else:
            waits.append(either(home, source.at[window], other.at[window], target, sems.at[number]))
        if number < slots and gains is not None:
            window, target, sem = slice(rows, rows + EXTRA), gains.at[owner], sems.at[2 * slots + number]
            if other is None:
                waits.append(start(source.at[window], target, sem))
            else:
                waits.append(either(home, source.at[window], other.at[window], target, sem))
    return waits


def load_feed_forward(place, layer, pieces, gate_up, down, sems):
    rows, cols = pieces[0].shape[0] // 3, pieces[0].shape[1]
    narrow = cols // 2
    home = place[0] == layer
    early, late = [], []
    for number, (half, owner, source, other) in enumerate(sides(place, layer, pieces)):
        for part in range(4):
            if part < 2:
                window = (slice(part * rows, (part + 1) * rows), slice(None))
                target = gate_up.at[half, pl.ds(pl.multiple_of(owner * rows, 16), rows), part * cols:(part + 1) * cols]
            else:
                i = part - 2
                window = (slice(2 * rows, 3 * rows), slice(i * narrow, (i + 1) * narrow))
                top = pl.multiple_of(half * (2 * rows) + i * rows, 16)
                target = down.at[pl.ds(top, rows), pl.ds(pl.multiple_of(owner * narrow, 128), narrow)]
            sem = sems.at[4 * number + part]
            if other is None:
                one = start(source.at[window], target, sem)
            else:
                one = either(home, source.at[window], other.at[window], target, sem)
            (early if part < 2 else late).append(one)
    return early, late


def fill_bias(first, bias):
    count = bias.shape[0]
    key = lax.broadcasted_iota(jnp.int32, (count, count), 0)
    query = lax.broadcasted_iota(jnp.int32, (count, count), 1)
    allowed = (key >= first[...]) & (key <= query)
    bias[...] = jnp.where(allowed, 0.0, masked_score).astype(F32)


def attention_forward(place, first, cos, sin, x_t, *rest, layer, tile, count_pieces):
    pieces = rest[:count_pieces]
    mid, q_out, k_out, v_out, o_out, lse_out, gain_out, weights, gain_parts, bias, sems = rest[count_pieces:]
    owners = gain_parts.shape[0]
    rows = weights.shape[1] // owners
    waits = load_attention(place, layer, pieces, weights, gain_parts, sems)
    count = x_t.shape[1]
    values = x_t[...].T.astype(F32)
    scaled = values * inverse_root(values)
    fill_bias(first, bias)
    for one in waits:
        one.wait()
    gain = jnp.concatenate([gain_parts[f][:2, :rows].astype(F32) for f in range(owners)], axis=1)
    gain_out[...] = gain
    normed = (scaled * gain[:1]).astype(BF16)
    qk = nt(weights[0].T, normed)
    v_out[...] = nt(weights[1, :, WIDTH:].T, normed).astype(BF16)
    c, s = cos[...], sin[...]

    def turned(part):
        low, high = part[:HALF], part[HALF:]
        return jnp.concatenate([low * c - high * s, high * c + low * s], axis=0)

    for head in range(HEADS):
        span = slice(head * HEAD, (head + 1) * HEAD)
        q_out[span, :] = (turned(qk[span]) * SCALE).astype(BF16)
    for j in range(KV_HEADS):
        at = WIDTH + j * HEAD
        k_out[j * HEAD:(j + 1) * HEAD, :] = turned(qk[at:at + HEAD]).astype(BF16)
    for j in range(KV_HEADS):
        keys = k_out[j * HEAD:(j + 1) * HEAD, :].T
        vals = v_out[j * HEAD:(j + 1) * HEAD, :]
        for g in range(GROUP):
            head = j * GROUP + g
            span = slice(head * HEAD, (head + 1) * HEAD)
            for at in range(0, count, tile):
                end = at + tile
                scores = nn(keys[:end], q_out[span, at:end]) + bias[:end, at:end]
                top = jnp.max(scores, axis=0, keepdims=True)
                power = jnp.exp(scores - top)
                total = jnp.sum(power, axis=0, keepdims=True)
                mixed = nn(vals[:, :end], power.astype(BF16))
                o_out[span, at:end] = (mixed / total).astype(BF16)
                lse_out[head:head + 1, at:end] = top + jnp.log(total)
    mid[...] = values + nn(o_out[...].T, weights[1, :, :WIDTH])


def attention_backward(place, first, cos, sin, x_t, gain, d_mid, g_ffn, q, k, v, o, lse, *rest, layer, tile, count_pieces):
    pieces = rest[:count_pieces]
    dx, dx_low, keep, send, weights, grads, bias, g_out, d_q, d_k, d_v, sems, sems_out = rest[count_pieces:]
    owners = grads.shape[1]
    rows = weights.shape[1] // owners
    sec = place[0]
    waits = load_attention(place, layer, pieces, weights, None, sems)
    count = x_t.shape[1]
    g_mid = d_mid[...].astype(BF16)
    fill_bias(first, bias)
    for one in waits:
        one.wait()
    g_out[...] = nt(weights[1, :, :WIDTH], g_mid).astype(BF16)

    def store(side, columns, value):
        for owner in range(owners):
            grads[side, owner, :rows, columns] = value[owner * rows:(owner + 1) * rows].astype(BF16)

    store(1, slice(0, WIDTH), nn(o[...], g_mid))
    c, s = cos[...], sin[...]

    def turned_back(part):
        low, high = part[:HALF], part[HALF:]
        return jnp.concatenate([low * c + high * s, high * c - low * s], axis=0)

    for j in range(KV_HEADS):
        own = slice(j * HEAD, (j + 1) * HEAD)
        keys_t = k[own, :]
        keys = keys_t.T
        vals = v[own, :].T
        k_sum = [jnp.zeros((HEAD, tile), F32) for _ in range(count // tile)]
        v_sum = [jnp.zeros((HEAD, tile), F32) for _ in range(count // tile)]
        for g in range(GROUP):
            head = j * GROUP + g
            span = slice(head * HEAD, (head + 1) * HEAD)
            for at in range(0, count, tile):
                end = at + tile
                q_part = q[span, at:end]
                g_part = g_out[span, at:end]
                power = jnp.exp(nn(keys[:end], q_part) + bias[:end, at:end] - lse[head:head + 1, at:end])
                d_prob = nn(vals[:end], g_part)
                delta = jnp.sum(power * d_prob, axis=0, keepdims=True)
                d_score = (power * (d_prob - delta)).astype(BF16)
                power = power.astype(BF16)
                v_add = nt(g_part, power)
                k_add = nt(q_part, d_score)
                for i in range(end // tile):
                    v_sum[i] = v_sum[i] + v_add[:, i * tile:(i + 1) * tile]
                    k_sum[i] = k_sum[i] + k_add[:, i * tile:(i + 1) * tile]
                d_q[span, at:end] = nn(keys_t[:, :end], d_score) * SCALE
        d_k[own, :] = jnp.concatenate(k_sum, axis=1)
        d_v[own, :] = jnp.concatenate(v_sum, axis=1).astype(BF16)
    turned = [turned_back(d_q[h * HEAD:(h + 1) * HEAD, :]).astype(BF16) for h in range(HEADS)]
    turned += [turned_back(d_k[h * HEAD:(h + 1) * HEAD, :]).astype(BF16) for h in range(KV_HEADS)]
    d_qk = jnp.concatenate(turned, axis=0)
    values = x_t[...].T.astype(F32)
    inv = inverse_root(values)
    attn_gain = gain[:1, :]
    normed_t = (values * inv * attn_gain).astype(BF16).T
    store(0, slice(None), nt(normed_t, d_qk))
    store(1, slice(WIDTH, None), nt(normed_t, d_v[...]))
    d_normed = (nn(weights[0], d_qk) + nn(weights[1, :, WIDTH:], d_v[...])).T
    back, gain_grad = norm_back(values, inv, attn_gain, d_normed)
    for owner in range(owners):
        span = slice(owner * rows, (owner + 1) * rows)
        both = jnp.concatenate([gain_grad[:, span], g_ffn[:, span]], axis=0)
        grads[:, owner, rows:, :] = jnp.zeros((2, EXTRA, grads.shape[3]), BF16)
        padded = jnp.concatenate([both, jnp.zeros((EXTRA - 2, rows), F32)], axis=0)
        grads[0, owner, rows:, :rows] = padded.astype(BF16)
    out = [start(grads.at[1 - sec], send, sems_out.at[0]), start(grads.at[sec], keep, sems_out.at[1])]
    total = (d_mid[...] + back).T
    dx[...] = total
    dx_low[...] = total.astype(BF16)
    for one in out:
        one.wait()


def feed_forward(place, mid, gain, *rest, layer, forward, backward, block, count_pieces):
    pieces = rest[:count_pieces]
    rest = list(rest[count_pieces:])
    take = lambda: rest.pop(0)
    dy_t = take() if backward else None
    kept = (take(), take()) if backward and not forward else None
    y_t = take() if forward else None
    keeping = (take(), take()) if forward and not backward else None
    if backward:
        d_mid, d_gain, keep, send = take(), take(), take(), take()
    gate_up, down, sems = take(), take(), take()
    if backward:
        grads, sems_out = take(), take()
    sec = place[0]
    early, late = load_feed_forward(place, layer, pieces, gate_up, down, sems)
    values = mid[...]
    inv = inverse_root(values)
    ffn_gain = gain[1:, :]
    normed = (values * inv * ffn_gain).astype(BF16)
    if backward:
        normed_t = normed.T
        dy = dy_t[...].T
        rows = grads.shape[2] // 3
        owners = grads.shape[1]
    for one in early:
        one.wait()
    units = down.shape[1]
    result, d_normed = None, None
    out = []
    for number, at in enumerate(range(0, units, block)):
        span = slice(at, at + block)
        if kept is None:
            gate, up = nn(normed, gate_up[0, :, span]), nn(normed, gate_up[1, :, span])
        else:
            gate, up = kept[0][:, span].astype(F32), kept[1][:, span].astype(F32)
        sg = sigmoid(gate)
        swish = gate * sg
        hidden = (swish * up).astype(BF16)
        if keeping is not None:
            keeping[0][:, span] = gate.astype(BF16)
            keeping[1][:, span] = up.astype(BF16)
        if number == 0:
            for one in late:
                one.wait()
        if forward:
            part = nt(hidden, down[:, span])
            result = part if result is None else result + part
        if backward:
            d_hidden = nn(dy, down[:, span])
            g_gate = (d_hidden * up * (sg * (1.0 + gate * (1.0 - sg)))).astype(BF16)
            g_up = (d_hidden * swish).astype(BF16)
            for half, grad in ((0, g_gate), (1, g_up)):
                value = nn(normed_t, grad).astype(BF16)
                for owner in range(owners):
                    grads[half, owner, number * rows:(number + 1) * rows, :] = value[owner * rows:(owner + 1) * rows]
            value = nn(dy_t[...], hidden).astype(BF16)
            narrow = block // 2
            for i in range(2):
                for half in range(2):
                    for k in range(2):
                        top = (2 * half + k) * rows
                        grads[half, 2 * number + i, 2 * rows:, k * narrow:(k + 1) * narrow] = value[
                            top:top + rows, i * narrow:(i + 1) * narrow
                        ]
            for side, target in ((1 - sec, send), (sec, keep)):
                for window in (
                    (slice(None), slice(number * rows, (number + 1) * rows)),
                    (slice(2 * number, 2 * number + 2), slice(2 * rows, 3 * rows)),
                ):
                    out.append(start(grads.at[(side,) + window], target.at[window], sems_out.at[len(out)]))
            part = nt(g_gate, gate_up[0, :, span]) + nt(g_up, gate_up[1, :, span])
            d_normed = part if d_normed is None else d_normed + part
    if forward:
        y_t[...] = (values + result).astype(BF16).T
    if backward:
        back, gain_grad = norm_back(values, inv, ffn_gain, d_normed)
        d_gain[...] = gain_grad
        d_mid[...] = dy.astype(F32) + back
        for one in out:
            one.wait()


VM = pl.BlockSpec(memory_space=pltpu.VMEM)
SM = pl.BlockSpec(memory_space=pltpu.SMEM)
AN = pl.BlockSpec(memory_space=pl.ANY)


def params(mib):
    return pltpu.CompilerParams(vmem_limit_bytes=mib * 1024 * 1024)


def shape(dims, kind):
    return jax.ShapeDtypeStruct(dims, kind)


def cost(gigaflops):
    return pl.CostEstimate(flops=int(gigaflops * 10**6), bytes_accessed=10**4, transcendentals=0)


def run_pack(kernel, name, place, dims, *arrays):
    return pl.pallas_call(
        kernel,
        out_shape=(shape(dims, BF16),) * 2,
        in_specs=[SM] + [VM] * len(arrays),
        out_specs=(VM,) * 2,
        compiler_params=params(56),
        name=name,
    )(place, *arrays)


def run_attention_forward(layer, place, tables, x_t, pieces, tile=256):
    first, cos, sin = tables
    wide, count = x_t.shape
    cols = pieces[0].shape[1]
    owners = place.shape[0] - 1
    return pl.pallas_call(
        functools.partial(attention_forward, layer=layer, tile=tile, count_pieces=len(pieces)),
        out_shape=(
            shape((count, wide), F32),
            shape((WIDTH, count), BF16),
            shape((KVW, count), BF16),
            shape((KVW, count), BF16),
            shape((WIDTH, count), BF16),
            shape((HEADS, count), F32),
            shape((2, wide), F32),
        ),
        in_specs=[SM] + [VM] * 4 + [AN] * len(pieces),
        out_specs=(VM,) * 7,
        scratch_shapes=[
            pltpu.VMEM((2, wide, cols), BF16),
            pltpu.VMEM((owners, EXTRA, cols), BF16),
            pltpu.VMEM((count, count), F32),
            pltpu.SemaphoreType.DMA((3 * owners,)),
        ],
        compiler_params=params(56),
        cost_estimate=cost(6),
        name="attention_forward",
    )(place, first, cos, sin, x_t, *pieces)


def run_attention_backward(layer, place, tables, x_t, gain, d_mid, g_ffn, saved, pieces, tile=256):
    first, cos, sin = tables
    wide, count = x_t.shape
    cols = pieces[0].shape[1]
    owners = place.shape[0] - 1
    padded = wide // owners + EXTRA
    return pl.pallas_call(
        functools.partial(attention_backward, layer=layer, tile=tile, count_pieces=len(pieces)),
        out_shape=(
            shape((wide, count), F32),
            shape((wide, count), BF16),
            shape((owners, padded, cols), BF16),
            shape((owners, padded, cols), BF16),
        ),
        in_specs=[SM] + [VM] * 12 + [AN] * len(pieces),
        out_specs=(VM, VM, AN, AN),
        scratch_shapes=[
            pltpu.VMEM((2, wide, cols), BF16),
            pltpu.VMEM((2, owners, padded, cols), BF16),
            pltpu.VMEM((count, count), F32),
            pltpu.VMEM((WIDTH, count), BF16),
            pltpu.VMEM((WIDTH, count), F32),
            pltpu.VMEM((KVW, count), F32),
            pltpu.VMEM((KVW, count), BF16),
            pltpu.SemaphoreType.DMA((2 * owners,)),
            pltpu.SemaphoreType.DMA((2,)),
        ],
        compiler_params=params(56),
        cost_estimate=cost(10),
        name="attention_backward",
    )(place, first, cos, sin, x_t, gain, d_mid, g_ffn, *saved, *pieces)


def run_feed_forward(layer, place, mid, gain, pieces, dy_t=None, kept=(), block=768):
    backward = dy_t is not None
    forward = not kept
    count, wide = mid.shape
    owners = place.shape[0] - 1
    rows, cols = pieces[0].shape[0] // 3, pieces[0].shape[1]
    out_shape, out_specs = [], []
    scratch = [
        pltpu.VMEM((2, wide, 2 * cols), BF16),
        pltpu.VMEM((wide, 2 * cols), BF16),
        pltpu.SemaphoreType.DMA((8 * owners,)),
    ]
    if forward:
        out_shape.append(shape((wide, count), BF16))
        out_specs.append(VM)
        if not backward:
            out_shape += [shape((count, 2 * cols), BF16)] * 2
            out_specs += [VM] * 2
    if backward:
        out_shape += [
            shape((count, wide), F32),
            shape((1, wide), F32),
            shape((owners, 3 * rows, cols), BF16),
            shape((owners, 3 * rows, cols), BF16),
        ]
        out_specs += [VM, VM, AN, AN]
        scratch += [
            pltpu.VMEM((2, owners, 3 * rows, cols), BF16),
            pltpu.SemaphoreType.DMA((8,)),
        ]
    flops = (7 if forward else 0) + (14 if backward else 0)
    extra = ([dy_t] if backward else []) + list(kept)
    return pl.pallas_call(
        functools.partial(
            feed_forward, layer=layer, forward=forward, backward=backward, block=block, count_pieces=len(pieces)
        ),
        out_shape=tuple(out_shape),
        in_specs=[SM, VM, VM] + [AN] * len(pieces) + [VM] * len(extra),
        out_specs=tuple(out_specs),
        scratch_shapes=scratch,
        compiler_params=params(56),
        cost_estimate=cost(flops),
        name="feed_forward",
    )(place, mid, gain, *pieces, *extra)


def make_tables(lengths, count):
    ends = jnp.cumsum(lengths)
    starts = ends - lengths
    places = jnp.arange(count, dtype=jnp.int32)
    document = jnp.sum((places[:, None] >= ends[None, :]).astype(jnp.int32), axis=1)
    inside = document[:, None] == jnp.arange(lengths.shape[0], dtype=jnp.int32)[None, :]
    first = jnp.sum(jnp.where(inside, starts[None, :], 0), axis=1)
    position = (places - first).astype(F32)
    frequency = rope_base ** (-(jnp.arange(HALF, dtype=F32) * 2.0 / HEAD))
    angles = frequency[:, None] * position[None, :]
    return first[None, :], jnp.cos(angles), jnp.sin(angles)


def swap(value):
    return lax.ppermute(value, "section", [(0, 1), (1, 0)])


def give(value, target):
    return lax.ppermute(value, "section", [(1 - target, target)])


def exchange(value, axis, bit):
    count = lax.axis_size(axis)
    return lax.ppermute(value, axis, [(i, i ^ bit) for i in range(count)])


def mixed_exchange(value, even_bit, odd_bit):
    owners, replicas = lax.axis_size("fsdp"), lax.axis_size("dp")
    pairs = []
    for i in range(owners):
        for z in range(replicas):
            partner = i ^ (odd_bit if z % 2 else even_bit)
            pairs.append((i * replicas + z, partner * replicas + z))
    return lax.ppermute(value, ("fsdp", "dp"), pairs)


def paired():
    return lax.axis_size("fsdp") == 4 and lax.axis_size("dp") % 2 == 0


def piece_places():
    own = lax.axis_index("fsdp")
    if not paired():
        count = lax.axis_size("fsdp")
        return [own] + [(own + i) % count for i in range(1, count)]
    odd = lax.axis_index("dp") % 2
    near, far = jnp.where(odd == 1, own ^ 2, own ^ 1), jnp.where(odd == 1, own ^ 1, own ^ 2)
    return [own, near, own ^ 3, far]


def first_hop(value):
    if not paired():
        return lax.all_gather(value, "fsdp")
    return mixed_exchange(value, 1, 2)


def second_hop(near):
    if not paired():
        count = lax.axis_size("fsdp")
        own = lax.axis_index("fsdp")
        return [pick(near, (own + i) % count, 0) for i in range(1, count)]
    return [near, mixed_exchange(near, 2, 1), exchange(near, "dp", 1)]


def shared(pieces):
    return pieces + [swap(piece) for piece in pieces]


def tie(*values):
    return lax.optimization_barrier(values)


def add(left, right):
    return (left.astype(F32) + right.astype(F32)).astype(BF16)


def pick(value, index, axis):
    return lax.dynamic_index_in_dim(value, index, axis, keepdims=False)


def split_first(place, keep, came, *outs, cut):
    y, x = place[1] // 2, place[1] % 2
    outs = list(outs)
    total = keep.shape[1]
    for by_x, low, high in ((True, 0, cut), (False, cut, total)):
        if low == high:
            continue
        hold, away = outs.pop(0), outs.pop(0)
        for i in range(2):
            for target, mine in ((hold, True), (away, False)):
                bit_x, bit_y = (x, y) if mine else (1 - x, 1 - y)
                block = 2 * i + bit_x if by_x else 2 * bit_y + i
                target[i] = (
                    keep[block, low:high].astype(F32) + came[block, low:high].astype(F32)
                ).astype(BF16)


def run_split_first(place, keep, came, cut):
    owners, total, cols = keep.shape
    out = []
    for low, high in ((0, cut), (cut, total)):
        if high > low:
            out += [shape((2, high - low, cols), BF16)] * 2
    return pl.pallas_call(
        functools.partial(split_first, cut=cut),
        out_shape=tuple(out),
        in_specs=[SM, VM, VM],
        out_specs=(VM,) * len(out),
        compiler_params=params(24),
        name="split_first",
    )(place, keep, came)


def split_second(place, *refs, cut, total):
    y, x = place[1] // 2, place[1] % 2
    ranges = [(True, 0, cut), (False, cut, total)]
    ranges = [r for r in ranges if r[2] > r[1]]
    ins, outs = list(refs[:2 * len(ranges)]), list(refs[2 * len(ranges):])
    for by_x, low, high in ranges:
        hold, came = ins.pop(0), ins.pop(0)
        stay, away = outs.pop(0), outs.pop(0)
        bit = y if by_x else x
        stay[...] = (hold[bit].astype(F32) + came[bit].astype(F32)).astype(BF16)
        away[...] = (hold[1 - bit].astype(F32) + came[1 - bit].astype(F32)).astype(BF16)


def run_split_second(place, parts, cut, total):
    out = []
    for hold in parts[::2]:
        out += [shape(hold.shape[1:], BF16)] * 2
    return pl.pallas_call(
        functools.partial(split_second, cut=cut, total=total),
        out_shape=tuple(out),
        in_specs=[SM] + [VM] * len(parts),
        out_specs=(VM,) * len(out),
        compiler_params=params(24),
        name="split_second",
    )(place, *parts)


class Sum:
    def __init__(self, place, keep, send, cut, layer, pairs=False):
        self.place, self.keep, self.cut, self.layer, self.pairs = place, keep, cut, layer, pairs
        self.total = keep.shape[1]
        self.direct = lax.axis_size("fsdp") == 4
        self.chain = lax.axis_size("dp") == 4
        self.came = [swap(send)]
        self.hold = [keep]

    def bits(self, second):
        order = (2, 1) if second else (1, 2)
        found = [order[0]] if self.cut > 0 else []
        return found + ([order[1]] if self.cut < self.total else [])

    def fsdp_first(self):
        if not self.direct:
            whole = add(self.hold[0], self.came[0])
            whole = lax.psum_scatter(whole, "fsdp", scatter_dimension=0, tiled=False)
            parts = [whole[:self.cut], whole[self.cut:]]
            self.hold = self.came = [part for part in parts if part.shape[0]]
            return
        parts = run_split_first(self.place, self.hold[0], self.came[0], self.cut)
        self.hold = list(parts[::2])
        self.came = [exchange(p, "fsdp", b) for p, b in zip(parts[1::2], self.bits(False))]

    def fsdp_second(self):
        if not self.direct:
            return
        parts = [p for pair in zip(self.hold, self.came) for p in pair]
        parts = run_split_second(self.place, parts, self.cut, self.total)
        self.hold = list(parts[::2])
        self.came = [exchange(p, "fsdp", b) for p, b in zip(parts[1::2], self.bits(True))]

    def dp_first(self, i):
        if self.direct:
            self.hold[i] = add(self.hold[i], self.came[i])
        if not self.chain:
            self.came[i] = lax.psum(self.hold[i], "dp")
        elif self.pairs:
            self.came[i] = exchange(self.hold[i], "dp", 1)
        else:
            self.came[i] = lax.ppermute(self.hold[i], "dp", [(0, 1), (3, 2)])

    def dp_second(self, i):
        if self.chain:
            self.hold[i] = add(self.hold[i], self.came[i])
            if self.pairs:
                self.came[i] = exchange(self.hold[i], "dp", 2)
            else:
                self.came[i] = lax.ppermute(self.hold[i], "dp", [(1, 2), (2, 1)])

    def dp_third(self, i):
        if self.chain:
            self.hold[i] = add(self.hold[i], self.came[i])
            if not self.pairs:
                self.came[i] = lax.ppermute(self.hold[i], "dp", [(1, 0), (2, 3)])

    def finish(self):
        place = lax.axis_index("dp")
        middle = (place == 1) | (place == 2)
        if not self.chain:
            self.result = self.came
        elif self.pairs:
            self.result = self.hold
        else:
            self.result = [jnp.where(middle, h, c) for h, c in zip(self.hold, self.came)]
        self.given = [give(value, self.layer) for value in self.result]


def unpack_feed_forward(place, own0, own0_more, given0, given0_more, own1, own1_more, given1, given1_more, gate, up, down):
    rows = gate.shape[0]
    narrow = down.shape[1]

    def emit(half, low, high):
        value = jnp.concatenate([low[...], high[...]], axis=0).astype(F32)
        wide = (gate, up)[half]
        for i in range(2):
            wide[:, 2 * i * narrow:(2 * i + 2) * narrow] = value[i * rows:(i + 1) * rows]
        top = 2 * half * rows
        down[top:top + rows, :] = value[2 * rows:, :narrow]
        down[top + rows:top + 2 * rows, :] = value[2 * rows:, narrow:]

    @pl.when(place[0] == 0)
    def _():
        emit(0, own0, own0_more)
        emit(1, given0, given0_more)

    @pl.when(place[0] == 1)
    def _():
        emit(1, own1, own1_more)
        emit(0, given1, given1_more)


def run_unpack_feed_forward(place, zero, one):
    rows = (zero.result[0].shape[0] + zero.result[1].shape[0]) // 3
    cols = zero.result[0].shape[1]
    return pl.pallas_call(
        unpack_feed_forward,
        out_shape=(
            shape((rows, 2 * cols), F32),
            shape((rows, 2 * cols), F32),
            shape((4 * rows, cols // 2), F32),
        ),
        in_specs=[SM] + [VM] * 8,
        out_specs=(VM,) * 3,
        compiler_params=params(32),
        name="unpack_feed_forward",
    )(place, *zero.result, *zero.given, *one.result, *one.given)


def unpack_attention(place, own0, given0, own1, given1, wq, wk, wv, wo, gains):
    rows = wq.shape[0]

    def emit(half, value):
        left, right = ((wq, wk), (wo, wv))[half]
        left[...] = value[:rows, :WIDTH].astype(F32)
        right[...] = value[:rows, WIDTH:].astype(F32)
        if half == 0:
            gains[...] = value[rows:, :rows].astype(F32)[:2]

    for sec in range(2):

        @pl.when(place[0] == sec)
        def _(sec=sec):
            own, given = ((own0, given0), (own1, given1))[sec]
            emit(sec, own)
            emit(1 - sec, given)


def run_unpack_attention(place, zero, one):
    rows = zero.result[0].shape[0] - EXTRA
    return pl.pallas_call(
        unpack_attention,
        out_shape=(
            shape((rows, WIDTH), F32),
            shape((rows, KVW), F32),
            shape((rows, KVW), F32),
            shape((rows, WIDTH), F32),
            shape((2, rows), F32),
        ),
        in_specs=[SM] + [VM] * 4,
        out_specs=(VM,) * 5,
        compiler_params=params(16),
        name="unpack_attention",
    )(place, zero.result[0], zero.given[0], one.result[0], one.given[0])


def local(
    tokens,
    cotangent,
    doc_lengths,
    w_query,
    w_key,
    w_value,
    w_out,
    w_gate,
    w_up,
    w_down,
    gain_attn,
    gain_ffn,
):
    sec = lax.axis_index("section")
    first_section = sec == 0
    count = tokens.shape[2]
    place = jnp.stack([jnp.asarray(i, jnp.int32) for i in [sec] + piece_places()])
    gains = jnp.concatenate([gain_attn, gain_ffn], axis=0)
    rows, cols = w_query.shape[1], w_query.shape[2] + w_key.shape[2]
    own_at, rest_at = run_pack(
        pack_attention, "pack_attention", place, (rows + EXTRA, cols), w_query[0], w_key[0], w_value[0], w_out[0], gains
    )
    own_ff, rest_ff = run_pack(
        pack_feed_forward, "pack_feed_forward", place, (3 * rows, cols), w_gate[0], w_up[0], w_down[0].T
    )

    def own_pieces(own, rest):
        came_own, came_rest = swap(rest), swap(own)
        home = [own, came_own, rest, came_rest]
        return home, jnp.where(first_section, own, came_own), jnp.where(first_section, came_own, own)

    at_home, at_zero, at_one = own_pieces(own_at, rest_at)
    ff_home, ff_zero, ff_one = own_pieces(own_ff, rest_ff)
    tables = make_tables(pick(doc_lengths[0], sec, 0), count)
    x0 = jnp.swapaxes(pick(tokens[0], sec, 0), 0, 1)
    dy1 = jnp.swapaxes(pick(cotangent[0], sec, 0), 0, 1)

    near_at0 = first_hop(at_zero)
    near_at0, ff_zero = tie(near_at0, ff_zero)
    at0 = shared(second_hop(near_at0))
    near_ff0 = first_hop(ff_zero)
    mid0, *saved0, gains0 = run_attention_forward(0, place, tables, x0, at_home + at0)
    mid0, near_ff0, at_one, ff_one = tie(mid0, near_ff0, at_one, ff_one)

    ff0 = second_hop(near_ff0)
    near_at1 = first_hop(at_one)
    near_ff1 = first_hop(ff_one)
    near_at1, *ff0 = tie(near_at1, *ff0)
    ff0 = shared(ff0)
    at1 = second_hop(near_at1)
    y0, gate0, up0 = run_feed_forward(0, place, mid0, gains0, ff_home + ff0)
    y0, near_ff1, *at1 = tie(y0, near_ff1, *at1)

    at1 = shared(at1)
    ff1 = second_hop(near_ff1)
    mid1, *saved1, gains1 = run_attention_forward(1, place, tables, y0, at_home + at1)
    mid1, *ff1 = tie(mid1, *ff1)
    ff1 = shared(ff1)
    y1, d_mid1, g_ffn1, ff_keep1, ff_send1 = run_feed_forward(1, place, mid1, gains1, ff_home + ff1, dy_t=dy1)

    sums = []

    def after(waited, *others):
        cells = [(one.came, i) for one, i in waited]
        for one in sums:
            cells += [(one.hold, i) for i in range(len(one.hold))]
        held = list(tie(*others, *[array[i] for array, i in cells]))
        for (array, i), value in zip(cells, held[len(others):]):
            array[i] = value
        return held[:len(others)]

    def both_rows(own0, own1):
        back = swap(jnp.where(first_section, own1, own0))
        both = jnp.where(first_section, jnp.stack([own0, back]), jnp.stack([back, own1]))
        return jnp.swapaxes(both, 1, 2)[None, None]

    ff_cut, at_rows = ff_keep1.shape[1] // 32 * 16, w_query.shape[1] + EXTRA
    f1 = Sum(place, ff_keep1, ff_send1, ff_cut, 1)
    sums.append(f1)
    dx1, dy0, at_keep1, at_send1 = run_attention_backward(
        1, place, tables, y0, gains1, d_mid1, g_ffn1, saved1, at_home + at1
    )
    dy0, at_keep1, at_send1 = after([(f1, 0)], dy0, at_keep1, at_send1)

    f1.fsdp_first()
    a1 = Sum(place, at_keep1, at_send1, 0, 1)
    sums.append(a1)
    (dy0,) = after([], dy0)
    d_mid0, g_ffn0, ff_keep0, ff_send0 = run_feed_forward(
        0, place, mid0, gains0, ff_home + ff0, dy_t=dy0, kept=(gate0, up0)
    )
    d_mid0, ff_keep0, ff_send0 = after([(f1, 0), (f1, 1), (a1, 0)], d_mid0, ff_keep0, ff_send0)

    f0 = Sum(place, ff_keep0, ff_send0, ff_cut, 0)
    sums.append(f0)
    f1.fsdp_second()
    a1.fsdp_first()
    (d_mid0,) = after([(f0, 0), (f1, 0), (f1, 1), (a1, 0)], d_mid0)

    f0.fsdp_first()
    f1.dp_first(0)
    f1.dp_first(1)
    a1.fsdp_second()
    (d_mid0,) = after([], d_mid0)
    dx0, _, at_keep0, at_send0 = run_attention_backward(
        0, place, tables, x0, gains0, d_mid0, g_ffn0, saved0, at_home + at0
    )
    at_send0, at_keep0 = after([(f0, 0), (f0, 1), (f1, 0), (f1, 1), (a1, 0)], at_send0, at_keep0)

    f0.fsdp_second()
    f1.dp_second(0)
    a1.dp_first(0)
    a0 = Sum(place, at_keep0, at_send0, at_rows, 0, True)
    sums.append(a0)
    (y0, y1) = after([(f0, 0), (f0, 1), (f1, 0), (a1, 0), (a0, 0)], y0, y1)

    f0.dp_first(0)
    f1.dp_second(1)
    a1.dp_second(0)
    a0.fsdp_first()
    dx0, dx1 = after([(f0, 0), (f1, 1), (a1, 0), (a0, 0)], dx0, dx1)

    f0.dp_second(0)
    f0.dp_first(1)
    f1.dp_third(0)
    a1.dp_third(0)
    a0.fsdp_second()
    after([(f0, 0), (f0, 1), (f1, 0), (a1, 0), (a0, 0)])

    f0.dp_third(0)
    f0.dp_second(1)
    f1.dp_third(1)
    a0.dp_first(0)
    after([(f0, 0), (f0, 1), (f1, 1), (a0, 0)])

    f0.dp_third(1)
    a0.dp_second(0)
    f1.finish()
    a1.finish()
    after([(f0, 1), (a0, 0)])

    a0.dp_third(0)
    f0.finish()
    a0.finish()
    gate, up, down = run_unpack_feed_forward(place, f0, f1)
    wq, wk, wv, wo, gain_grads = run_unpack_attention(place, a0, a1)

    return (
        both_rows(y0, y1),
        both_rows(dx0, dx1),
        wq[None],
        wk[None],
        wv[None],
        wo[None],
        gate[None],
        up[None],
        down.T[None],
        gain_grads[:1],
        gain_grads[1:],
    )


def solution(mesh):
    whole = P(("fsdp", "dp"), None, None, None)
    weight = P("section", "fsdp", None)
    gain = P("section", "fsdp")
    rows = P("section", ("fsdp", "dp"), None, None, None)
    in_specs = (whole, whole, P(("fsdp", "dp"), None, None)) + (weight,) * 7 + (gain,) * 2
    out_specs = (rows, rows) + (weight,) * 7 + (gain,) * 2
    return jax.shard_map(local, mesh=mesh, in_specs=in_specs, out_specs=out_specs, check_vma=False)
```

```python
import functools
import jax
import jax.numpy as jnp
from jax import lax
from jax.experimental import pallas as pl
from jax.experimental.pallas import tpu as pltpu
from jax.sharding import PartitionSpec as P

HEADS = 9
KV_HEADS = 3
GROUP = HEADS // KV_HEADS
HEAD = 64
HALF = HEAD // 2
WIDTH = HEADS * HEAD
KVW = KV_HEADS * HEAD

epsilon = 1e-05
rope_base = 100000.0
masked_score = -1e30
SCALE = HEAD ** (-0.5)
EXTRA = 16
F32 = jnp.float32
BF16 = jnp.bfloat16


def nn(left, right):
    return lax.dot_general(left, right, (((1,), (0,)), ((), ())), preferred_element_type=F32)


def nt(left, right):
    return lax.dot_general(left, right, (((1,), (1,)), ((), ())), preferred_element_type=F32)


def inverse_root(values):
    return lax.rsqrt(jnp.mean(values * values, axis=-1, keepdims=True) + epsilon)


def norm_back(values, inv_root, gain, upstream):
    gain_grad = jnp.sum(upstream * values * inv_root, axis=0, keepdims=True)
    scaled = upstream * gain
    dot = jnp.mean(scaled * values, axis=-1, keepdims=True)
    return inv_root * scaled - values * (inv_root * inv_root * inv_root * dot), gain_grad


def sigmoid(values):
    return 0.5 * jnp.tanh(0.5 * values) + 0.5


def pack_first(place, wq, wk, wv, wo, gain_attn, gain_ffn, down, own, rest):
    rows, cols = wq.shape[0], own.shape[1]
    down_cols = down.shape[1]
    half_down = down.shape[0] // 2
    top = rows + EXTRA

    def write(target, half):
        left, right = ((wq, wk), (wo, wv))[half]
        target[:rows, :] = jnp.concatenate([left[...], right[...]], axis=1)
        target[rows:top, :] = jnp.zeros((EXTRA, cols), BF16)
        target[rows:top, :rows] = jnp.concatenate(
            [gain_attn[...].astype(F32), gain_ffn[...].astype(F32), jnp.zeros((EXTRA - 2, rows), F32)], axis=0
        ).astype(BF16)
        for i in range(2):
            at = half * half_down + i * rows
            target[top:, i * down_cols:(i + 1) * down_cols] = down[at:at + rows, :]

    for number in range(2):

        @pl.when(place[0] == number)
        def _(number=number):
            write(own, number)
            write(rest, 1 - number)


def pack_second(place, gate, up, own, rest):
    rows, cols = gate.shape[0], own.shape[1]

    def write(target, half):
        wide = (gate, up)[half]
        target[:rows, :] = wide[:, :cols]
        target[rows:, :] = wide[:, cols:]

    for number in range(2):

        @pl.when(place[0] == number)
        def _(number=number):
            write(own, number)
            write(rest, 1 - number)


def either(condition, first, second, target, sem):
    @pl.when(condition)
    def _():
        pltpu.make_async_copy(first, target, sem).start()

    @pl.when(jnp.logical_not(condition))
    def _():
        pltpu.make_async_copy(second, target, sem).start()

    return pltpu.make_async_copy(first, target, sem)


def start(source, target, sem):
    one = pltpu.make_async_copy(source, target, sem)
    one.start()
    return one


def sides(place, layer, pieces):
    sec = place[0]
    slots = place.shape[0] - 1
    found = []
    for number, (half, rest) in enumerate(((sec, pieces[4:3 + slots]), (1 - sec, pieces[3 + slots:]))):
        found.append((half, place[1], pieces[2 * number], pieces[2 * number + 1]))
        for slot, piece in enumerate(rest):
            found.append((half, place[2 + slot], piece, None))
    return found


def load_attention(place, layer, pieces, weights, gains, sems):
    rows = (pieces[0].shape[0] - EXTRA) // 2
    home = place[0] == layer
    waits = []
    slots = place.shape[0] - 1
    for number, (half, owner, source, other) in enumerate(sides(place, layer, pieces)):
        target = weights.at[half, pl.ds(pl.multiple_of(owner * rows, 16), rows), :]
        window = slice(0, rows)
        if other is None:
            waits.append(start(source.at[window], target, sems.at[number]))
        else:
            waits.append(either(home, source.at[window], other.at[window], target, sems.at[number]))
        if number < slots and gains is not None:
            window, target, sem = slice(rows, rows + EXTRA), gains.at[owner], sems.at[2 * slots + number]
            if other is None:
                waits.append(start(source.at[window], target, sem))
            else:
                waits.append(either(home, source.at[window], other.at[window], target, sem))
    return waits


def load_gate_up(place, layer, pieces, gate_up, sems):
    rows, cols = pieces[0].shape[0] // 2, pieces[0].shape[1]
    home = place[0] == layer
    waits = []
    for number, (half, owner, source, other) in enumerate(sides(place, layer, pieces)):
        for part in range(2):
            window = slice(part * rows, (part + 1) * rows)
            target = gate_up.at[half, pl.ds(pl.multiple_of(owner * rows, 16), rows), part * cols:(part + 1) * cols]
            sem = sems.at[4 * number + part]
            if other is None:
                waits.append(start(source.at[window], target, sem))
            else:
                waits.append(either(home, source.at[window], other.at[window], target, sem))
    return waits


def load_down(place, layer, pieces, down, sems, first_sem):
    rows, narrow = (pieces[0].shape[0] - EXTRA) // 2, pieces[0].shape[1] // 2
    home = place[0] == layer
    waits = []
    for number, (half, owner, source, other) in enumerate(sides(place, layer, pieces)):
        for i in range(2):
            window = (slice(rows + EXTRA, 2 * rows + EXTRA), slice(i * narrow, (i + 1) * narrow))
            top = pl.multiple_of(half * (2 * rows) + i * rows, 16)
            target = down.at[pl.ds(top, rows), pl.ds(pl.multiple_of(owner * narrow, 128), narrow)]
            sem = sems.at[4 * number + first_sem + i]
            if other is None:
                waits.append(start(source.at[window], target, sem))
            else:
                waits.append(either(home, source.at[window], other.at[window], target, sem))
    return waits


def fill_bias(first, bias):
    count = bias.shape[0]
    key = lax.broadcasted_iota(jnp.int32, (count, count), 0)
    query = lax.broadcasted_iota(jnp.int32, (count, count), 1)
    allowed = (key >= first[...]) & (key <= query)
    bias[...] = jnp.where(allowed, 0.0, masked_score).astype(F32)


def attention_forward(place, first, cos, sin, x_t, *rest, layer, tile, count_pieces):
    pieces = rest[:count_pieces]
    mid, q_out, k_out, v_out, o_out, lse_out, gain_out, weights, gain_parts, bias, sems = rest[count_pieces:]
    owners = gain_parts.shape[0]
    rows = weights.shape[1] // owners
    waits = load_attention(place, layer, pieces, weights, gain_parts, sems)
    count = x_t.shape[1]
    values = x_t[...].T.astype(F32)
    scaled = values * inverse_root(values)
    fill_bias(first, bias)
    for one in waits:
        one.wait()
    gain = jnp.concatenate([gain_parts[f][:2, :rows].astype(F32) for f in range(owners)], axis=1)
    gain_out[...] = gain
    normed = (scaled * gain[:1]).astype(BF16)
    qk = nt(weights[0].T, normed)
    v_out[...] = nt(weights[1, :, WIDTH:].T, normed).astype(BF16)
    c, s = cos[...], sin[...]

    def turned(part):
        low, high = part[:HALF], part[HALF:]
        return jnp.concatenate([low * c - high * s, high * c + low * s], axis=0)

    for head in range(HEADS):
        span = slice(head * HEAD, (head + 1) * HEAD)
        q_out[span, :] = (turned(qk[span]) * SCALE).astype(BF16)
    for j in range(KV_HEADS):
        at = WIDTH + j * HEAD
        k_out[j * HEAD:(j + 1) * HEAD, :] = turned(qk[at:at + HEAD]).astype(BF16)
    for j in range(KV_HEADS):
        keys = k_out[j * HEAD:(j + 1) * HEAD, :].T
        vals = v_out[j * HEAD:(j + 1) * HEAD, :]
        for g in range(GROUP):
            head = j * GROUP + g
            span = slice(head * HEAD, (head + 1) * HEAD)
            for at in range(0, count, tile):
                end = at + tile
                scores = nn(keys[:end], q_out[span, at:end]) + bias[:end, at:end]
                top = jnp.max(scores, axis=0, keepdims=True)
                power = jnp.exp(scores - top)
                total = jnp.sum(power, axis=0, keepdims=True)
                mixed = nn(vals[:, :end], power.astype(BF16))
                o_out[span, at:end] = (mixed / total).astype(BF16)
                lse_out[head:head + 1, at:end] = top + jnp.log(total)
    mid[...] = values + nn(o_out[...].T, weights[1, :, :WIDTH])


def attention_backward(place, first, cos, sin, x_t, gain, d_mid, g_ffn, q, k, v, o, lse, *rest, layer, tile, count_pieces):
    pieces = rest[:count_pieces]
    dx, dx_low, keep, send, weights, grads, bias, g_out, d_q, d_k, d_v, sems, sems_out = rest[count_pieces:]
    owners = grads.shape[1]
    rows = weights.shape[1] // owners
    sec = place[0]
    waits = load_attention(place, layer, pieces, weights, None, sems)
    count = x_t.shape[1]
    g_mid = d_mid[...].astype(BF16)
    fill_bias(first, bias)
    for one in waits:
        one.wait()
    g_out[...] = nt(weights[1, :, :WIDTH], g_mid).astype(BF16)

    def store(side, columns, value):
        for owner in range(owners):
            grads[side, owner, :rows, columns] = value[owner * rows:(owner + 1) * rows].astype(BF16)

    store(1, slice(0, WIDTH), nn(o[...], g_mid))
    c, s = cos[...], sin[...]

    def turned_back(part):
        low, high = part[:HALF], part[HALF:]
        return jnp.concatenate([low * c + high * s, high * c - low * s], axis=0)

    for j in range(KV_HEADS):
        own = slice(j * HEAD, (j + 1) * HEAD)
        keys_t = k[own, :]
        keys = keys_t.T
        vals = v[own, :].T
        k_sum = [jnp.zeros((HEAD, tile), F32) for _ in range(count // tile)]
        v_sum = [jnp.zeros((HEAD, tile), F32) for _ in range(count // tile)]
        for g in range(GROUP):
            head = j * GROUP + g
            span = slice(head * HEAD, (head + 1) * HEAD)
            for at in range(0, count, tile):
                end = at + tile
                q_part = q[span, at:end]
                g_part = g_out[span, at:end]
                power = jnp.exp(nn(keys[:end], q_part) + bias[:end, at:end] - lse[head:head + 1, at:end])
                d_prob = nn(vals[:end], g_part)
                delta = jnp.sum(power * d_prob, axis=0, keepdims=True)
                d_score = (power * (d_prob - delta)).astype(BF16)
                power = power.astype(BF16)
                v_add = nt(g_part, power)
                k_add = nt(q_part, d_score)
                for i in range(end // tile):
                    v_sum[i] = v_sum[i] + v_add[:, i * tile:(i + 1) * tile]
                    k_sum[i] = k_sum[i] + k_add[:, i * tile:(i + 1) * tile]
                d_q[span, at:end] = nn(keys_t[:, :end], d_score) * SCALE
        d_k[own, :] = jnp.concatenate(k_sum, axis=1)
        d_v[own, :] = jnp.concatenate(v_sum, axis=1).astype(BF16)
    turned = [turned_back(d_q[h * HEAD:(h + 1) * HEAD, :]).astype(BF16) for h in range(HEADS)]
    turned += [turned_back(d_k[h * HEAD:(h + 1) * HEAD, :]).astype(BF16) for h in range(KV_HEADS)]
    d_qk = jnp.concatenate(turned, axis=0)
    values = x_t[...].T.astype(F32)
    inv = inverse_root(values)
    attn_gain = gain[:1, :]
    normed_t = (values * inv * attn_gain).astype(BF16).T
    store(0, slice(None), nt(normed_t, d_qk))
    store(1, slice(WIDTH, None), nt(normed_t, d_v[...]))
    d_normed = (nn(weights[0], d_qk) + nn(weights[1, :, WIDTH:], d_v[...])).T
    back, gain_grad = norm_back(values, inv, attn_gain, d_normed)
    for owner in range(owners):
        span = slice(owner * rows, (owner + 1) * rows)
        both = jnp.concatenate([gain_grad[:, span], g_ffn[:, span]], axis=0)
        grads[:, owner, rows:, :] = jnp.zeros((2, EXTRA, grads.shape[3]), BF16)
        padded = jnp.concatenate([both, jnp.zeros((EXTRA - 2, rows), F32)], axis=0)
        grads[0, owner, rows:, :rows] = padded.astype(BF16)
    out = [start(grads.at[1 - sec], send, sems_out.at[0]), start(grads.at[sec], keep, sems_out.at[1])]
    total = (d_mid[...] + back).T
    dx[...] = total
    dx_low[...] = total.astype(BF16)
    for one in out:
        one.wait()


def attention_scores_backward(place, first, cos, sin, d_mid, q, k, v, lse, *rest, layer, tile, count_pieces):
    pieces = rest[:count_pieces]
    d_qk, d_v, weights, bias, g_out, d_q, d_k, sems = rest[count_pieces:]
    waits = load_attention(place, layer, pieces, weights, None, sems)
    count = d_mid.shape[0]
    g_mid = d_mid[...].astype(BF16)
    fill_bias(first, bias)
    for one in waits:
        one.wait()
    g_out[...] = nt(weights[1, :, :WIDTH], g_mid).astype(BF16)
    c, s = cos[...], sin[...]

    def turned_back(part):
        low, high = part[:HALF], part[HALF:]
        return jnp.concatenate([low * c + high * s, high * c - low * s], axis=0)

    for j in range(KV_HEADS):
        own = slice(j * HEAD, (j + 1) * HEAD)
        keys_t = k[own, :]
        keys = keys_t.T
        vals = v[own, :].T
        k_sum = [jnp.zeros((HEAD, tile), F32) for _ in range(count // tile)]
        v_sum = [jnp.zeros((HEAD, tile), F32) for _ in range(count // tile)]
        for g in range(GROUP):
            head = j * GROUP + g
            span = slice(head * HEAD, (head + 1) * HEAD)
            for at in range(0, count, tile):
                end = at + tile
                q_part = q[span, at:end]
                g_part = g_out[span, at:end]
                power = jnp.exp(nn(keys[:end], q_part) + bias[:end, at:end] - lse[head:head + 1, at:end])
                d_prob = nn(vals[:end], g_part)
                delta = jnp.sum(power * d_prob, axis=0, keepdims=True)
                d_score = (power * (d_prob - delta)).astype(BF16)
                power = power.astype(BF16)
                v_add = nt(g_part, power)
                k_add = nt(q_part, d_score)
                for i in range(end // tile):
                    v_sum[i] = v_sum[i] + v_add[:, i * tile:(i + 1) * tile]
                    k_sum[i] = k_sum[i] + k_add[:, i * tile:(i + 1) * tile]
                d_q[span, at:end] = nn(keys_t[:, :end], d_score) * SCALE
        d_k[own, :] = jnp.concatenate(k_sum, axis=1)
        d_v[own, :] = jnp.concatenate(v_sum, axis=1).astype(BF16)
    for h in range(HEADS):
        d_qk[h * HEAD:(h + 1) * HEAD, :] = turned_back(d_q[h * HEAD:(h + 1) * HEAD, :]).astype(BF16)
    for h in range(KV_HEADS):
        d_qk[WIDTH + h * HEAD:WIDTH + (h + 1) * HEAD, :] = turned_back(d_k[h * HEAD:(h + 1) * HEAD, :]).astype(BF16)


def attention_weights_backward(place, x_t, gain, d_mid, g_ffn, o, d_qk, d_v, *rest, layer, count_pieces):
    pieces = rest[:count_pieces]
    dx, dx_low, keep, send, weights, grads, sems, sems_out = rest[count_pieces:]
    owners = grads.shape[1]
    rows = weights.shape[1] // owners
    sec = place[0]
    waits = load_attention(place, layer, pieces, weights, None, sems)

    def store(side, columns, value):
        for owner in range(owners):
            grads[side, owner, :rows, columns] = value[owner * rows:(owner + 1) * rows].astype(BF16)

    store(1, slice(0, WIDTH), nn(o[...], d_mid[...].astype(BF16)))
    values = x_t[...].T.astype(F32)
    inv = inverse_root(values)
    attn_gain = gain[:1, :]
    normed_t = (values * inv * attn_gain).astype(BF16).T
    store(0, slice(None), nt(normed_t, d_qk[...]))
    store(1, slice(WIDTH, None), nt(normed_t, d_v[...]))
    for one in waits:
        one.wait()
    d_normed = (nn(weights[0], d_qk[...]) + nn(weights[1, :, WIDTH:], d_v[...])).T
    back, gain_grad = norm_back(values, inv, attn_gain, d_normed)
    for owner in range(owners):
        span = slice(owner * rows, (owner + 1) * rows)
        both = jnp.concatenate([gain_grad[:, span], g_ffn[:, span]], axis=0)
        grads[:, owner, rows:, :] = jnp.zeros((2, EXTRA, grads.shape[3]), BF16)
        padded = jnp.concatenate([both, jnp.zeros((EXTRA - 2, rows), F32)], axis=0)
        grads[0, owner, rows:, :rows] = padded.astype(BF16)
    out = [start(grads.at[1 - sec], send, sems_out.at[0]), start(grads.at[sec], keep, sems_out.at[1])]
    total = (d_mid[...] + back).T
    dx[...] = total
    dx_low[...] = total.astype(BF16)
    for one in out:
        one.wait()


def feed_forward(place, mid, gain, *rest, layer, forward, backward, block, count_pieces):
    pieces = rest[:count_pieces]
    rest = list(rest[count_pieces:])
    take = lambda: rest.pop(0)
    dy_t = take() if backward else None
    kept = (take(), take()) if backward and not forward else None
    y_t = take() if forward and not backward else None
    hidden_out = take() if forward and backward else None
    keeping = (take(), take()) if forward and not backward else None
    if backward:
        d_mid, d_gain, keep, send = take(), take(), take(), take()
    gate_up, down, sems = take(), take(), take()
    middle = take()
    if backward:
        grads, sems_out, gate_back, up_back = take(), take(), take(), take()
    sec = place[0]
    first_count = len(pieces) // 2
    if kept is None:
        early = load_gate_up(place, layer, pieces[first_count:], gate_up, sems)
        late = load_down(place, layer, pieces[:first_count], down, sems, 2)
    else:
        late = load_down(place, layer, pieces[:first_count], down, sems, 2)
        kept_here, kept_sems = take(), take()
        kept_waits = []
        for number, at in enumerate(range(0, down.shape[1], block)):
            for i in range(2):
                span = slice(at, at + block)
                kept_waits.append(start(kept[i].at[:, span], kept_here.at[i, :, span], kept_sems.at[2 * number + i]))
        early = load_gate_up(place, layer, pieces[first_count:], gate_up, sems)
    values = mid[...]
    inv = inverse_root(values)
    ffn_gain = gain[1:, :]
    normed = (values * inv * ffn_gain).astype(BF16)
    if backward:
        normed_t = normed.T
        dy = dy_t[...].T
        rows = grads.shape[2] // 3
        owners = grads.shape[1]
    for one in early if kept is None else late:
        one.wait()
    units = down.shape[1]
    result, d_normed = None, None
    out = []
    for number, at in enumerate(range(0, units, block)):
        span = slice(at, at + block)
        if kept is None:
            gate, up = nn(normed, gate_up[0, :, span]), nn(normed, gate_up[1, :, span])
        else:
            for one in kept_waits[2 * number:2 * number + 2]:
                one.wait()
            gate, up = kept_here[0, :, span], kept_here[1, :, span]
        if keeping is not None:
            keeping[0][:, span] = gate.astype(BF16)
            keeping[1][:, span] = up.astype(BF16)
        if number == 0 and kept is None:
            for one in late:
                one.wait()
        if backward:
            d_hidden = nn(dy, down[:, span])
        for at_column in range(0, block, 128):
            strip = slice(at_column, at_column + 128)
            g, u = gate[:, strip].astype(F32), up[:, strip].astype(F32)
            sg = sigmoid(g)
            swish = g * sg
            if hidden_out is None:
                middle[:, strip] = (swish * u).astype(BF16)
            else:
                hidden_out[:, at + at_column:at + at_column + 128] = (swish * u).astype(BF16)
            if backward:
                d = d_hidden[:, strip]
                gate_back[:, strip] = (d * u * (sg * (1.0 + g * (1.0 - sg)))).astype(BF16)
                up_back[:, strip] = (d * swish).astype(BF16)
        hidden = middle[...] if hidden_out is None else hidden_out[:, span]
        if y_t is not None:
            part = nt(hidden, down[:, span])
            result = part if result is None else result + part
        if backward:
            g_gate, g_up = gate_back[...], up_back[...]
            for half, grad in ((0, g_gate), (1, g_up)):
                value = nn(normed_t, grad).astype(BF16)
                for owner in range(owners):
                    grads[half, owner, number * rows:(number + 1) * rows, :] = value[owner * rows:(owner + 1) * rows]
            value = nn(dy_t[...], hidden).astype(BF16)
            narrow = block // 2
            for i in range(2):
                for half in range(2):
                    for k in range(2):
                        top = (2 * half + k) * rows
                        grads[half, 2 * number + i, 2 * rows:, k * narrow:(k + 1) * narrow] = value[
                            top:top + rows, i * narrow:(i + 1) * narrow
                        ]
            for side, target in ((1 - sec, send), (sec, keep)):
                for window in (
                    (slice(None), slice(number * rows, (number + 1) * rows)),
                    (slice(2 * number, 2 * number + 2), slice(2 * rows, 3 * rows)),
                ):
                    out.append(start(grads.at[(side,) + window], target.at[window], sems_out.at[len(out)]))
            if number == 0 and kept is not None:
                for one in early:
                    one.wait()
            part = nt(g_gate, gate_up[0, :, span]) + nt(g_up, gate_up[1, :, span])
            d_normed = part if d_normed is None else d_normed + part
    if y_t is not None:
        y_t[...] = (values + result).astype(BF16).T
    if backward:
        back, gain_grad = norm_back(values, inv, ffn_gain, d_normed)
        d_gain[...] = gain_grad
        d_mid[...] = dy.astype(F32) + back
        for one in out:
            one.wait()


def feed_forward_result(place, mid, hidden, *rest, layer, count_pieces):
    pieces = rest[:count_pieces]
    y_t, down, sems = rest[count_pieces:]
    waits = load_down(place, layer, pieces, down, sems, 0)
    for one in waits:
        one.wait()
    y_t[...] = (mid[...] + nt(hidden[...], down[...])).astype(BF16).T


VM = pl.BlockSpec(memory_space=pltpu.VMEM)
SM = pl.BlockSpec(memory_space=pltpu.SMEM)
AN = pl.BlockSpec(memory_space=pl.ANY)


def params(mib):
    return pltpu.CompilerParams(vmem_limit_bytes=mib * 1024 * 1024)


def shape(dims, kind):
    return jax.ShapeDtypeStruct(dims, kind)


def cost(gigaflops):
    return pl.CostEstimate(flops=int(gigaflops * 10**6), bytes_accessed=10**4, transcendentals=0)


def run_pack(kernel, name, place, dims, *arrays):
    return pl.pallas_call(
        kernel,
        out_shape=(shape(dims, BF16),) * 2,
        in_specs=[SM] + [VM] * len(arrays),
        out_specs=(VM,) * 2,
        compiler_params=params(56),
        name=name,
    )(place, *arrays)


def run_attention_forward(layer, place, tables, x_t, pieces, tile=256):
    first, cos, sin = tables
    wide, count = x_t.shape
    cols = pieces[0].shape[1]
    owners = place.shape[0] - 1
    return pl.pallas_call(
        functools.partial(attention_forward, layer=layer, tile=tile, count_pieces=len(pieces)),
        out_shape=(
            shape((count, wide), F32),
            shape((WIDTH, count), BF16),
            shape((KVW, count), BF16),
            shape((KVW, count), BF16),
            shape((WIDTH, count), BF16),
            shape((HEADS, count), F32),
            shape((2, wide), F32),
        ),
        in_specs=[SM] + [VM] * 4 + [AN] * len(pieces),
        out_specs=(VM,) * 7,
        scratch_shapes=[
            pltpu.VMEM((2, wide, cols), BF16),
            pltpu.VMEM((owners, EXTRA, cols), BF16),
            pltpu.VMEM((count, count), F32),
            pltpu.SemaphoreType.DMA((3 * owners,)),
        ],
        compiler_params=params(56),
        cost_estimate=cost(6),
        name="attention_forward",
    )(place, first, cos, sin, x_t, *pieces)


def run_attention_backward(layer, place, tables, x_t, gain, d_mid, g_ffn, saved, pieces, tile=256):
    first, cos, sin = tables
    wide, count = x_t.shape
    cols = pieces[0].shape[1]
    owners = place.shape[0] - 1
    padded = wide // owners + EXTRA
    return pl.pallas_call(
        functools.partial(attention_backward, layer=layer, tile=tile, count_pieces=len(pieces)),
        out_shape=(
            shape((wide, count), F32),
            shape((wide, count), BF16),
            shape((owners, padded, cols), BF16),
            shape((owners, padded, cols), BF16),
        ),
        in_specs=[SM] + [VM] * 12 + [AN] * len(pieces),
        out_specs=(VM, VM, AN, AN),
        scratch_shapes=[
            pltpu.VMEM((2, wide, cols), BF16),
            pltpu.VMEM((2, owners, padded, cols), BF16),
            pltpu.VMEM((count, count), F32),
            pltpu.VMEM((WIDTH, count), BF16),
            pltpu.VMEM((WIDTH, count), F32),
            pltpu.VMEM((KVW, count), F32),
            pltpu.VMEM((KVW, count), BF16),
            pltpu.SemaphoreType.DMA((2 * owners,)),
            pltpu.SemaphoreType.DMA((2,)),
        ],
        compiler_params=params(56),
        cost_estimate=cost(10),
        name="attention_backward",
    )(place, first, cos, sin, x_t, gain, d_mid, g_ffn, *saved, *pieces)


def run_attention_scores_backward(layer, place, tables, d_mid, saved, pieces, tile=256):
    first, cos, sin = tables
    count, wide = d_mid.shape
    cols = pieces[0].shape[1]
    owners = place.shape[0] - 1
    q, k, v, o, lse = saved
    return pl.pallas_call(
        functools.partial(attention_scores_backward, layer=layer, tile=tile, count_pieces=len(pieces)),
        out_shape=(shape((WIDTH + KVW, count), BF16), shape((KVW, count), BF16)),
        in_specs=[SM] + [VM] * 8 + [AN] * len(pieces),
        out_specs=(VM, VM),
        scratch_shapes=[
            pltpu.VMEM((2, wide, cols), BF16),
            pltpu.VMEM((count, count), F32),
            pltpu.VMEM((WIDTH, count), BF16),
            pltpu.VMEM((WIDTH, count), F32),
            pltpu.VMEM((KVW, count), F32),
            pltpu.SemaphoreType.DMA((2 * owners,)),
        ],
        compiler_params=params(56),
        cost_estimate=cost(7),
        name="attention_scores_backward",
    )(place, first, cos, sin, d_mid, q, k, v, lse, *pieces)


def run_attention_weights_backward(layer, place, x_t, gain, d_mid, g_ffn, saved, d_qk, d_v, pieces):
    wide, count = x_t.shape
    cols = pieces[0].shape[1]
    owners = place.shape[0] - 1
    padded = wide // owners + EXTRA
    return pl.pallas_call(
        functools.partial(attention_weights_backward, layer=layer, count_pieces=len(pieces)),
        out_shape=(
            shape((wide, count), F32),
            shape((wide, count), BF16),
            shape((owners, padded, cols), BF16),
            shape((owners, padded, cols), BF16),
        ),
        in_specs=[SM] + [VM] * 7 + [AN] * len(pieces),
        out_specs=(VM, VM, AN, AN),
        scratch_shapes=[
            pltpu.VMEM((2, wide, cols), BF16),
            pltpu.VMEM((2, owners, padded, cols), BF16),
            pltpu.SemaphoreType.DMA((2 * owners,)),
            pltpu.SemaphoreType.DMA((2,)),
        ],
        compiler_params=params(56),
        cost_estimate=cost(3),
        name="attention_weights_backward",
    )(place, x_t, gain, d_mid, g_ffn, saved[3], d_qk, d_v, *pieces)


def run_feed_forward(layer, place, mid, gain, pieces, dy_t=None, kept=(), block=768):
    backward = dy_t is not None
    forward = not kept
    count, wide = mid.shape
    owners = place.shape[0] - 1
    rows, cols = (pieces[0].shape[0] - EXTRA) // 2, pieces[0].shape[1]
    out_shape, out_specs = [], []
    scratch = [
        pltpu.VMEM((2, wide, 2 * cols), BF16),
        pltpu.VMEM((wide, 2 * cols), BF16),
        pltpu.SemaphoreType.DMA((8 * owners,)),
    ]
    if forward and backward:
        out_shape.append(shape((count, 2 * cols), BF16))
        out_specs.append(VM)
    elif forward:
        out_shape += [shape((wide, count), BF16)] + [shape((count, 2 * cols), BF16)] * 2
        out_specs += [VM] * 3
    scratch.append(pltpu.VMEM((count, block), BF16))
    if backward:
        out_shape += [
            shape((count, wide), F32),
            shape((1, wide), F32),
            shape((owners, 3 * rows, cols), BF16),
            shape((owners, 3 * rows, cols), BF16),
        ]
        out_specs += [VM, VM, AN, AN]
        scratch += [
            pltpu.VMEM((2, owners, 3 * rows, cols), BF16),
            pltpu.SemaphoreType.DMA((8,)),
            pltpu.VMEM((count, block), BF16),
            pltpu.VMEM((count, block), BF16),
        ]
    if kept:
        scratch += [pltpu.VMEM((2, count, 2 * cols), BF16), pltpu.SemaphoreType.DMA((4 * cols // block,))]
    flops = (7 if forward else 0) + (14 if backward else 0)
    extra = ([dy_t] if backward else []) + list(kept)
    return pl.pallas_call(
        functools.partial(
            feed_forward, layer=layer, forward=forward, backward=backward, block=block, count_pieces=len(pieces)
        ),
        out_shape=tuple(out_shape),
        in_specs=[SM, VM, VM] + [AN] * len(pieces) + [VM] * (len(extra) - len(kept)) + [AN] * len(kept),
        out_specs=tuple(out_specs),
        scratch_shapes=scratch,
        compiler_params=params(56),
        cost_estimate=cost(flops),
        name="feed_forward",
    )(place, mid, gain, *pieces, *extra)


def run_feed_forward_result(layer, place, mid, hidden, pieces):
    count, wide = mid.shape
    owners = place.shape[0] - 1
    return pl.pallas_call(
        functools.partial(feed_forward_result, layer=layer, count_pieces=len(pieces)),
        out_shape=shape((wide, count), BF16),
        in_specs=[SM, VM, VM] + [AN] * len(pieces),
        out_specs=VM,
        scratch_shapes=[pltpu.VMEM((wide, hidden.shape[1]), BF16), pltpu.SemaphoreType.DMA((8 * owners,))],
        compiler_params=params(24),
        cost_estimate=cost(2),
        name="feed_forward_result",
    )(place, mid, hidden, *pieces)


def make_tables(lengths, count):
    ends = jnp.cumsum(lengths)
    starts = ends - lengths
    places = jnp.arange(count, dtype=jnp.int32)
    document = jnp.sum((places[:, None] >= ends[None, :]).astype(jnp.int32), axis=1)
    inside = document[:, None] == jnp.arange(lengths.shape[0], dtype=jnp.int32)[None, :]
    first = jnp.sum(jnp.where(inside, starts[None, :], 0), axis=1)
    position = (places - first).astype(F32)
    frequency = rope_base ** (-(jnp.arange(HALF, dtype=F32) * 2.0 / HEAD))
    angles = frequency[:, None] * position[None, :]
    return first[None, :], jnp.cos(angles), jnp.sin(angles)


def swap(value):
    return lax.ppermute(value, "section", [(0, 1), (1, 0)])


def give(value, target):
    return lax.ppermute(value, "section", [(1 - target, target)])


def exchange(value, axis, bit):
    count = lax.axis_size(axis)
    return lax.ppermute(value, axis, [(i, i ^ bit) for i in range(count)])


def mixed_exchange(value, even_bit, odd_bit):
    owners, replicas = lax.axis_size("fsdp"), lax.axis_size("dp")
    pairs = []
    for i in range(owners):
        for z in range(replicas):
            partner = i ^ (odd_bit if z % 2 else even_bit)
            pairs.append((i * replicas + z, partner * replicas + z))
    return lax.ppermute(value, ("fsdp", "dp"), pairs)


def paired():
    return lax.axis_size("fsdp") == 4 and lax.axis_size("dp") % 2 == 0


def piece_places():
    own = lax.axis_index("fsdp")
    if not paired():
        count = lax.axis_size("fsdp")
        return [own] + [(own + i) % count for i in range(1, count)]
    odd = lax.axis_index("dp") % 2
    near, far = jnp.where(odd == 1, own ^ 2, own ^ 1), jnp.where(odd == 1, own ^ 1, own ^ 2)
    return [own, near, own ^ 3, far]


def first_hop(value):
    if not paired():
        return lax.all_gather(value, "fsdp")
    return mixed_exchange(value, 1, 2)


def second_hop(near):
    if not paired():
        count = lax.axis_size("fsdp")
        own = lax.axis_index("fsdp")
        return [pick(near, (own + i) % count, 0) for i in range(1, count)]
    return [near, mixed_exchange(near, 2, 1), exchange(near, "dp", 1)]


def shared(pieces):
    return pieces + [swap(piece) for piece in pieces]


def tie(*values):
    return lax.optimization_barrier(values)


def pick(value, index, axis):
    return lax.dynamic_index_in_dim(value, index, axis, keepdims=False)


def total(left, right):
    return (left.astype(F32) + right.astype(F32)).astype(BF16)


def split_first(place, ins, outs, cut):
    (keep, came), outs = ins, list(outs)
    y, x = place[1] // 2, place[1] % 2
    for by_x, low, high in ((True, 0, cut), (False, cut, keep.shape[1])):
        if low == high:
            continue
        hold, away = outs.pop(0), outs.pop(0)
        for i in range(2):
            for target, mine in ((hold, True), (away, False)):
                bit_x, bit_y = (x, y) if mine else (1 - x, 1 - y)
                block = 2 * i + bit_x if by_x else 2 * bit_y + i
                target[i] = total(keep[block, low:high], came[block, low:high])


def split_second(place, ins, outs, order):
    y, x = place[1] // 2, place[1] % 2
    for i, by_x in enumerate(order):
        hold, came, stay, away = ins[2 * i], ins[2 * i + 1], outs[2 * i], outs[2 * i + 1]
        bit = y if by_x else x
        stay[...] = total(hold[bit], came[bit])
        away[...] = total(hold[1 - bit], came[1 - bit])


def stack_sums(place, ins, outs):
    at = 0
    for i in range(0, len(ins), 2):
        rows = ins[i].shape[0]
        outs[0][at:at + rows, :] = total(ins[i][...], ins[i + 1][...])
        at += rows


def from_middle(place, ins, outs):
    z = place[place.shape[0] - 1]
    inner = (z == 1) | (z == 2)

    @pl.when(inner)
    def _():
        outs[0][...] = ins[0][...]

    @pl.when(jnp.logical_not(inner))
    def _():
        outs[0][...] = ins[1][...]


def work(place, *refs, steps):
    ins, outs = [], list(refs)
    for _, count_in, _ in steps:
        ins.append(outs[:count_in])
        outs = outs[count_in:]
    for (body, _, count_out), taken in zip(steps, ins):
        body(place, taken, outs[:count_out])
        outs = outs[count_out:]


def run_work(place, jobs, mib=24):
    ins = [value for job in jobs for value in job[1]]
    out = [shape(dims, BF16) for job in jobs for dims in job[2]]
    done = list(pl.pallas_call(
        functools.partial(work, steps=tuple((job[0], len(job[1]), len(job[2])) for job in jobs)),
        out_shape=tuple(out),
        in_specs=[SM] + [VM] * len(ins),
        out_specs=(VM,) * len(out),
        compiler_params=params(mib),
        name="work",
    )(place, *ins))
    for job in jobs:
        job[3](done[:len(job[2])])
        done = done[len(job[2]):]


class Sum:
    def __init__(self, keep, send, cut, pairs=False):
        self.hold, self.cut, self.pairs = [keep], cut, pairs
        self.chain = lax.axis_size("dp") == 4
        self.came = [swap(send)]
        rows = keep.shape[1]
        self.order = [by_x for by_x, some in ((True, cut > 0), (False, cut < rows)) if some]

    def split(self, second):
        def then(outs):
            self.hold = list(outs[::2])
            self.came = [
                exchange(value, "fsdp", 1 if by_x != second else 2) for value, by_x in zip(outs[1::2], self.order)
            ]
        return then

    def fsdp_first(self):
        _, rows, cols = self.hold[0].shape
        dims = [(2, self.cut if by_x else rows - self.cut, cols) for by_x in self.order for _ in range(2)]
        return functools.partial(split_first, cut=self.cut), self.hold + self.came, dims, self.split(False)

    def fsdp_second(self):
        ins = [value for pair in zip(self.hold, self.came) for value in pair]
        dims = [value.shape[1:] for value in self.hold for _ in range(2)]
        return functools.partial(split_second, order=tuple(self.order)), ins, dims, self.split(True)

    def dp(self, hop):
        ins = [value for pair in zip(self.hold, self.came) for value in pair]
        dims = [(sum(value.shape[0] for value in self.hold), self.hold[0].shape[1])]

        def then(outs):
            value = outs[0]
            self.hold = [value]
            if not self.chain:
                self.came = [lax.psum(value, "dp") if hop == 0 else jnp.zeros_like(value)]
                if hop == 0:
                    self.hold = [jnp.zeros_like(value)]
            elif self.pairs:
                self.came = [exchange(value, "dp", 1 + hop)] if hop < 2 else []
            else:
                pairs = ([(0, 1), (3, 2)], [(1, 2), (2, 1)], [(1, 0), (2, 3)])[hop]
                self.came = [lax.ppermute(value, "dp", pairs)]

        return stack_sums, ins, dims, then

    def finish(self):
        def then(outs):
            self.hold, self.came = list(outs), []

        if not self.chain or self.pairs:
            return self.dp(2)[:3] + (then,)
        return from_middle, self.hold + self.came, [self.hold[0].shape], then


def choose(place, ff1, ff0, at1, at0, ff_own, ff_send, at_own, at_send):
    for sec, ff, ff_rest, at, at_rest in ((0, ff0, ff1, at0, at1), (1, ff1, ff0, at1, at0)):

        @pl.when(place[0] == sec)
        def _(ff=ff, ff_rest=ff_rest, at=at, at_rest=at_rest):
            ff_own[...] = ff[...]
            ff_send[...] = ff_rest[...]
            at_own[...] = at[...]
            at_send[...] = at_rest[...]


def run_choose(place, ff1, ff0, at1, at0):
    return pl.pallas_call(
        choose,
        out_shape=(shape(ff0.shape, BF16),) * 2 + (shape(at0.shape, BF16),) * 2,
        in_specs=[SM] + [VM] * 4,
        out_specs=(VM,) * 4,
        compiler_params=params(16),
        name="choose",
    )(place, ff1, ff0, at1, at0)


def unpack(place, ff_own, ff_given, at_own, at_given, gate, up, down, wq, wk, wv, wo, gains):
    rows = gate.shape[0]
    narrow = down.shape[1]

    def emit(half, part, value):
        wide = (gate, up)[half]
        for i in range(2):
            wide[:, 2 * i * narrow:(2 * i + 2) * narrow] = part[i * rows:(i + 1) * rows, :].astype(F32)
        top = 2 * half * rows
        down[top:top + rows, :] = part[2 * rows:, :narrow].astype(F32)
        down[top + rows:top + 2 * rows, :] = part[2 * rows:, narrow:].astype(F32)
        left, right = ((wq, wk), (wo, wv))[half]
        left[...] = value[:rows, :WIDTH].astype(F32)
        right[...] = value[:rows, WIDTH:].astype(F32)
        if half == 0:
            gains[...] = value[rows:, :rows].astype(F32)[:2]

    for sec in range(2):

        @pl.when(place[0] == sec)
        def _(sec=sec):
            emit(sec, ff_own, at_own)
            emit(1 - sec, ff_given, at_given)


def run_unpack(place, ff_own, ff_given, at_own, at_given):
    rows, cols = ff_own.shape[0] // 3, ff_own.shape[1]
    return pl.pallas_call(
        unpack,
        out_shape=(
            shape((rows, 2 * cols), F32),
            shape((rows, 2 * cols), F32),
            shape((4 * rows, cols // 2), F32),
            shape((rows, WIDTH), F32),
            shape((rows, KVW), F32),
            shape((rows, KVW), F32),
            shape((rows, WIDTH), F32),
            shape((2, rows), F32),
        ),
        in_specs=[SM] + [VM] * 4,
        out_specs=(VM,) * 8,
        compiler_params=params(32),
        name="unpack",
    )(place, ff_own, ff_given, at_own, at_given)


def local(
    tokens,
    cotangent,
    doc_lengths,
    w_query,
    w_key,
    w_value,
    w_out,
    w_gate,
    w_up,
    w_down,
    gain_attn,
    gain_ffn,
):
    sec = lax.axis_index("section")
    first_section = sec == 0
    count = tokens.shape[2]
    place = jnp.stack([jnp.asarray(i, jnp.int32) for i in [sec] + piece_places()])
    line = jnp.concatenate([place, lax.axis_index("dp").astype(jnp.int32)[None]])
    rows, cols = w_query.shape[1], w_query.shape[2] + w_key.shape[2]
    own_at, rest_at = run_pack(
        pack_first, "pack_first", place, (2 * rows + EXTRA, cols),
        w_query[0], w_key[0], w_value[0], w_out[0], gain_attn, gain_ffn, w_down[0].T,
    )
    later, own_at, rest_at = tie(place, own_at, rest_at)
    own_ff, rest_ff = run_pack(pack_second, "pack_second", later, (2 * rows, cols), w_gate[0], w_up[0])

    def own_pieces(own, rest):
        came_own, came_rest = swap(rest), swap(own)
        home = [own, came_own, rest, came_rest]
        return home, jnp.where(first_section, own, came_own), jnp.where(first_section, came_own, own)

    at_home, at_zero, at_one = own_pieces(own_at, rest_at)
    ff_home, ff_zero, ff_one = own_pieces(own_ff, rest_ff)
    tables = make_tables(pick(doc_lengths[0], sec, 0), count)
    x0 = jnp.swapaxes(pick(tokens[0], sec, 0), 0, 1)
    dy1 = jnp.swapaxes(pick(cotangent[0], sec, 0), 0, 1)

    near_at0 = first_hop(at_zero)
    near_ff0 = first_hop(ff_zero)
    near_at0, ff_one, x0, dy1, *tables = tie(near_at0, ff_one, x0, dy1, *tables)
    at0 = second_hop(near_at0)
    near_ff0, at_one, ff_one, *at0 = tie(near_ff0, at_one, ff_one, *at0)
    ff0 = second_hop(near_ff0)
    near_at1 = first_hop(at_one)
    near_ff1 = first_hop(ff_one)
    at0 = shared(at0)
    mid0, *saved0, gains0 = run_attention_forward(0, place, tables, x0, at_home + at0)
    mid0, near_at1, *ff0 = tie(mid0, near_at1, *ff0)

    ff0 = shared(ff0)
    at1 = second_hop(near_at1)
    near_ff1, *ff0 = tie(near_ff1, *ff0)
    y0, gate0, up0 = run_feed_forward(0, place, mid0, gains0, at_home + at0 + ff_home + ff0)
    y0, near_ff1, *at1 = tie(y0, near_ff1, *at1)

    at1 = shared(at1)
    ff1 = second_hop(near_ff1)
    mid1, *saved1, gains1 = run_attention_forward(1, place, tables, y0, at_home + at1)
    mid1, *ff1 = tie(mid1, *ff1)
    ff1 = shared(ff1)
    hidden1, d_mid1, g_ffn1, ff_keep1, ff_send1 = run_feed_forward(
        1, place, mid1, gains1, at_home + at1 + ff_home + ff1, dy_t=dy1
    )

    sums = []

    def after(waited, *others):
        cells = [(one.came, i) for one, i in waited]
        for one in sums:
            cells += [(one.hold, i) for i in range(len(one.hold))]
        held = list(tie(*others, *[array[i] for array, i in cells]))
        for (array, i), value in zip(cells, held[len(others):]):
            array[i] = value
        return held[:len(others)]

    def both_rows(own0, own1):
        back = swap(jnp.where(first_section, own1, own0))
        both = jnp.where(first_section, jnp.stack([own0, back]), jnp.stack([back, own1]))
        return jnp.swapaxes(both, 1, 2)[None, None]

    ff_cut, at_cut = ff_keep1.shape[1] // 32 * 16, (rows + EXTRA) // 32 * 16
    f1 = Sum(ff_keep1, ff_send1, ff_cut)
    sums.append(f1)
    dx1, dy0, at_keep1, at_send1 = run_attention_backward(
        1, place, tables, y0, gains1, d_mid1, g_ffn1, saved1, at_home + at1
    )
    dy0, at_keep1, at_send1 = after([(f1, 0)], dy0, at_keep1, at_send1)

    run_work(line, [f1.fsdp_first()])
    a1 = Sum(at_keep1, at_send1, at_cut)
    sums.append(a1)
    (dy0,) = after([], dy0)
    d_mid0, g_ffn0, ff_keep0, ff_send0 = run_feed_forward(
        0, place, mid0, gains0, at_home + at0 + ff_home + ff0, dy_t=dy0, kept=(gate0, up0)
    )
    d_mid0, ff_keep0, ff_send0 = after([(f1, 0), (f1, 1), (a1, 0)], d_mid0, ff_keep0, ff_send0)

    f0 = Sum(ff_keep0, ff_send0, ff_cut)
    sums.append(f0)
    run_work(line, [f1.fsdp_second(), a1.fsdp_first()])
    (d_mid0,) = after([], d_mid0)
    d_qk0, d_v0 = run_attention_scores_backward(0, place, tables, d_mid0, saved0, at_home + at0)
    d_qk0, d_v0 = after([(f0, 0), (f1, 0), (f1, 1), (a1, 0), (a1, 1)], d_qk0, d_v0)

    run_work(line, [f0.fsdp_first(), f1.dp(0), a1.fsdp_second()], 56)
    (d_qk0,) = after([], d_qk0)
    dx0, _, at_keep0, at_send0 = run_attention_weights_backward(
        0, place, x0, gains0, d_mid0, g_ffn0, saved0, d_qk0, d_v0, at_home + at0
    )
    at_send0, at_keep0 = after([(f0, 0), (f0, 1), (f1, 0), (a1, 0), (a1, 1)], at_send0, at_keep0)

    a0 = Sum(at_keep0, at_send0, rows + EXTRA, True)
    sums.append(a0)
    run_work(line, [f0.fsdp_second(), f1.dp(1)])
    after([(a0, 0)])
    run_work(line, [a0.fsdp_first(), a1.dp(0)])
    dx0, dx1, hidden1 = after([(f0, 0), (f0, 1), (f1, 0), (a1, 0), (a0, 0)], dx0, dx1, hidden1)

    run_work(line, [f0.dp(0), f1.dp(2), a1.dp(1), a0.fsdp_second()])
    y1 = run_feed_forward_result(1, place, mid1, hidden1, at_home + at1)
    dx0, dx1, y1 = after([(f0, 0), (f1, 0), (a1, 0), (a0, 0)], dx0, dx1, y1)

    run_work(line, [f0.dp(1), a1.dp(2), a0.dp(0), f1.finish()])
    dx0, dx1 = after([], dx0, dx1)
    grad = both_rows(dx0, dx1)
    (grad,) = after([(f0, 0), (a1, 0), (a0, 0)], grad)

    run_work(line, [f0.dp(2), a0.dp(1), a1.finish()])
    y0, y1 = after([], y0, y1)
    out = both_rows(y0, y1)
    (out,) = after([(f0, 0), (a0, 0)], out)

    run_work(line, [f0.finish(), a0.finish()])
    ff_own, ff_send, at_own, at_send = run_choose(place, f1.hold[0], f0.hold[0], a1.hold[0], a0.hold[0])
    gate, up, down, wq, wk, wv, wo, gain_grads = run_unpack(place, ff_own, swap(ff_send), at_own, swap(at_send))

    return (
        out,
        grad,
        wq[None],
        wk[None],
        wv[None],
        wo[None],
        gate[None],
        up[None],
        down.T[None],
        gain_grads[:1],
        gain_grads[1:],
    )


def solution(mesh):
    whole = P(("fsdp", "dp"), None, None, None)
    weight = P("section", "fsdp", None)
    gain = P("section", "fsdp")
    rows = P("section", ("fsdp", "dp"), None, None, None)
    in_specs = (whole, whole, P(("fsdp", "dp"), None, None)) + (weight,) * 7 + (gain,) * 2
    out_specs = (rows, rows) + (weight,) * 7 + (gain,) * 2
    return jax.shard_map(local, mesh=mesh, in_specs=in_specs, out_specs=out_specs, check_vma=False)
```

```python
import functools
import jax
import jax.numpy as jnp
from jax import lax
from jax.experimental import pallas as pl
from jax.experimental.pallas import tpu as pltpu
from jax.sharding import PartitionSpec as P

HEADS = 9
KV_HEADS = 3
GROUP = HEADS // KV_HEADS
HEAD = 64
HALF = HEAD // 2
WIDTH = HEADS * HEAD
KVW = KV_HEADS * HEAD

epsilon = 1e-05
rope_base = 100000.0
masked_score = -1e30
SCALE = HEAD ** (-0.5)
EXTRA = 16
F32 = jnp.float32
BF16 = jnp.bfloat16


def nn(left, right):
    return lax.dot_general(left, right, (((1,), (0,)), ((), ())), preferred_element_type=F32)


def nt(left, right):
    return lax.dot_general(left, right, (((1,), (1,)), ((), ())), preferred_element_type=F32)


def inverse_root(values):
    return lax.rsqrt(jnp.mean(values * values, axis=-1, keepdims=True) + epsilon)


def norm_back(values, inv_root, gain, upstream):
    gain_grad = jnp.sum(upstream * values * inv_root, axis=0, keepdims=True)
    scaled = upstream * gain
    dot = jnp.mean(scaled * values, axis=-1, keepdims=True)
    return inv_root * scaled - values * (inv_root * inv_root * inv_root * dot), gain_grad


def sigmoid(values):
    return 0.5 * jnp.tanh(0.5 * values) + 0.5


def pack_first(place, wq, wk, wv, wo, gain_attn, gain_ffn, down, own, rest):
    rows, cols = wq.shape[0], own.shape[1]
    down_cols = down.shape[1]
    half_down = down.shape[0] // 2
    top = rows + EXTRA

    def write(target, half):
        left, right = ((wq, wk), (wo, wv))[half]
        target[:rows, :] = jnp.concatenate([left[...], right[...]], axis=1)
        target[rows:top, :] = jnp.zeros((EXTRA, cols), BF16)
        target[rows:top, :rows] = jnp.concatenate(
            [gain_attn[...].astype(F32), gain_ffn[...].astype(F32), jnp.zeros((EXTRA - 2, rows), F32)], axis=0
        ).astype(BF16)
        for i in range(2):
            at = half * half_down + i * rows
            target[top:, i * down_cols:(i + 1) * down_cols] = down[at:at + rows, :]

    for number in range(2):

        @pl.when(place[0] == number)
        def _(number=number):
            write(own, number)
            write(rest, 1 - number)


def pack_second(place, gate, up, own, rest):
    rows, cols = gate.shape[0], own.shape[1]

    def write(target, half):
        wide = (gate, up)[half]
        target[:rows, :] = wide[:, :cols]
        target[rows:, :] = wide[:, cols:]

    for number in range(2):

        @pl.when(place[0] == number)
        def _(number=number):
            write(own, number)
            write(rest, 1 - number)


def either(condition, first, second, target, sem):
    first, second = ((first, target), (second, target)) if target is not None else (first, second)

    @pl.when(condition)
    def _():
        pltpu.make_async_copy(*first, sem).start()

    @pl.when(jnp.logical_not(condition))
    def _():
        pltpu.make_async_copy(*second, sem).start()

    return pltpu.make_async_copy(*first, sem)


def start(source, target, sem):
    one = pltpu.make_async_copy(source, target, sem)
    one.start()
    return one


def sides(place, layer, pieces):
    sec = place[0]
    slots = place.shape[0] - 1
    found = []
    for number, (half, rest) in enumerate(((sec, pieces[4:3 + slots]), (1 - sec, pieces[3 + slots:]))):
        found.append((half, place[1], pieces[2 * number], pieces[2 * number + 1]))
        for slot, piece in enumerate(rest):
            found.append((half, place[2 + slot], piece, None))
    return found


def load_attention(place, layer, pieces, weights, gains, sems):
    rows = (pieces[0].shape[0] - EXTRA) // 2
    home = place[0] == layer
    waits = []
    slots = place.shape[0] - 1
    for number, (half, owner, source, other) in enumerate(sides(place, layer, pieces)):
        target = weights.at[half, pl.ds(pl.multiple_of(owner * rows, 16), rows), :]
        window = slice(0, rows)
        if other is None:
            waits.append(start(source.at[window], target, sems.at[number]))
        else:
            waits.append(either(home, source.at[window], other.at[window], target, sems.at[number]))
        if number < slots and gains is not None:
            window, target, sem = slice(rows, rows + EXTRA), gains.at[owner], sems.at[2 * slots + number]
            if other is None:
                waits.append(start(source.at[window], target, sem))
            else:
                waits.append(either(home, source.at[window], other.at[window], target, sem))
    return waits


def load_gate_up(place, layer, pieces, gate_up, sems):
    rows, cols = pieces[0].shape[0] // 2, pieces[0].shape[1]
    home = place[0] == layer
    waits = []
    for number, (half, owner, source, other) in enumerate(sides(place, layer, pieces)):
        for part in range(2):
            window = slice(part * rows, (part + 1) * rows)
            target = gate_up.at[half, pl.ds(pl.multiple_of(owner * rows, 16), rows), part * cols:(part + 1) * cols]
            sem = sems.at[4 * number + part]
            if other is None:
                waits.append(start(source.at[window], target, sem))
            else:
                waits.append(either(home, source.at[window], other.at[window], target, sem))
    return waits


def load_down(place, layer, pieces, down, sems, first_sem):
    rows, narrow = (pieces[0].shape[0] - EXTRA) // 2, pieces[0].shape[1] // 2
    home = place[0] == layer
    waits = []
    for number, (half, owner, source, other) in enumerate(sides(place, layer, pieces)):
        for i in range(2):
            window = (slice(rows + EXTRA, 2 * rows + EXTRA), slice(i * narrow, (i + 1) * narrow))
            top = pl.multiple_of(half * (2 * rows) + i * rows, 16)
            target = down.at[pl.ds(top, rows), pl.ds(pl.multiple_of(owner * narrow, 128), narrow)]
            sem = sems.at[4 * number + first_sem + i]
            if other is None:
                waits.append(start(source.at[window], target, sem))
            else:
                waits.append(either(home, source.at[window], other.at[window], target, sem))
    return waits


def fill_bias(first, bias):
    count = bias.shape[0]
    key = lax.broadcasted_iota(jnp.int32, (count, count), 0)
    query = lax.broadcasted_iota(jnp.int32, (count, count), 1)
    allowed = (key >= first[...]) & (key <= query)
    bias[...] = jnp.where(allowed, 0.0, masked_score).astype(F32)


def attention_forward(place, first, cos, sin, x_t, *rest, layer, tile, count_pieces):
    pieces = rest[:count_pieces]
    mid, q_out, k_out, v_out, o_out, lse_out, gain_out, weights, gain_parts, bias, sems = rest[count_pieces:]
    owners = gain_parts.shape[0]
    rows = weights.shape[1] // owners
    waits = load_attention(place, layer, pieces, weights, gain_parts, sems)
    count = x_t.shape[1]
    values = x_t[...].T.astype(F32)
    scaled = values * inverse_root(values)
    fill_bias(first, bias)
    for one in waits:
        one.wait()
    gain = jnp.concatenate([gain_parts[f][:2, :rows].astype(F32) for f in range(owners)], axis=1)
    gain_out[...] = gain
    normed = (scaled * gain[:1]).astype(BF16)
    qk = nt(weights[0].T, normed)
    v_out[...] = nt(weights[1, :, WIDTH:].T, normed).astype(BF16)
    c, s = cos[...], sin[...]

    def turned(part):
        low, high = part[:HALF], part[HALF:]
        return jnp.concatenate([low * c - high * s, high * c + low * s], axis=0)

    for head in range(HEADS):
        span = slice(head * HEAD, (head + 1) * HEAD)
        q_out[span, :] = (turned(qk[span]) * SCALE).astype(BF16)
    for j in range(KV_HEADS):
        at = WIDTH + j * HEAD
        k_out[j * HEAD:(j + 1) * HEAD, :] = turned(qk[at:at + HEAD]).astype(BF16)
    for j in range(KV_HEADS):
        keys = k_out[j * HEAD:(j + 1) * HEAD, :].T
        vals = v_out[j * HEAD:(j + 1) * HEAD, :]
        for g in range(GROUP):
            head = j * GROUP + g
            span = slice(head * HEAD, (head + 1) * HEAD)
            for at in range(0, count, tile):
                end = at + tile
                scores = nn(keys[:end], q_out[span, at:end]) + bias[:end, at:end]
                top = jnp.max(scores, axis=0, keepdims=True)
                power = jnp.exp(scores - top)
                total = jnp.sum(power, axis=0, keepdims=True)
                mixed = nn(vals[:, :end], power.astype(BF16))
                o_out[span, at:end] = (mixed / total).astype(BF16)
                lse_out[head:head + 1, at:end] = top + jnp.log(total)
    mid[...] = values + nn(o_out[...].T, weights[1, :, :WIDTH])


def attention_backward(place, first, cos, sin, x_t, gain, d_mid, g_ffn, q, k, v, o, lse, *rest, layer, tile, count_pieces):
    pieces = rest[:count_pieces]
    dx, dx_low, keep, send, weights, grads, bias, g_out, d_q, d_k, d_v, sems, sems_out = rest[count_pieces:]
    owners = grads.shape[1]
    rows = weights.shape[1] // owners
    sec = place[0]
    waits = load_attention(place, layer, pieces, weights, None, sems)
    count = x_t.shape[1]
    g_mid = d_mid[...].astype(BF16)
    fill_bias(first, bias)
    for one in waits:
        one.wait()
    g_out[...] = nt(weights[1, :, :WIDTH], g_mid).astype(BF16)

    def store(side, columns, value):
        for owner in range(owners):
            grads[side, owner, :rows, columns] = value[owner * rows:(owner + 1) * rows].astype(BF16)

    store(1, slice(0, WIDTH), nn(o[...], g_mid))
    c, s = cos[...], sin[...]

    def turned_back(part):
        low, high = part[:HALF], part[HALF:]
        return jnp.concatenate([low * c + high * s, high * c - low * s], axis=0)

    for j in range(KV_HEADS):
        own = slice(j * HEAD, (j + 1) * HEAD)
        keys_t = k[own, :]
        keys = keys_t.T
        vals = v[own, :].T
        k_sum = [jnp.zeros((HEAD, tile), F32) for _ in range(count // tile)]
        v_sum = [jnp.zeros((HEAD, tile), F32) for _ in range(count // tile)]
        for g in range(GROUP):
            head = j * GROUP + g
            span = slice(head * HEAD, (head + 1) * HEAD)
            for at in range(0, count, tile):
                end = at + tile
                q_part = q[span, at:end]
                g_part = g_out[span, at:end]
                power = jnp.exp(nn(keys[:end], q_part) + bias[:end, at:end] - lse[head:head + 1, at:end])
                d_prob = nn(vals[:end], g_part)
                delta = jnp.sum(power * d_prob, axis=0, keepdims=True)
                d_score = (power * (d_prob - delta)).astype(BF16)
                power = power.astype(BF16)
                v_add = nt(g_part, power)
                k_add = nt(q_part, d_score)
                for i in range(end // tile):
                    v_sum[i] = v_sum[i] + v_add[:, i * tile:(i + 1) * tile]
                    k_sum[i] = k_sum[i] + k_add[:, i * tile:(i + 1) * tile]
                d_q[span, at:end] = nn(keys_t[:, :end], d_score) * SCALE
        d_k[own, :] = jnp.concatenate(k_sum, axis=1)
        d_v[own, :] = jnp.concatenate(v_sum, axis=1).astype(BF16)
    turned = [turned_back(d_q[h * HEAD:(h + 1) * HEAD, :]).astype(BF16) for h in range(HEADS)]
    turned += [turned_back(d_k[h * HEAD:(h + 1) * HEAD, :]).astype(BF16) for h in range(KV_HEADS)]
    d_qk = jnp.concatenate(turned, axis=0)
    values = x_t[...].T.astype(F32)
    inv = inverse_root(values)
    attn_gain = gain[:1, :]
    normed_t = (values * inv * attn_gain).astype(BF16).T
    store(0, slice(None), nt(normed_t, d_qk))
    store(1, slice(WIDTH, None), nt(normed_t, d_v[...]))
    d_normed = (nn(weights[0], d_qk) + nn(weights[1, :, WIDTH:], d_v[...])).T
    back, gain_grad = norm_back(values, inv, attn_gain, d_normed)
    for owner in range(owners):
        span = slice(owner * rows, (owner + 1) * rows)
        both = jnp.concatenate([gain_grad[:, span], g_ffn[:, span]], axis=0)
        grads[:, owner, rows:, :] = jnp.zeros((2, EXTRA, grads.shape[3]), BF16)
        padded = jnp.concatenate([both, jnp.zeros((EXTRA - 2, rows), F32)], axis=0)
        grads[0, owner, rows:, :rows] = padded.astype(BF16)
    out = [start(grads.at[1 - sec], send, sems_out.at[0]), start(grads.at[sec], keep, sems_out.at[1])]
    total = (d_mid[...] + back).T
    dx[...] = total
    dx_low[...] = total.astype(BF16)
    for one in out:
        one.wait()


def attention_scores_backward(place, first, cos, sin, d_mid, q, k, v, lse, *rest, layer, tile, count_pieces):
    pieces = rest[:count_pieces]
    d_qk, d_v, weights, bias, g_out, d_q, d_k, sems = rest[count_pieces:]
    waits = load_attention(place, layer, pieces, weights, None, sems)
    count = d_mid.shape[0]
    g_mid = d_mid[...].astype(BF16)
    fill_bias(first, bias)
    for one in waits:
        one.wait()
    g_out[...] = nt(weights[1, :, :WIDTH], g_mid).astype(BF16)
    c, s = cos[...], sin[...]

    def turned_back(part):
        low, high = part[:HALF], part[HALF:]
        return jnp.concatenate([low * c + high * s, high * c - low * s], axis=0)

    for j in range(KV_HEADS):
        own = slice(j * HEAD, (j + 1) * HEAD)
        keys_t = k[own, :]
        keys = keys_t.T
        vals = v[own, :].T
        k_sum = [jnp.zeros((HEAD, tile), F32) for _ in range(count // tile)]
        v_sum = [jnp.zeros((HEAD, tile), F32) for _ in range(count // tile)]
        for g in range(GROUP):
            head = j * GROUP + g
            span = slice(head * HEAD, (head + 1) * HEAD)
            for at in range(0, count, tile):
                end = at + tile
                q_part = q[span, at:end]
                g_part = g_out[span, at:end]
                power = jnp.exp(nn(keys[:end], q_part) + bias[:end, at:end] - lse[head:head + 1, at:end])
                d_prob = nn(vals[:end], g_part)
                delta = jnp.sum(power * d_prob, axis=0, keepdims=True)
                d_score = (power * (d_prob - delta)).astype(BF16)
                power = power.astype(BF16)
                v_add = nt(g_part, power)
                k_add = nt(q_part, d_score)
                for i in range(end // tile):
                    v_sum[i] = v_sum[i] + v_add[:, i * tile:(i + 1) * tile]
                    k_sum[i] = k_sum[i] + k_add[:, i * tile:(i + 1) * tile]
                d_q[span, at:end] = nn(keys_t[:, :end], d_score) * SCALE
        d_k[own, :] = jnp.concatenate(k_sum, axis=1)
        d_v[own, :] = jnp.concatenate(v_sum, axis=1).astype(BF16)
    for h in range(HEADS):
        d_qk[h * HEAD:(h + 1) * HEAD, :] = turned_back(d_q[h * HEAD:(h + 1) * HEAD, :]).astype(BF16)
    for h in range(KV_HEADS):
        d_qk[WIDTH + h * HEAD:WIDTH + (h + 1) * HEAD, :] = turned_back(d_k[h * HEAD:(h + 1) * HEAD, :]).astype(BF16)


def attention_weights_backward(place, x_t, gain, d_mid, g_ffn, o, d_qk, d_v, *rest, layer, count_pieces):
    pieces = rest[:count_pieces]
    dx, dx_low, keep, send, weights, grads, sems, sems_out = rest[count_pieces:]
    owners = grads.shape[1]
    rows = weights.shape[1] // owners
    sec = place[0]
    waits = load_attention(place, layer, pieces, weights, None, sems)

    def store(side, columns, value):
        for owner in range(owners):
            grads[side, owner, :rows, columns] = value[owner * rows:(owner + 1) * rows].astype(BF16)

    store(1, slice(0, WIDTH), nn(o[...], d_mid[...].astype(BF16)))
    values = x_t[...].T.astype(F32)
    inv = inverse_root(values)
    attn_gain = gain[:1, :]
    normed_t = (values * inv * attn_gain).astype(BF16).T
    store(0, slice(None), nt(normed_t, d_qk[...]))
    store(1, slice(WIDTH, None), nt(normed_t, d_v[...]))
    for one in waits:
        one.wait()
    d_normed = (nn(weights[0], d_qk[...]) + nn(weights[1, :, WIDTH:], d_v[...])).T
    back, gain_grad = norm_back(values, inv, attn_gain, d_normed)
    for owner in range(owners):
        span = slice(owner * rows, (owner + 1) * rows)
        both = jnp.concatenate([gain_grad[:, span], g_ffn[:, span]], axis=0)
        grads[:, owner, rows:, :] = jnp.zeros((2, EXTRA, grads.shape[3]), BF16)
        padded = jnp.concatenate([both, jnp.zeros((EXTRA - 2, rows), F32)], axis=0)
        grads[0, owner, rows:, :rows] = padded.astype(BF16)
    out = [start(grads.at[1 - sec], send, sems_out.at[0]), start(grads.at[sec], keep, sems_out.at[1])]
    total = (d_mid[...] + back).T
    dx[...] = total
    dx_low[...] = total.astype(BF16)
    for one in out:
        one.wait()


def feed_forward(place, mid, gain, *rest, layer, forward, backward, block, count_pieces):
    pieces = rest[:count_pieces]
    rest = list(rest[count_pieces:])
    take = lambda: rest.pop(0)
    dy_t = take() if backward else None
    kept = (take(), take()) if backward and not forward else None
    y_t = take() if forward and not backward else None
    hidden_out = take() if forward and backward else None
    keeping = (take(), take()) if forward and not backward else None
    if backward:
        d_mid, d_gain, keep, send = take(), take(), take(), take()
    gate_up, down, sems = take(), take(), take()
    middle = take()
    if backward:
        grads, sems_out, gate_back, up_back = take(), take(), take(), take()
    sec = place[0]
    first_count = len(pieces) // 2
    if kept is None:
        early = load_gate_up(place, layer, pieces[first_count:], gate_up, sems)
        late = load_down(place, layer, pieces[:first_count], down, sems, 2)
    else:
        late = load_down(place, layer, pieces[:first_count], down, sems, 2)
        kept_here, kept_sems = take(), take()
        kept_waits = []
        for number, at in enumerate(range(0, down.shape[1], block)):
            for i in range(2):
                span = slice(at, at + block)
                kept_waits.append(start(kept[i].at[:, span], kept_here.at[i, :, span], kept_sems.at[2 * number + i]))
        early = load_gate_up(place, layer, pieces[first_count:], gate_up, sems)
    values = mid[...]
    inv = inverse_root(values)
    ffn_gain = gain[1:, :]
    normed = (values * inv * ffn_gain).astype(BF16)
    if backward:
        normed_t = normed.T
        dy = dy_t[...].T
        rows = grads.shape[2] // 3
        owners = grads.shape[1]
    for one in early if kept is None else late:
        one.wait()
    units = down.shape[1]
    result, d_normed = None, None
    out = []
    for number, at in enumerate(range(0, units, block)):
        span = slice(at, at + block)
        if kept is None:
            gate, up = nn(normed, gate_up[0, :, span]), nn(normed, gate_up[1, :, span])
        else:
            for one in kept_waits[2 * number:2 * number + 2]:
                one.wait()
            gate, up = kept_here[0, :, span], kept_here[1, :, span]
        if keeping is not None:
            keeping[0][:, span] = gate.astype(BF16)
            keeping[1][:, span] = up.astype(BF16)
        if number == 0 and kept is None:
            for one in late:
                one.wait()
        if backward:
            d_hidden = nn(dy, down[:, span])
        for at_column in range(0, block, 128):
            strip = slice(at_column, at_column + 128)
            g, u = gate[:, strip].astype(F32), up[:, strip].astype(F32)
            sg = sigmoid(g)
            swish = g * sg
            if hidden_out is None:
                middle[:, strip] = (swish * u).astype(BF16)
            else:
                hidden_out[:, at + at_column:at + at_column + 128] = (swish * u).astype(BF16)
            if backward:
                d = d_hidden[:, strip]
                gate_back[:, strip] = (d * u * (sg * (1.0 + g * (1.0 - sg)))).astype(BF16)
                up_back[:, strip] = (d * swish).astype(BF16)
        hidden = middle[...] if hidden_out is None else hidden_out[:, span]
        if y_t is not None:
            part = nt(hidden, down[:, span])
            result = part if result is None else result + part
        if backward:
            g_gate, g_up = gate_back[...], up_back[...]
            for half, grad in ((0, g_gate), (1, g_up)):
                value = nn(normed_t, grad).astype(BF16)
                for owner in range(owners):
                    grads[half, owner, number * rows:(number + 1) * rows, :] = value[owner * rows:(owner + 1) * rows]
            value = nn(dy_t[...], hidden).astype(BF16)
            narrow = block // 2
            for i in range(2):
                for half in range(2):
                    for k in range(2):
                        top = (2 * half + k) * rows
                        grads[half, 2 * number + i, 2 * rows:, k * narrow:(k + 1) * narrow] = value[
                            top:top + rows, i * narrow:(i + 1) * narrow
                        ]
            for side, target in ((1 - sec, send), (sec, keep)):
                for window in (
                    (slice(None), slice(number * rows, (number + 1) * rows)),
                    (slice(2 * number, 2 * number + 2), slice(2 * rows, 3 * rows)),
                ):
                    out.append(start(grads.at[(side,) + window], target.at[window], sems_out.at[len(out)]))
            if number == 0 and kept is not None:
                for one in early:
                    one.wait()
            part = nt(g_gate, gate_up[0, :, span]) + nt(g_up, gate_up[1, :, span])
            d_normed = part if d_normed is None else d_normed + part
    if y_t is not None:
        y_t[...] = (values + result).astype(BF16).T
    if backward:
        back, gain_grad = norm_back(values, inv, ffn_gain, d_normed)
        d_gain[...] = gain_grad
        d_mid[...] = dy.astype(F32) + back
        for one in out:
            one.wait()


def feed_forward_result(place, mid, hidden, *rest, layer, count_pieces):
    pieces = rest[:count_pieces]
    y_t, down, sems = rest[count_pieces:]
    waits = load_down(place, layer, pieces, down, sems, 0)
    for one in waits:
        one.wait()
    y_t[...] = (mid[...] + nt(hidden[...], down[...])).astype(BF16).T


VM = pl.BlockSpec(memory_space=pltpu.VMEM)
SM = pl.BlockSpec(memory_space=pltpu.SMEM)
AN = pl.BlockSpec(memory_space=pl.ANY)


def params(mib):
    return pltpu.CompilerParams(vmem_limit_bytes=mib * 1024 * 1024)


def shape(dims, kind):
    return jax.ShapeDtypeStruct(dims, kind)


def cost(gigaflops):
    return pl.CostEstimate(flops=int(gigaflops * 10**6), bytes_accessed=10**4, transcendentals=0)


def run_pack(kernel, name, place, dims, *arrays):
    return pl.pallas_call(
        kernel,
        out_shape=(shape(dims, BF16),) * 2,
        in_specs=[SM] + [VM] * len(arrays),
        out_specs=(VM,) * 2,
        compiler_params=params(56),
        name=name,
    )(place, *arrays)


def run_attention_forward(layer, place, tables, x_t, pieces, tile=256):
    first, cos, sin = tables
    wide, count = x_t.shape
    cols = pieces[0].shape[1]
    owners = place.shape[0] - 1
    return pl.pallas_call(
        functools.partial(attention_forward, layer=layer, tile=tile, count_pieces=len(pieces)),
        out_shape=(
            shape((count, wide), F32),
            shape((WIDTH, count), BF16),
            shape((KVW, count), BF16),
            shape((KVW, count), BF16),
            shape((WIDTH, count), BF16),
            shape((HEADS, count), F32),
            shape((2, wide), F32),
        ),
        in_specs=[SM] + [VM] * 4 + [AN] * len(pieces),
        out_specs=(VM,) * 7,
        scratch_shapes=[
            pltpu.VMEM((2, wide, cols), BF16),
            pltpu.VMEM((owners, EXTRA, cols), BF16),
            pltpu.VMEM((count, count), F32),
            pltpu.SemaphoreType.DMA((3 * owners,)),
        ],
        compiler_params=params(56),
        cost_estimate=cost(6),
        name="attention_forward",
    )(place, first, cos, sin, x_t, *pieces)


def run_attention_backward(layer, place, tables, x_t, gain, d_mid, g_ffn, saved, pieces, tile=256):
    first, cos, sin = tables
    wide, count = x_t.shape
    cols = pieces[0].shape[1]
    owners = place.shape[0] - 1
    padded = wide // owners + EXTRA
    return pl.pallas_call(
        functools.partial(attention_backward, layer=layer, tile=tile, count_pieces=len(pieces)),
        out_shape=(
            shape((wide, count), F32),
            shape((wide, count), BF16),
            shape((owners, padded, cols), BF16),
            shape((owners, padded, cols), BF16),
        ),
        in_specs=[SM] + [VM] * 12 + [AN] * len(pieces),
        out_specs=(VM, VM, AN, AN),
        scratch_shapes=[
            pltpu.VMEM((2, wide, cols), BF16),
            pltpu.VMEM((2, owners, padded, cols), BF16),
            pltpu.VMEM((count, count), F32),
            pltpu.VMEM((WIDTH, count), BF16),
            pltpu.VMEM((WIDTH, count), F32),
            pltpu.VMEM((KVW, count), F32),
            pltpu.VMEM((KVW, count), BF16),
            pltpu.SemaphoreType.DMA((2 * owners,)),
            pltpu.SemaphoreType.DMA((2,)),
        ],
        compiler_params=params(56),
        cost_estimate=cost(10),
        name="attention_backward",
    )(place, first, cos, sin, x_t, gain, d_mid, g_ffn, *saved, *pieces)


def run_attention_scores_backward(layer, place, tables, d_mid, saved, pieces, tile=256):
    first, cos, sin = tables
    count, wide = d_mid.shape
    cols = pieces[0].shape[1]
    owners = place.shape[0] - 1
    q, k, v, o, lse = saved
    return pl.pallas_call(
        functools.partial(attention_scores_backward, layer=layer, tile=tile, count_pieces=len(pieces)),
        out_shape=(shape((WIDTH + KVW, count), BF16), shape((KVW, count), BF16)),
        in_specs=[SM] + [VM] * 8 + [AN] * len(pieces),
        out_specs=(VM, VM),
        scratch_shapes=[
            pltpu.VMEM((2, wide, cols), BF16),
            pltpu.VMEM((count, count), F32),
            pltpu.VMEM((WIDTH, count), BF16),
            pltpu.VMEM((WIDTH, count), F32),
            pltpu.VMEM((KVW, count), F32),
            pltpu.SemaphoreType.DMA((2 * owners,)),
        ],
        compiler_params=params(56),
        cost_estimate=cost(7),
        name="attention_scores_backward",
    )(place, first, cos, sin, d_mid, q, k, v, lse, *pieces)


def run_attention_weights_backward(layer, place, x_t, gain, d_mid, g_ffn, saved, d_qk, d_v, pieces):
    wide, count = x_t.shape
    cols = pieces[0].shape[1]
    owners = place.shape[0] - 1
    padded = wide // owners + EXTRA
    return pl.pallas_call(
        functools.partial(attention_weights_backward, layer=layer, count_pieces=len(pieces)),
        out_shape=(
            shape((wide, count), F32),
            shape((wide, count), BF16),
            shape((owners, padded, cols), BF16),
            shape((owners, padded, cols), BF16),
        ),
        in_specs=[SM] + [VM] * 7 + [AN] * len(pieces),
        out_specs=(VM, VM, AN, AN),
        scratch_shapes=[
            pltpu.VMEM((2, wide, cols), BF16),
            pltpu.VMEM((2, owners, padded, cols), BF16),
            pltpu.SemaphoreType.DMA((2 * owners,)),
            pltpu.SemaphoreType.DMA((2,)),
        ],
        compiler_params=params(56),
        cost_estimate=cost(3),
        name="attention_weights_backward",
    )(place, x_t, gain, d_mid, g_ffn, saved[3], d_qk, d_v, *pieces)


def run_feed_forward(layer, place, mid, gain, pieces, dy_t=None, kept=(), block=768):
    backward = dy_t is not None
    forward = not kept
    count, wide = mid.shape
    owners = place.shape[0] - 1
    rows, cols = (pieces[0].shape[0] - EXTRA) // 2, pieces[0].shape[1]
    out_shape, out_specs = [], []
    scratch = [
        pltpu.VMEM((2, wide, 2 * cols), BF16),
        pltpu.VMEM((wide, 2 * cols), BF16),
        pltpu.SemaphoreType.DMA((8 * owners,)),
    ]
    if forward and backward:
        out_shape.append(shape((count, 2 * cols), BF16))
        out_specs.append(VM)
    elif forward:
        out_shape += [shape((wide, count), BF16)] + [shape((count, 2 * cols), BF16)] * 2
        out_specs += [VM] * 3
    scratch.append(pltpu.VMEM((count, block), BF16))
    if backward:
        out_shape += [
            shape((count, wide), F32),
            shape((1, wide), F32),
            shape((owners, 3 * rows, cols), BF16),
            shape((owners, 3 * rows, cols), BF16),
        ]
        out_specs += [VM, VM, AN, AN]
        scratch += [
            pltpu.VMEM((2, owners, 3 * rows, cols), BF16),
            pltpu.SemaphoreType.DMA((8,)),
            pltpu.VMEM((count, block), BF16),
            pltpu.VMEM((count, block), BF16),
        ]
    if kept:
        scratch += [pltpu.VMEM((2, count, 2 * cols), BF16), pltpu.SemaphoreType.DMA((4 * cols // block,))]
    flops = (7 if forward else 0) + (14 if backward else 0)
    extra = ([dy_t] if backward else []) + list(kept)
    return pl.pallas_call(
        functools.partial(
            feed_forward, layer=layer, forward=forward, backward=backward, block=block, count_pieces=len(pieces)
        ),
        out_shape=tuple(out_shape),
        in_specs=[SM, VM, VM] + [AN] * len(pieces) + [VM] * (len(extra) - len(kept)) + [AN] * len(kept),
        out_specs=tuple(out_specs),
        scratch_shapes=scratch,
        compiler_params=params(56),
        cost_estimate=cost(flops),
        name="feed_forward",
    )(place, mid, gain, *pieces, *extra)


def run_feed_forward_result(layer, place, mid, hidden, pieces):
    count, wide = mid.shape
    owners = place.shape[0] - 1
    return pl.pallas_call(
        functools.partial(feed_forward_result, layer=layer, count_pieces=len(pieces)),
        out_shape=shape((wide, count), BF16),
        in_specs=[SM, VM, VM] + [AN] * len(pieces),
        out_specs=VM,
        scratch_shapes=[pltpu.VMEM((wide, hidden.shape[1]), BF16), pltpu.SemaphoreType.DMA((8 * owners,))],
        compiler_params=params(24),
        cost_estimate=cost(2),
        name="feed_forward_result",
    )(place, mid, hidden, *pieces)


def make_tables(lengths, count):
    ends = jnp.cumsum(lengths)
    starts = ends - lengths
    places = jnp.arange(count, dtype=jnp.int32)
    document = jnp.sum((places[:, None] >= ends[None, :]).astype(jnp.int32), axis=1)
    inside = document[:, None] == jnp.arange(lengths.shape[0], dtype=jnp.int32)[None, :]
    first = jnp.sum(jnp.where(inside, starts[None, :], 0), axis=1)
    position = (places - first).astype(F32)
    frequency = rope_base ** (-(jnp.arange(HALF, dtype=F32) * 2.0 / HEAD))
    angles = frequency[:, None] * position[None, :]
    return first[None, :], jnp.cos(angles), jnp.sin(angles)


def swap(value):
    return lax.ppermute(value, "section", [(0, 1), (1, 0)])


def give(value, target):
    return lax.ppermute(value, "section", [(1 - target, target)])


def exchange(value, axis, bit):
    count = lax.axis_size(axis)
    return lax.ppermute(value, axis, [(i, i ^ bit) for i in range(count)])


def mixed_exchange(value, even_bit, odd_bit):
    owners, replicas = lax.axis_size("fsdp"), lax.axis_size("dp")
    pairs = []
    for i in range(owners):
        for z in range(replicas):
            partner = i ^ (odd_bit if z % 2 else even_bit)
            pairs.append((i * replicas + z, partner * replicas + z))
    return lax.ppermute(value, ("fsdp", "dp"), pairs)


def paired():
    return lax.axis_size("fsdp") == 4 and lax.axis_size("dp") % 2 == 0


def piece_places():
    own = lax.axis_index("fsdp")
    if not paired():
        count = lax.axis_size("fsdp")
        return [own] + [(own + i) % count for i in range(1, count)]
    odd = lax.axis_index("dp") % 2
    near, far = jnp.where(odd == 1, own ^ 2, own ^ 1), jnp.where(odd == 1, own ^ 1, own ^ 2)
    return [own, near, own ^ 3, far]


def first_hop(value):
    if not paired():
        return lax.all_gather(value, "fsdp")
    return mixed_exchange(value, 1, 2)


def second_hop(near):
    if not paired():
        count = lax.axis_size("fsdp")
        own = lax.axis_index("fsdp")
        return [pick(near, (own + i) % count, 0) for i in range(1, count)]
    return [near, mixed_exchange(near, 2, 1), exchange(near, "dp", 1)]


def shared(pieces):
    return pieces + [swap(piece) for piece in pieces]


def tie(*values):
    return lax.optimization_barrier(values)


def pick(value, index, axis):
    return lax.dynamic_index_in_dim(value, index, axis, keepdims=False)


def total(left, right):
    return left + right


def split_first(place, ins, outs, cut):
    (keep, came), outs = ins, list(outs)
    y, x = place[1] // 2, place[1] % 2
    for by_x, low, high in ((True, 0, cut), (False, cut, keep.shape[1])):
        if low == high:
            continue
        hold, away = outs.pop(0), outs.pop(0)
        for i in range(2):
            for target, mine in ((hold, True), (away, False)):
                bit_x, bit_y = (x, y) if mine else (1 - x, 1 - y)
                block = 2 * i + bit_x if by_x else 2 * bit_y + i
                target[i] = total(keep[block, low:high], came[block, low:high])


def split_second(place, ins, outs, order):
    y, x = place[1] // 2, place[1] % 2
    for i, by_x in enumerate(order):
        hold, came, stay, away = ins[2 * i], ins[2 * i + 1], outs[2 * i], outs[2 * i + 1]
        bit = y if by_x else x
        stay[...] = total(hold[bit], came[bit])
        away[...] = total(hold[1 - bit], came[1 - bit])


def stack_sums(place, ins, outs):
    at = 0
    for i in range(0, len(ins), 2):
        rows = ins[i].shape[0]
        outs[0][at:at + rows, :] = total(ins[i][...], ins[i + 1][...])
        at += rows


def from_middle(place, ins, outs):
    z = place[place.shape[0] - 1]
    inner = (z == 1) | (z == 2)

    @pl.when(inner)
    def _():
        outs[0][...] = ins[0][...]

    @pl.when(jnp.logical_not(inner))
    def _():
        outs[0][...] = ins[1][...]


def work(place, *refs, steps):
    ins, outs = [], list(refs)
    for _, count_in, _ in steps:
        ins.append(outs[:count_in])
        outs = outs[count_in:]
    for (body, _, count_out), taken in zip(steps, ins):
        body(place, taken, outs[:count_out])
        outs = outs[count_out:]


def run_work(place, jobs, mib=24):
    ins = [value for job in jobs for value in job[1]]
    out = [shape(dims, BF16) for job in jobs for dims in job[2]]
    done = list(pl.pallas_call(
        functools.partial(work, steps=tuple((job[0], len(job[1]), len(job[2])) for job in jobs)),
        out_shape=tuple(out),
        in_specs=[SM] + [VM] * len(ins),
        out_specs=(VM,) * len(out),
        compiler_params=params(mib),
        name="work",
    )(place, *ins))
    for job in jobs:
        job[3](done[:len(job[2])])
        done = done[len(job[2]):]


def split_large(place, keep, came, hold_x, away_x, hold_y, away_y, left, right, sems_in, sems_out, *, cut):
    owners = keep.shape[0]
    y, x = place[1] // 2, place[1] % 2
    loads = [
        (start(keep.at[f], left.at[f], sems_in.at[2 * f]), start(came.at[f], right.at[f], sems_in.at[2 * f + 1]))
        for f in range(owners)
    ]
    stores = []
    for f in range(owners):
        for one in loads[f]:
            one.wait()
        left[f] = total(left[f], right[f])
        low, high = left.at[f, :cut], left.at[f, cut:]
        stores.append(either(x == f % 2, (low, hold_x.at[f // 2]), (low, away_x.at[f // 2]), None, sems_out.at[2 * f]))
        stores.append(
            either(y == f // 2, (high, hold_y.at[f % 2]), (high, away_y.at[f % 2]), None, sems_out.at[2 * f + 1])
        )
    for one in stores:
        one.wait()


def run_split_large(place, keep, came, cut):
    owners, rows, cols = keep.shape
    low, high = shape((2, cut, cols), BF16), shape((2, rows - cut, cols), BF16)
    return pl.pallas_call(
        functools.partial(split_large, cut=cut),
        out_shape=(low, low, high, high),
        in_specs=[SM, AN, AN],
        out_specs=(AN,) * 4,
        scratch_shapes=[
            pltpu.VMEM(keep.shape, BF16),
            pltpu.VMEM(keep.shape, BF16),
            pltpu.SemaphoreType.DMA((2 * owners,)),
            pltpu.SemaphoreType.DMA((2 * owners,)),
        ],
        compiler_params=params(56),
        name="split_large",
    )(place, keep, came)


class Sum:
    def __init__(self, keep, send, cut, pairs=False):
        self.hold, self.cut, self.pairs = [keep], cut, pairs
        self.chain = lax.axis_size("dp") == 4
        self.came = [swap(send)]
        rows = keep.shape[1]
        self.order = [by_x for by_x, some in ((True, cut > 0), (False, cut < rows)) if some]

    def split(self, second):
        def then(outs):
            self.hold = list(outs[::2])
            self.came = [
                exchange(value, "fsdp", 1 if by_x != second else 2) for value, by_x in zip(outs[1::2], self.order)
            ]
        return then

    def fsdp_first(self):
        _, rows, cols = self.hold[0].shape
        dims = [(2, self.cut if by_x else rows - self.cut, cols) for by_x in self.order for _ in range(2)]
        return functools.partial(split_first, cut=self.cut), self.hold + self.came, dims, self.split(False)

    def fsdp_first_large(self, place):
        self.split(False)(run_split_large(place, self.hold[0], self.came[0], self.cut))

    def fsdp_second(self):
        ins = [value for pair in zip(self.hold, self.came) for value in pair]
        dims = [value.shape[1:] for value in self.hold for _ in range(2)]
        return functools.partial(split_second, order=tuple(self.order)), ins, dims, self.split(True)

    def dp(self, hop):
        ins = [value for pair in zip(self.hold, self.came) for value in pair]
        dims = [(sum(value.shape[0] for value in self.hold), self.hold[0].shape[1])]

        def then(outs):
            value = outs[0]
            self.hold = [value]
            if not self.chain:
                self.came = [lax.psum(value, "dp") if hop == 0 else jnp.zeros_like(value)]
                if hop == 0:
                    self.hold = [jnp.zeros_like(value)]
            elif self.pairs:
                self.came = [exchange(value, "dp", 1 + hop)] if hop < 2 else []
            else:
                pairs = ([(0, 1), (3, 2)], [(1, 2), (2, 1)], [(1, 0), (2, 3)])[hop]
                self.came = [lax.ppermute(value, "dp", pairs)]

        return stack_sums, ins, dims, then

    def finish(self):
        def then(outs):
            self.hold, self.came = list(outs), []

        if not self.chain or self.pairs:
            return self.dp(2)[:3] + (then,)
        return from_middle, self.hold + self.came, [self.hold[0].shape], then


def choose(line, ff1, ff0, ff0_came, at1, at0, at0_came, ff_own, ff_send, at_own, at_send, *, chain):
    z = line[line.shape[0] - 1]
    inner = (z == 1) | (z == 2)
    for sec in range(2):
        targets = (ff_own, at_own, ff_send, at_send) if sec == 0 else (ff_send, at_send, ff_own, at_own)

        @pl.when(line[0] == sec)
        def _(targets=targets):
            if chain:

                @pl.when(inner)
                def _():
                    targets[0][...] = ff0[...]

                @pl.when(jnp.logical_not(inner))
                def _():
                    targets[0][...] = ff0_came[...]
            else:
                targets[0][...] = total(ff0[...], ff0_came[...])
            targets[1][...] = total(at0[...], at0_came[...])
            targets[2][...] = ff1[...]
            targets[3][...] = at1[...]


def run_choose(line, ff1, ff0, at1, at0):
    ff, at = shape(ff1.shape, BF16), shape(at1.shape, BF16)
    return pl.pallas_call(
        functools.partial(choose, chain=ff0.chain),
        out_shape=(ff, ff, at, at),
        in_specs=[SM] + [VM] * 6,
        out_specs=(VM,) * 4,
        compiler_params=params(24),
        name="choose",
    )(line, ff1, ff0.hold[0], ff0.came[0], at1, at0.hold[0], at0.came[0])


def unpack(place, ff_own, ff_given, at_own, at_given, gate, up, down, wq, wk, wv, wo, gains):
    rows = gate.shape[0]
    narrow = down.shape[1]

    def emit(half, part, value):
        wide = (gate, up)[half]
        for i in range(2):
            wide[:, 2 * i * narrow:(2 * i + 2) * narrow] = part[i * rows:(i + 1) * rows, :].astype(F32)
        top = 2 * half * rows
        down[top:top + rows, :] = part[2 * rows:, :narrow].astype(F32)
        down[top + rows:top + 2 * rows, :] = part[2 * rows:, narrow:].astype(F32)
        left, right = ((wq, wk), (wo, wv))[half]
        left[...] = value[:rows, :WIDTH].astype(F32)
        right[...] = value[:rows, WIDTH:].astype(F32)
        if half == 0:
            gains[...] = value[rows:, :rows].astype(F32)[:2]

    for sec in range(2):

        @pl.when(place[0] == sec)
        def _(sec=sec):
            emit(sec, ff_own, at_own)
            emit(1 - sec, ff_given, at_given)


def run_unpack(place, ff_own, ff_given, at_own, at_given):
    rows, cols = ff_own.shape[0] // 3, ff_own.shape[1]
    return pl.pallas_call(
        unpack,
        out_shape=(
            shape((rows, 2 * cols), F32),
            shape((rows, 2 * cols), F32),
            shape((4 * rows, cols // 2), F32),
            shape((rows, WIDTH), F32),
            shape((rows, KVW), F32),
            shape((rows, KVW), F32),
            shape((rows, WIDTH), F32),
            shape((2, rows), F32),
        ),
        in_specs=[SM] + [VM] * 4,
        out_specs=(VM,) * 8,
        compiler_params=params(32),
        name="unpack",
    )(place, ff_own, ff_given, at_own, at_given)


def local(
    tokens,
    cotangent,
    doc_lengths,
    w_query,
    w_key,
    w_value,
    w_out,
    w_gate,
    w_up,
    w_down,
    gain_attn,
    gain_ffn,
):
    sec = lax.axis_index("section")
    first_section = sec == 0
    count = tokens.shape[2]
    place = jnp.stack([jnp.asarray(i, jnp.int32) for i in [sec] + piece_places()])
    line = jnp.concatenate([place, lax.axis_index("dp").astype(jnp.int32)[None]])
    rows, cols = w_query.shape[1], w_query.shape[2] + w_key.shape[2]
    own_at, rest_at = run_pack(
        pack_first, "pack_first", place, (2 * rows + EXTRA, cols),
        w_query[0], w_key[0], w_value[0], w_out[0], gain_attn, gain_ffn, w_down[0].T,
    )
    later, own_at, rest_at = tie(place, own_at, rest_at)
    own_ff, rest_ff = run_pack(pack_second, "pack_second", later, (2 * rows, cols), w_gate[0], w_up[0])

    def own_pieces(own, rest):
        came_own, came_rest = swap(rest), swap(own)
        home = [own, came_own, rest, came_rest]
        return home, jnp.where(first_section, own, came_own), jnp.where(first_section, came_own, own)

    at_home, at_zero, at_one = own_pieces(own_at, rest_at)
    ff_home, ff_zero, ff_one = own_pieces(own_ff, rest_ff)
    tables = make_tables(pick(doc_lengths[0], sec, 0), count)
    x0 = jnp.swapaxes(pick(tokens[0], sec, 0), 0, 1)
    dy1 = jnp.swapaxes(pick(cotangent[0], sec, 0), 0, 1)

    near_at0 = first_hop(at_zero)
    near_ff0 = first_hop(ff_zero)
    near_at0, ff_one, x0, dy1, *tables = tie(near_at0, ff_one, x0, dy1, *tables)
    at0 = second_hop(near_at0)
    near_ff0, at_one, ff_one, *at0 = tie(near_ff0, at_one, ff_one, *at0)
    ff0 = second_hop(near_ff0)
    near_at1 = first_hop(at_one)
    near_ff1 = first_hop(ff_one)
    at0 = shared(at0)
    mid0, *saved0, gains0 = run_attention_forward(0, place, tables, x0, at_home + at0)
    mid0, near_at1, *ff0 = tie(mid0, near_at1, *ff0)

    ff0 = shared(ff0)
    at1 = second_hop(near_at1)
    y0, gate0, up0 = run_feed_forward(0, place, mid0, gains0, at_home + at0 + ff_home + ff0)
    y0, near_ff1, *at1 = tie(y0, near_ff1, *at1)

    at1 = shared(at1)
    ff1 = second_hop(near_ff1)
    mid1, *saved1, gains1 = run_attention_forward(1, place, tables, y0, at_home + at1)
    mid1, *ff1 = tie(mid1, *ff1)
    ff1 = shared(ff1)
    hidden1, d_mid1, g_ffn1, ff_keep1, ff_send1 = run_feed_forward(
        1, place, mid1, gains1, at_home + at1 + ff_home + ff1, dy_t=dy1
    )

    sums = []

    def after(waited, *others):
        cells = [(one.came, i) for one, i in waited]
        for one in sums:
            cells += [(one.hold, i) for i in range(len(one.hold))]
        held = list(tie(*others, *[array[i] for array, i in cells]))
        for (array, i), value in zip(cells, held[len(others):]):
            array[i] = value
        return held[:len(others)]

    def both_rows(own0, own1):
        back = swap(jnp.where(first_section, own1, own0))
        both = jnp.where(first_section, jnp.stack([own0, back]), jnp.stack([back, own1]))
        return jnp.swapaxes(both, 1, 2)[None, None]

    ff_cut, at_cut = ff_keep1.shape[1] // 32 * 16, (rows + EXTRA) // 32 * 16
    f1 = Sum(ff_keep1, ff_send1, ff_cut)
    sums.append(f1)
    dx1, dy0, at_keep1, at_send1 = run_attention_backward(
        1, place, tables, y0, gains1, d_mid1, g_ffn1, saved1, at_home + at1
    )
    dy0, at_keep1, at_send1 = after([(f1, 0)], dy0, at_keep1, at_send1)

    f1.fsdp_first_large(place)
    a1 = Sum(at_keep1, at_send1, at_cut)
    sums.append(a1)
    (dy0,) = after([], dy0)
    d_mid0, g_ffn0, ff_keep0, ff_send0 = run_feed_forward(
        0, place, mid0, gains0, at_home + at0 + ff_home + ff0, dy_t=dy0, kept=(gate0, up0)
    )
    d_mid0, ff_keep0, ff_send0 = after([(f1, 0), (f1, 1), (a1, 0)], d_mid0, ff_keep0, ff_send0)

    f0 = Sum(ff_keep0, ff_send0, ff_cut)
    sums.append(f0)
    run_work(line, [f1.fsdp_second(), a1.fsdp_first()])
    (d_mid0,) = after([], d_mid0)
    d_qk0, d_v0 = run_attention_scores_backward(0, place, tables, d_mid0, saved0, at_home + at0)
    d_qk0, d_v0 = after([(f0, 0), (f1, 0), (f1, 1), (a1, 0), (a1, 1)], d_qk0, d_v0)

    f0.fsdp_first_large(place)
    after([])
    run_work(line, [f1.dp(0), a1.fsdp_second()])
    (d_qk0,) = after([], d_qk0)
    dx0, _, at_keep0, at_send0 = run_attention_weights_backward(
        0, place, x0, gains0, d_mid0, g_ffn0, saved0, d_qk0, d_v0, at_home + at0
    )
    at_send0, at_keep0 = after([(f0, 0), (f0, 1), (f1, 0), (a1, 0), (a1, 1)], at_send0, at_keep0)

    a0 = Sum(at_keep0, at_send0, at_cut, True)
    sums.append(a0)
    run_work(line, [f0.fsdp_second(), f1.dp(1)])
    after([(a0, 0)])
    run_work(line, [a0.fsdp_first(), a1.dp(0)])
    dx0, dx1, hidden1 = after([(f0, 0), (f0, 1), (f1, 0), (a1, 0), (a0, 0), (a0, 1)], dx0, dx1, hidden1)

    run_work(line, [f0.dp(0), f1.dp(2), a1.dp(1), a0.fsdp_second()])
    y1 = run_feed_forward_result(1, place, mid1, hidden1, at_home + at1)
    dx0, dx1, y1 = after([(f0, 0), (f1, 0), (a1, 0), (a0, 0), (a0, 1)], dx0, dx1, y1)

    run_work(line, [f0.dp(1), a1.dp(2), a0.dp(0), f1.finish()])
    dx0, dx1 = after([], dx0, dx1)
    grad = both_rows(dx0, dx1)
    (grad,) = after([(f0, 0), (a1, 0), (a0, 0)], grad)

    run_work(line, [f0.dp(2), a0.dp(1), a1.finish()])
    y0, y1 = after([], y0, y1)
    out = both_rows(y0, y1)
    (out,) = after([(f0, 0), (a0, 0)], out)

    ff_own, ff_send, at_own, at_send = run_choose(line, f1.hold[0], f0, a1.hold[0], a0)
    gate, up, down, wq, wk, wv, wo, gain_grads = run_unpack(place, ff_own, swap(ff_send), at_own, swap(at_send))

    return (
        out,
        grad,
        wq[None],
        wk[None],
        wv[None],
        wo[None],
        gate[None],
        up[None],
        down.T[None],
        gain_grads[:1],
        gain_grads[1:],
    )


def solution(mesh):
    whole = P(("fsdp", "dp"), None, None, None)
    weight = P("section", "fsdp", None)
    gain = P("section", "fsdp")
    rows = P("section", ("fsdp", "dp"), None, None, None)
    in_specs = (whole, whole, P(("fsdp", "dp"), None, None)) + (weight,) * 7 + (gain,) * 2
    out_specs = (rows, rows) + (weight,) * 7 + (gain,) * 2
    return jax.shard_map(local, mesh=mesh, in_specs=in_specs, out_specs=out_specs, check_vma=False)
```

```python
import functools
import jax
import jax.numpy as jnp
from jax import lax
from jax.experimental import pallas as pl
from jax.experimental.pallas import tpu as pltpu
from jax.sharding import PartitionSpec as P

HEADS = 9
KV_HEADS = 3
GROUP = HEADS // KV_HEADS
HEAD = 64
HALF = HEAD // 2
WIDTH = HEADS * HEAD
KVW = KV_HEADS * HEAD

epsilon = 1e-05
rope_base = 100000.0
masked_score = -1e30
SCALE = HEAD ** (-0.5)
EXTRA = 16
F32 = jnp.float32
BF16 = jnp.bfloat16


def nn(left, right):
    return lax.dot_general(left, right, (((1,), (0,)), ((), ())), preferred_element_type=F32)


def nt(left, right):
    return lax.dot_general(left, right, (((1,), (1,)), ((), ())), preferred_element_type=F32)


def inverse_root(values):
    return lax.rsqrt(jnp.mean(values * values, axis=-1, keepdims=True) + epsilon)


def norm_back(values, inv_root, gain, upstream):
    gain_grad = jnp.sum(upstream * values * inv_root, axis=0, keepdims=True)
    scaled = upstream * gain
    dot = jnp.mean(scaled * values, axis=-1, keepdims=True)
    return inv_root * scaled - values * (inv_root * inv_root * inv_root * dot), gain_grad


def sigmoid(values):
    return 0.5 * jnp.tanh(0.5 * values) + 0.5


def pack_first(wq, wk, wv, wo, gain_attn, gain_ffn, down, own, rest):
    rows, cols = wq.shape[0], own.shape[1]
    down_cols = down.shape[1]
    half_down = down.shape[0] // 2
    top = rows + EXTRA

    def write(target, half):
        left, right = ((wq, wk), (wo, wv))[half]
        target[:rows, :] = jnp.concatenate([left[...], right[...]], axis=1)
        target[rows:top, :] = jnp.zeros((EXTRA, cols), BF16)
        target[rows:top, :rows] = jnp.concatenate(
            [gain_attn[...].astype(F32), gain_ffn[...].astype(F32), jnp.zeros((EXTRA - 2, rows), F32)], axis=0
        ).astype(BF16)
        for i in range(2):
            at = half * half_down + i * rows
            target[top:, i * down_cols:(i + 1) * down_cols] = down[at:at + rows, :]

    for number in range(2):

        @pl.when(lax.axis_index("section") == number)
        def _(number=number):
            write(own, number)
            write(rest, 1 - number)


def pack_second(gate, up, own, rest):
    rows, cols = gate.shape[0], own.shape[1]

    def write(target, half):
        wide = (gate, up)[half]
        target[:rows, :] = wide[:, :cols]
        target[rows:, :] = wide[:, cols:]

    for number in range(2):

        @pl.when(lax.axis_index("section") == number)
        def _(number=number):
            write(own, number)
            write(rest, 1 - number)


def either(condition, first, second, target, sem):
    first, second = ((first, target), (second, target)) if target is not None else (first, second)

    @pl.when(condition)
    def _():
        pltpu.make_async_copy(*first, sem).start()

    @pl.when(jnp.logical_not(condition))
    def _():
        pltpu.make_async_copy(*second, sem).start()

    return pltpu.make_async_copy(*first, sem)


def start(source, target, sem):
    one = pltpu.make_async_copy(source, target, sem)
    one.start()
    return one


def sides(place, layer, pieces):
    sec = place[0]
    slots = place.shape[0] - 1
    found = []
    for number, (half, rest) in enumerate(((sec, pieces[4:3 + slots]), (1 - sec, pieces[3 + slots:]))):
        found.append((half, place[1], pieces[2 * number], pieces[2 * number + 1]))
        for slot, piece in enumerate(rest):
            found.append((half, place[2 + slot], piece, None))
    return found


def load_attention(place, layer, pieces, weights, gains, sems):
    rows = (pieces[0].shape[0] - EXTRA) // 2
    home = place[0] == layer
    waits = []
    slots = place.shape[0] - 1
    for number, (half, owner, source, other) in enumerate(sides(place, layer, pieces)):
        target = weights.at[half, pl.ds(pl.multiple_of(owner * rows, 16), rows), :]
        window = slice(0, rows)
        if other is None:
            waits.append(start(source.at[window], target, sems.at[number]))
        else:
            waits.append(either(home, source.at[window], other.at[window], target, sems.at[number]))
        if number < slots and gains is not None:
            window, target, sem = slice(rows, rows + EXTRA), gains.at[owner], sems.at[2 * slots + number]
            if other is None:
                waits.append(start(source.at[window], target, sem))
            else:
                waits.append(either(home, source.at[window], other.at[window], target, sem))
    return waits


def load_gate_up(place, layer, pieces, gate_up, sems):
    rows, cols = pieces[0].shape[0] // 2, pieces[0].shape[1]
    home = place[0] == layer
    waits = []
    for part in range(2):
        waits.append([])
        for number, (half, owner, source, other) in enumerate(sides(place, layer, pieces)):
            window = slice(part * rows, (part + 1) * rows)
            target = gate_up.at[half, pl.ds(pl.multiple_of(owner * rows, 16), rows), part * cols:(part + 1) * cols]
            sem = sems.at[4 * number + part]
            if other is None:
                waits[part].append(start(source.at[window], target, sem))
            else:
                waits[part].append(either(home, source.at[window], other.at[window], target, sem))
    return waits


def load_down(place, layer, pieces, down, sems, first_sem):
    rows, narrow = (pieces[0].shape[0] - EXTRA) // 2, pieces[0].shape[1] // 2
    home = place[0] == layer
    waits = []
    for number, (half, owner, source, other) in enumerate(sides(place, layer, pieces)):
        for i in range(2):
            window = (slice(rows + EXTRA, 2 * rows + EXTRA), slice(i * narrow, (i + 1) * narrow))
            top = pl.multiple_of(half * (2 * rows) + i * rows, 16)
            target = down.at[pl.ds(top, rows), pl.ds(pl.multiple_of(owner * narrow, 128), narrow)]
            sem = sems.at[4 * number + first_sem + i]
            if other is None:
                waits.append(start(source.at[window], target, sem))
            else:
                waits.append(either(home, source.at[window], other.at[window], target, sem))
    return waits


def fill_bias(first, bias):
    count = bias.shape[0]
    key = lax.broadcasted_iota(jnp.int32, (count, count), 0)
    query = lax.broadcasted_iota(jnp.int32, (count, count), 1)
    allowed = (key >= first[...]) & (key <= query)
    bias[...] = jnp.where(allowed, 0.0, masked_score).astype(F32)


def attention_forward(place, first, cos, sin, x_t, *rest, layer, tile, count_pieces):
    pieces = rest[:count_pieces]
    mid, q_out, k_out, v_out, o_out, lse_out, gain_out, weights, gain_parts, bias, sems = rest[count_pieces:]
    owners = gain_parts.shape[0]
    rows = weights.shape[1] // owners
    waits = load_attention(place, layer, pieces, weights, gain_parts, sems)
    count = x_t.shape[1]
    values = x_t[...].T.astype(F32)
    scaled = values * inverse_root(values)
    fill_bias(first, bias)
    for one in waits:
        one.wait()
    gain = jnp.concatenate([gain_parts[f][:2, :rows].astype(F32) for f in range(owners)], axis=1)
    gain_out[...] = gain
    normed = (scaled * gain[:1]).astype(BF16)
    qk = nt(weights[0].T, normed)
    v_out[...] = nt(weights[1, :, WIDTH:].T, normed).astype(BF16)
    c, s = cos[...], sin[...]

    def turned(part):
        low, high = part[:HALF], part[HALF:]
        return jnp.concatenate([low * c - high * s, high * c + low * s], axis=0)

    for head in range(HEADS):
        span = slice(head * HEAD, (head + 1) * HEAD)
        q_out[span, :] = (turned(qk[span]) * SCALE).astype(BF16)
    for j in range(KV_HEADS):
        at = WIDTH + j * HEAD
        k_out[j * HEAD:(j + 1) * HEAD, :] = turned(qk[at:at + HEAD]).astype(BF16)
    for j in range(KV_HEADS):
        keys = k_out[j * HEAD:(j + 1) * HEAD, :].T
        vals = v_out[j * HEAD:(j + 1) * HEAD, :]
        for g in range(GROUP):
            head = j * GROUP + g
            span = slice(head * HEAD, (head + 1) * HEAD)
            for at in range(0, count, tile):
                end = at + tile
                scores = nn(keys[:end], q_out[span, at:end]) + bias[:end, at:end]
                top = jnp.max(scores, axis=0, keepdims=True)
                power = jnp.exp(scores - top)
                total = jnp.sum(power, axis=0, keepdims=True)
                mixed = nn(vals[:, :end], power.astype(BF16))
                o_out[span, at:end] = (mixed / total).astype(BF16)
                lse_out[head:head + 1, at:end] = top + jnp.log(total)
    mid[...] = values + nn(o_out[...].T, weights[1, :, :WIDTH])


def attention_backward(place, first, cos, sin, x_t, gain, d_mid, g_ffn, q, k, v, o, lse, *rest, layer, tile, count_pieces):
    pieces = rest[:count_pieces]
    dx, dx_low, keep, send, weights, grads, bias, g_out, d_q, d_k, d_v, sems, sems_out = rest[count_pieces:]
    owners = grads.shape[1]
    rows = weights.shape[1] // owners
    sec = place[0]
    waits = load_attention(place, layer, pieces, weights, None, sems)
    count = x_t.shape[1]
    g_mid = d_mid[...].astype(BF16)
    fill_bias(first, bias)
    for one in waits:
        one.wait()
    g_out[...] = nt(weights[1, :, :WIDTH], g_mid).astype(BF16)

    def store(side, columns, value):
        for owner in range(owners):
            grads[side, owner, :rows, columns] = value[owner * rows:(owner + 1) * rows].astype(BF16)

    store(1, slice(0, WIDTH), nn(o[...], g_mid))
    c, s = cos[...], sin[...]

    def turned_back(part):
        low, high = part[:HALF], part[HALF:]
        return jnp.concatenate([low * c + high * s, high * c - low * s], axis=0)

    for j in range(KV_HEADS):
        own = slice(j * HEAD, (j + 1) * HEAD)
        keys_t = k[own, :]
        keys = keys_t.T
        vals = v[own, :].T
        k_sum = [jnp.zeros((HEAD, tile), F32) for _ in range(count // tile)]
        v_sum = [jnp.zeros((HEAD, tile), F32) for _ in range(count // tile)]
        for g in range(GROUP):
            head = j * GROUP + g
            span = slice(head * HEAD, (head + 1) * HEAD)
            for at in range(0, count, tile):
                end = at + tile
                q_part = q[span, at:end]
                g_part = g_out[span, at:end]
                power = jnp.exp(nn(keys[:end], q_part) + bias[:end, at:end] - lse[head:head + 1, at:end])
                d_prob = nn(vals[:end], g_part)
                delta = jnp.sum(power * d_prob, axis=0, keepdims=True)
                d_score = (power * (d_prob - delta)).astype(BF16)
                power = power.astype(BF16)
                v_add = nt(g_part, power)
                k_add = nt(q_part, d_score)
                for i in range(end // tile):
                    v_sum[i] = v_sum[i] + v_add[:, i * tile:(i + 1) * tile]
                    k_sum[i] = k_sum[i] + k_add[:, i * tile:(i + 1) * tile]
                d_q[span, at:end] = nn(keys_t[:, :end], d_score) * SCALE
        d_k[own, :] = jnp.concatenate(k_sum, axis=1)
        d_v[own, :] = jnp.concatenate(v_sum, axis=1).astype(BF16)
    turned = [turned_back(d_q[h * HEAD:(h + 1) * HEAD, :]).astype(BF16) for h in range(HEADS)]
    turned += [turned_back(d_k[h * HEAD:(h + 1) * HEAD, :]).astype(BF16) for h in range(KV_HEADS)]
    d_qk = jnp.concatenate(turned, axis=0)
    values = x_t[...].T.astype(F32)
    inv = inverse_root(values)
    attn_gain = gain[:1, :]
    normed_t = (values * inv * attn_gain).astype(BF16).T
    store(0, slice(None), nt(normed_t, d_qk))
    store(1, slice(WIDTH, None), nt(normed_t, d_v[...]))
    d_normed = (nn(weights[0], d_qk) + nn(weights[1, :, WIDTH:], d_v[...])).T
    back, gain_grad = norm_back(values, inv, attn_gain, d_normed)
    for owner in range(owners):
        span = slice(owner * rows, (owner + 1) * rows)
        both = jnp.concatenate([gain_grad[:, span], g_ffn[:, span]], axis=0)
        grads[:, owner, rows:, :] = jnp.zeros((2, EXTRA, grads.shape[3]), BF16)
        padded = jnp.concatenate([both, jnp.zeros((EXTRA - 2, rows), F32)], axis=0)
        grads[0, owner, rows:, :rows] = padded.astype(BF16)
    out = [start(grads.at[1 - sec], send, sems_out.at[0]), start(grads.at[sec], keep, sems_out.at[1])]
    total = (d_mid[...] + back).T
    dx[...] = total
    dx_low[...] = total.astype(BF16)
    for one in out:
        one.wait()


def attention_scores_backward(place, first, cos, sin, d_mid, q, k, v, lse, *rest, layer, tile, count_pieces):
    pieces = rest[:count_pieces]
    d_qk, d_v, weights, bias, g_out, d_q, d_k, sems = rest[count_pieces:]
    waits = load_attention(place, layer, pieces, weights, None, sems)
    count = d_mid.shape[0]
    g_mid = d_mid[...].astype(BF16)
    fill_bias(first, bias)
    for one in waits:
        one.wait()
    g_out[...] = nt(weights[1, :, :WIDTH], g_mid).astype(BF16)
    c, s = cos[...], sin[...]

    def turned_back(part):
        low, high = part[:HALF], part[HALF:]
        return jnp.concatenate([low * c + high * s, high * c - low * s], axis=0)

    for j in range(KV_HEADS):
        own = slice(j * HEAD, (j + 1) * HEAD)
        keys_t = k[own, :]
        keys = keys_t.T
        vals = v[own, :].T
        k_sum = [jnp.zeros((HEAD, tile), F32) for _ in range(count // tile)]
        v_sum = [jnp.zeros((HEAD, tile), F32) for _ in range(count // tile)]
        for g in range(GROUP):
            head = j * GROUP + g
            span = slice(head * HEAD, (head + 1) * HEAD)
            for at in range(0, count, tile):
                end = at + tile
                q_part = q[span, at:end]
                g_part = g_out[span, at:end]
                power = jnp.exp(nn(keys[:end], q_part) + bias[:end, at:end] - lse[head:head + 1, at:end])
                d_prob = nn(vals[:end], g_part)
                delta = jnp.sum(power * d_prob, axis=0, keepdims=True)
                d_score = (power * (d_prob - delta)).astype(BF16)
                power = power.astype(BF16)
                v_add = nt(g_part, power)
                k_add = nt(q_part, d_score)
                for i in range(end // tile):
                    v_sum[i] = v_sum[i] + v_add[:, i * tile:(i + 1) * tile]
                    k_sum[i] = k_sum[i] + k_add[:, i * tile:(i + 1) * tile]
                d_q[span, at:end] = nn(keys_t[:, :end], d_score) * SCALE
        d_k[own, :] = jnp.concatenate(k_sum, axis=1)
        d_v[own, :] = jnp.concatenate(v_sum, axis=1).astype(BF16)
    for h in range(HEADS):
        d_qk[h * HEAD:(h + 1) * HEAD, :] = turned_back(d_q[h * HEAD:(h + 1) * HEAD, :]).astype(BF16)
    for h in range(KV_HEADS):
        d_qk[WIDTH + h * HEAD:WIDTH + (h + 1) * HEAD, :] = turned_back(d_k[h * HEAD:(h + 1) * HEAD, :]).astype(BF16)


def attention_weights_backward(place, x_t, gain, d_mid, g_ffn, o, d_qk, d_v, *rest, layer, count_pieces):
    pieces = rest[:count_pieces]
    dx, dx_low, keep, send, weights, grads, sems, sems_out = rest[count_pieces:]
    owners = grads.shape[1]
    rows = weights.shape[1] // owners
    sec = place[0]
    waits = load_attention(place, layer, pieces, weights, None, sems)

    def store(side, columns, value):
        for owner in range(owners):
            grads[side, owner, :rows, columns] = value[owner * rows:(owner + 1) * rows].astype(BF16)

    store(1, slice(0, WIDTH), nn(o[...], d_mid[...].astype(BF16)))
    values = x_t[...].T.astype(F32)
    inv = inverse_root(values)
    attn_gain = gain[:1, :]
    normed_t = (values * inv * attn_gain).astype(BF16).T
    store(0, slice(None), nt(normed_t, d_qk[...]))
    store(1, slice(WIDTH, None), nt(normed_t, d_v[...]))
    for one in waits:
        one.wait()
    d_normed = (nn(weights[0], d_qk[...]) + nn(weights[1, :, WIDTH:], d_v[...])).T
    back, gain_grad = norm_back(values, inv, attn_gain, d_normed)
    for owner in range(owners):
        span = slice(owner * rows, (owner + 1) * rows)
        both = jnp.concatenate([gain_grad[:, span], g_ffn[:, span]], axis=0)
        grads[:, owner, rows:, :] = jnp.zeros((2, EXTRA, grads.shape[3]), BF16)
        padded = jnp.concatenate([both, jnp.zeros((EXTRA - 2, rows), F32)], axis=0)
        grads[0, owner, rows:, :rows] = padded.astype(BF16)
    out = [start(grads.at[1 - sec], send, sems_out.at[0]), start(grads.at[sec], keep, sems_out.at[1])]
    total = (d_mid[...] + back).T
    dx[...] = total
    dx_low[...] = total.astype(BF16)
    for one in out:
        one.wait()


def feed_forward(place, mid, gain, *rest, layer, forward, backward, block, count_pieces):
    pieces = rest[:count_pieces]
    rest = list(rest[count_pieces:])
    take = lambda: rest.pop(0)
    dy_t = take() if backward else None
    kept = (take(), take()) if backward and not forward else None
    y_t = take() if forward and not backward else None
    hidden_out = take() if forward and backward else None
    keeping = (take(), take()) if forward and not backward else None
    if backward:
        d_mid, d_gain, keep, send = take(), take(), take(), take()
    gate_up, down, sems = take(), take(), take()
    middle = take()
    if backward:
        grads, sems_out, gate_back, up_back = take(), take(), take(), take()
    sec = place[0]
    first_count = len(pieces) // 2
    if kept is None:
        early = load_gate_up(place, layer, pieces[first_count:], gate_up, sems)
        late = load_down(place, layer, pieces[:first_count], down, sems, 2)
    else:
        late = load_down(place, layer, pieces[:first_count], down, sems, 2)
        kept_here, kept_sems = take(), take()
        kept_waits = []
        for number, at in enumerate(range(0, down.shape[1], block)):
            for i in range(2):
                span = slice(at, at + block)
                kept_waits.append(start(kept[i].at[:, span], kept_here.at[i, :, span], kept_sems.at[2 * number + i]))
        early = load_gate_up(place, layer, pieces[first_count:], gate_up, sems)
    values = mid[...]
    inv = inverse_root(values)
    ffn_gain = gain[1:, :]
    normed = (values * inv * ffn_gain).astype(BF16)
    if backward:
        normed_t = normed.T
        dy = dy_t[...].T
        rows = grads.shape[2] // 3
        owners = grads.shape[1]
    if kept is not None:
        for one in late:
            one.wait()
    units = down.shape[1]
    result, d_normed = None, None
    out = []
    for number, at in enumerate(range(0, units, block)):
        span = slice(at, at + block)
        if kept is None:
            for one in early[number]:
                one.wait()
            gate, up = nn(normed, gate_up[0, :, span]), nn(normed, gate_up[1, :, span])
        else:
            for one in kept_waits[2 * number:2 * number + 2]:
                one.wait()
            gate, up = kept_here[0, :, span], kept_here[1, :, span]
        if keeping is not None:
            keeping[0][:, span] = gate.astype(BF16)
            keeping[1][:, span] = up.astype(BF16)
        if number == 0 and kept is None:
            for one in late:
                one.wait()
        if backward:
            d_hidden = nn(dy, down[:, span])
        for at_column in range(0, block, 128):
            strip = slice(at_column, at_column + 128)
            g, u = gate[:, strip].astype(F32), up[:, strip].astype(F32)
            sg = sigmoid(g)
            swish = g * sg
            if hidden_out is None:
                middle[:, strip] = (swish * u).astype(BF16)
            else:
                hidden_out[:, at + at_column:at + at_column + 128] = (swish * u).astype(BF16)
            if backward:
                d = d_hidden[:, strip]
                gate_back[:, strip] = (d * u * (sg * (1.0 + g * (1.0 - sg)))).astype(BF16)
                up_back[:, strip] = (d * swish).astype(BF16)
        hidden = middle[...] if hidden_out is None else hidden_out[:, span]
        if y_t is not None:
            part = nt(hidden, down[:, span])
            result = part if result is None else result + part
        if backward:
            g_gate, g_up = gate_back[...], up_back[...]
            for half, grad in ((0, g_gate), (1, g_up)):
                value = nn(normed_t, grad).astype(BF16)
                for owner in range(owners):
                    grads[half, owner, number * rows:(number + 1) * rows, :] = value[owner * rows:(owner + 1) * rows]
            value = nn(dy_t[...], hidden).astype(BF16)
            narrow = block // 2
            for i in range(2):
                for half in range(2):
                    for k in range(2):
                        top = (2 * half + k) * rows
                        grads[half, 2 * number + i, 2 * rows:, k * narrow:(k + 1) * narrow] = value[
                            top:top + rows, i * narrow:(i + 1) * narrow
                        ]
            for side, target in ((1 - sec, send), (sec, keep)):
                for window in (
                    (slice(None), slice(number * rows, (number + 1) * rows)),
                    (slice(2 * number, 2 * number + 2), slice(2 * rows, 3 * rows)),
                ):
                    out.append(start(grads.at[(side,) + window], target.at[window], sems_out.at[len(out)]))
            if kept is not None:
                for one in early[number]:
                    one.wait()
            part = nt(g_gate, gate_up[0, :, span]) + nt(g_up, gate_up[1, :, span])
            d_normed = part if d_normed is None else d_normed + part
    if y_t is not None:
        y_t[...] = (values + result).astype(BF16).T
    if backward:
        back, gain_grad = norm_back(values, inv, ffn_gain, d_normed)
        d_gain[...] = gain_grad
        d_mid[...] = dy.astype(F32) + back
        for one in out:
            one.wait()


def feed_forward_result(place, mid, hidden, *rest, layer, count_pieces):
    pieces = rest[:count_pieces]
    y_t, down, sems = rest[count_pieces:]
    waits = load_down(place, layer, pieces, down, sems, 0)
    for one in waits:
        one.wait()
    y_t[...] = (mid[...] + nt(hidden[...], down[...])).astype(BF16).T


VM = pl.BlockSpec(memory_space=pltpu.VMEM)
SM = pl.BlockSpec(memory_space=pltpu.SMEM)
AN = pl.BlockSpec(memory_space=pl.ANY)


def params(mib):
    return pltpu.CompilerParams(vmem_limit_bytes=mib * 1024 * 1024)


def shape(dims, kind):
    return jax.ShapeDtypeStruct(dims, kind)


def cost(gigaflops):
    return pl.CostEstimate(flops=int(gigaflops * 10**6), bytes_accessed=10**4, transcendentals=0)


def run_pack(kernel, name, dims, *arrays):
    return pl.pallas_call(
        kernel,
        out_shape=(shape(dims, BF16),) * 2,
        in_specs=[VM] * len(arrays),
        out_specs=(VM,) * 2,
        compiler_params=params(56),
        name=name,
    )(*arrays)


def run_attention_forward(layer, place, tables, x_t, pieces, tile=256):
    first, cos, sin = tables
    wide, count = x_t.shape
    cols = pieces[0].shape[1]
    owners = place.shape[0] - 1
    return pl.pallas_call(
        functools.partial(attention_forward, layer=layer, tile=tile, count_pieces=len(pieces)),
        out_shape=(
            shape((count, wide), F32),
            shape((WIDTH, count), BF16),
            shape((KVW, count), BF16),
            shape((KVW, count), BF16),
            shape((WIDTH, count), BF16),
            shape((HEADS, count), F32),
            shape((2, wide), F32),
        ),
        in_specs=[SM] + [VM] * 4 + [AN] * len(pieces),
        out_specs=(VM,) * 7,
        scratch_shapes=[
            pltpu.VMEM((2, wide, cols), BF16),
            pltpu.VMEM((owners, EXTRA, cols), BF16),
            pltpu.VMEM((count, count), F32),
            pltpu.SemaphoreType.DMA((3 * owners,)),
        ],
        compiler_params=params(62),
        cost_estimate=cost(6),
        name="attention_forward",
    )(place, first, cos, sin, x_t, *pieces)


def run_attention_backward(layer, place, tables, x_t, gain, d_mid, g_ffn, saved, pieces, tile=256):
    first, cos, sin = tables
    wide, count = x_t.shape
    cols = pieces[0].shape[1]
    owners = place.shape[0] - 1
    padded = wide // owners + EXTRA
    return pl.pallas_call(
        functools.partial(attention_backward, layer=layer, tile=tile, count_pieces=len(pieces)),
        out_shape=(
            shape((wide, count), F32),
            shape((wide, count), BF16),
            shape((owners, padded, cols), BF16),
            shape((owners, padded, cols), BF16),
        ),
        in_specs=[SM] + [VM] * 12 + [AN] * len(pieces),
        out_specs=(VM, VM, AN, AN),
        scratch_shapes=[
            pltpu.VMEM((2, wide, cols), BF16),
            pltpu.VMEM((2, owners, padded, cols), BF16),
            pltpu.VMEM((count, count), F32),
            pltpu.VMEM((WIDTH, count), BF16),
            pltpu.VMEM((WIDTH, count), F32),
            pltpu.VMEM((KVW, count), F32),
            pltpu.VMEM((KVW, count), BF16),
            pltpu.SemaphoreType.DMA((2 * owners,)),
            pltpu.SemaphoreType.DMA((2,)),
        ],
        compiler_params=params(62),
        cost_estimate=cost(10),
        name="attention_backward",
    )(place, first, cos, sin, x_t, gain, d_mid, g_ffn, *saved, *pieces)


def run_attention_scores_backward(layer, place, tables, d_mid, saved, pieces, tile=256):
    first, cos, sin = tables
    count, wide = d_mid.shape
    cols = pieces[0].shape[1]
    owners = place.shape[0] - 1
    q, k, v, o, lse = saved
    return pl.pallas_call(
        functools.partial(attention_scores_backward, layer=layer, tile=tile, count_pieces=len(pieces)),
        out_shape=(shape((WIDTH + KVW, count), BF16), shape((KVW, count), BF16)),
        in_specs=[SM] + [VM] * 8 + [AN] * len(pieces),
        out_specs=(VM, VM),
        scratch_shapes=[
            pltpu.VMEM((2, wide, cols), BF16),
            pltpu.VMEM((count, count), F32),
            pltpu.VMEM((WIDTH, count), BF16),
            pltpu.VMEM((WIDTH, count), F32),
            pltpu.VMEM((KVW, count), F32),
            pltpu.SemaphoreType.DMA((2 * owners,)),
        ],
        compiler_params=params(56),
        cost_estimate=cost(7),
        name="attention_scores_backward",
    )(place, first, cos, sin, d_mid, q, k, v, lse, *pieces)


def run_attention_weights_backward(layer, place, x_t, gain, d_mid, g_ffn, saved, d_qk, d_v, pieces):
    wide, count = x_t.shape
    cols = pieces[0].shape[1]
    owners = place.shape[0] - 1
    padded = wide // owners + EXTRA
    return pl.pallas_call(
        functools.partial(attention_weights_backward, layer=layer, count_pieces=len(pieces)),
        out_shape=(
            shape((wide, count), F32),
            shape((wide, count), BF16),
            shape((owners, padded, cols), BF16),
            shape((owners, padded, cols), BF16),
        ),
        in_specs=[SM] + [VM] * 7 + [AN] * len(pieces),
        out_specs=(VM, VM, AN, AN),
        scratch_shapes=[
            pltpu.VMEM((2, wide, cols), BF16),
            pltpu.VMEM((2, owners, padded, cols), BF16),
            pltpu.SemaphoreType.DMA((2 * owners,)),
            pltpu.SemaphoreType.DMA((2,)),
        ],
        compiler_params=params(56),
        cost_estimate=cost(3),
        name="attention_weights_backward",
    )(place, x_t, gain, d_mid, g_ffn, saved[3], d_qk, d_v, *pieces)


def run_feed_forward(layer, place, mid, gain, pieces, dy_t=None, kept=(), block=768):
    backward = dy_t is not None
    forward = not kept
    count, wide = mid.shape
    owners = place.shape[0] - 1
    rows, cols = (pieces[0].shape[0] - EXTRA) // 2, pieces[0].shape[1]
    out_shape, out_specs = [], []
    scratch = [
        pltpu.VMEM((2, wide, 2 * cols), BF16),
        pltpu.VMEM((wide, 2 * cols), BF16),
        pltpu.SemaphoreType.DMA((8 * owners,)),
    ]
    if forward and backward:
        out_shape.append(shape((count, 2 * cols), BF16))
        out_specs.append(VM)
    elif forward:
        out_shape += [shape((wide, count), BF16)] + [shape((count, 2 * cols), BF16)] * 2
        out_specs += [VM] * 3
    scratch.append(pltpu.VMEM((count, block), BF16))
    if backward:
        out_shape += [
            shape((count, wide), F32),
            shape((1, wide), F32),
            shape((owners, 3 * rows, cols), BF16),
            shape((owners, 3 * rows, cols), BF16),
        ]
        out_specs += [VM, VM, AN, AN]
        scratch += [
            pltpu.VMEM((2, owners, 3 * rows, cols), BF16),
            pltpu.SemaphoreType.DMA((8,)),
            pltpu.VMEM((count, block), BF16),
            pltpu.VMEM((count, block), BF16),
        ]
    if kept:
        scratch += [pltpu.VMEM((2, count, 2 * cols), BF16), pltpu.SemaphoreType.DMA((4 * cols // block,))]
    flops = (7 if forward else 0) + (14 if backward else 0)
    extra = ([dy_t] if backward else []) + list(kept)
    return pl.pallas_call(
        functools.partial(
            feed_forward, layer=layer, forward=forward, backward=backward, block=block, count_pieces=len(pieces)
        ),
        out_shape=tuple(out_shape),
        in_specs=[SM, VM, VM] + [AN] * len(pieces) + [VM] * (len(extra) - len(kept)) + [AN] * len(kept),
        out_specs=tuple(out_specs),
        scratch_shapes=scratch,
        compiler_params=params(56 if kept else 62),
        cost_estimate=cost(flops),
        name="feed_forward",
    )(place, mid, gain, *pieces, *extra)


def run_feed_forward_result(layer, place, mid, hidden, pieces):
    count, wide = mid.shape
    owners = place.shape[0] - 1
    return pl.pallas_call(
        functools.partial(feed_forward_result, layer=layer, count_pieces=len(pieces)),
        out_shape=shape((wide, count), BF16),
        in_specs=[SM, VM, VM] + [AN] * len(pieces),
        out_specs=VM,
        scratch_shapes=[pltpu.VMEM((wide, hidden.shape[1]), BF16), pltpu.SemaphoreType.DMA((8 * owners,))],
        compiler_params=params(24),
        cost_estimate=cost(2),
        name="feed_forward_result",
    )(place, mid, hidden, *pieces)


def make_tables(lengths, count):
    ends = jnp.cumsum(lengths)
    starts = ends - lengths
    places = jnp.arange(count, dtype=jnp.int32)
    document = jnp.sum((places[:, None] >= ends[None, :]).astype(jnp.int32), axis=1)
    inside = document[:, None] == jnp.arange(lengths.shape[0], dtype=jnp.int32)[None, :]
    first = jnp.sum(jnp.where(inside, starts[None, :], 0), axis=1)
    position = (places - first).astype(F32)
    frequency = rope_base ** (-(jnp.arange(HALF, dtype=F32) * 2.0 / HEAD))
    angles = frequency[:, None] * position[None, :]
    return first[None, :], jnp.cos(angles), jnp.sin(angles)


def swap(value):
    return lax.ppermute(value, "section", [(0, 1), (1, 0)])


def give(value, target):
    return lax.ppermute(value, "section", [(1 - target, target)])


def exchange(value, axis, bit):
    count = lax.axis_size(axis)
    return lax.ppermute(value, axis, [(i, i ^ bit) for i in range(count)])


def mixed_exchange(value, even_bit, odd_bit):
    owners, replicas = lax.axis_size("fsdp"), lax.axis_size("dp")
    pairs = []
    for i in range(owners):
        for z in range(replicas):
            partner = i ^ (odd_bit if z % 2 else even_bit)
            pairs.append((i * replicas + z, partner * replicas + z))
    return lax.ppermute(value, ("fsdp", "dp"), pairs)


def paired():
    return lax.axis_size("fsdp") == 4 and lax.axis_size("dp") % 2 == 0


def piece_places():
    own = lax.axis_index("fsdp")
    if not paired():
        count = lax.axis_size("fsdp")
        return [own] + [(own + i) % count for i in range(1, count)]
    odd = lax.axis_index("dp") % 2
    near, far = jnp.where(odd == 1, own ^ 2, own ^ 1), jnp.where(odd == 1, own ^ 1, own ^ 2)
    return [own, near, own ^ 3, far]


def first_hop(value):
    if not paired():
        return lax.all_gather(value, "fsdp")
    return mixed_exchange(value, 1, 2)


def second_hop(near):
    if not paired():
        count = lax.axis_size("fsdp")
        own = lax.axis_index("fsdp")
        return [pick(near, (own + i) % count, 0) for i in range(1, count)]
    return [near, mixed_exchange(near, 2, 1), exchange(near, "dp", 1)]


def shared(pieces):
    return pieces + [swap(piece) for piece in pieces]


def tie(*values):
    return lax.optimization_barrier(values)


def pick(value, index, axis):
    return lax.dynamic_index_in_dim(value, index, axis, keepdims=False)


def total(left, right):
    return left + right


def split_first(place, ins, outs, cut):
    (keep, came), outs = ins, list(outs)
    y, x = place[1] // 2, place[1] % 2
    for by_x, low, high in ((True, 0, cut), (False, cut, keep.shape[1])):
        if low == high:
            continue
        hold, away = outs.pop(0), outs.pop(0)
        for i in range(2):
            for target, mine in ((hold, True), (away, False)):
                bit_x, bit_y = (x, y) if mine else (1 - x, 1 - y)
                block = 2 * i + bit_x if by_x else 2 * bit_y + i
                target[i] = total(keep[block, low:high], came[block, low:high])


def split_second(place, ins, outs, order):
    y, x = place[1] // 2, place[1] % 2
    for i, by_x in enumerate(order):
        hold, came, stay, away = ins[2 * i], ins[2 * i + 1], outs[2 * i], outs[2 * i + 1]
        bit = y if by_x else x
        stay[...] = total(hold[bit], came[bit])
        away[...] = total(hold[1 - bit], came[1 - bit])


def stack_sums(place, ins, outs):
    at = 0
    for i in range(0, len(ins), 2):
        rows = ins[i].shape[0]
        outs[0][at:at + rows, :] = total(ins[i][...], ins[i + 1][...])
        at += rows


def from_middle(place, ins, outs):
    z = place[place.shape[0] - 1]
    inner = (z == 1) | (z == 2)

    @pl.when(inner)
    def _():
        outs[0][...] = ins[0][...]

    @pl.when(jnp.logical_not(inner))
    def _():
        outs[0][...] = ins[1][...]


def work(place, *refs, steps):
    ins, outs = [], list(refs)
    for _, count_in, _ in steps:
        ins.append(outs[:count_in])
        outs = outs[count_in:]
    for (body, _, count_out), taken in zip(steps, ins):
        body(place, taken, outs[:count_out])
        outs = outs[count_out:]


def run_work(place, jobs, mib=24):
    ins = [value for job in jobs for value in job[1]]
    out = [shape(dims, BF16) for job in jobs for dims in job[2]]
    done = list(pl.pallas_call(
        functools.partial(work, steps=tuple((job[0], len(job[1]), len(job[2])) for job in jobs)),
        out_shape=tuple(out),
        in_specs=[SM] + [VM] * len(ins),
        out_specs=(VM,) * len(out),
        compiler_params=params(mib),
        name="work",
    )(place, *ins))
    for job in jobs:
        job[3](done[:len(job[2])])
        done = done[len(job[2]):]


def split_large(place, keep, came, hold_x, away_x, hold_y, away_y, left, right, sems_in, sems_out, *, cut):
    owners = keep.shape[0]
    y, x = place[1] // 2, place[1] % 2
    loads = [
        (start(keep.at[f], left.at[f], sems_in.at[2 * f]), start(came.at[f], right.at[f], sems_in.at[2 * f + 1]))
        for f in range(owners)
    ]
    stores = []
    for f in range(owners):
        for one in loads[f]:
            one.wait()
        left[f] = total(left[f], right[f])
        low, high = left.at[f, :cut], left.at[f, cut:]
        stores.append(either(x == f % 2, (low, hold_x.at[f // 2]), (low, away_x.at[f // 2]), None, sems_out.at[2 * f]))
        stores.append(
            either(y == f // 2, (high, hold_y.at[f % 2]), (high, away_y.at[f % 2]), None, sems_out.at[2 * f + 1])
        )
    for one in stores:
        one.wait()


def run_split_large(place, keep, came, cut):
    owners, rows, cols = keep.shape
    low, high = shape((2, cut, cols), BF16), shape((2, rows - cut, cols), BF16)
    return pl.pallas_call(
        functools.partial(split_large, cut=cut),
        out_shape=(low, low, high, high),
        in_specs=[SM, AN, AN],
        out_specs=(AN,) * 4,
        scratch_shapes=[
            pltpu.VMEM(keep.shape, BF16),
            pltpu.VMEM(keep.shape, BF16),
            pltpu.SemaphoreType.DMA((2 * owners,)),
            pltpu.SemaphoreType.DMA((2 * owners,)),
        ],
        compiler_params=params(56),
        name="split_large",
    )(place, keep, came)


class Sum:
    def __init__(self, keep, send, cut, pairs=False):
        self.hold, self.cut, self.pairs = [keep], cut, pairs
        self.chain = lax.axis_size("dp") == 4
        self.came = [swap(send)]
        rows = keep.shape[1]
        self.order = [by_x for by_x, some in ((True, cut > 0), (False, cut < rows)) if some]

    def split(self, second):
        def then(outs):
            self.hold = list(outs[::2])
            self.came = [
                exchange(value, "fsdp", 1 if by_x != second else 2) for value, by_x in zip(outs[1::2], self.order)
            ]
        return then

    def fsdp_first(self):
        _, rows, cols = self.hold[0].shape
        dims = [(2, self.cut if by_x else rows - self.cut, cols) for by_x in self.order for _ in range(2)]
        return functools.partial(split_first, cut=self.cut), self.hold + self.came, dims, self.split(False)

    def fsdp_first_large(self, place):
        self.split(False)(run_split_large(place, self.hold[0], self.came[0], self.cut))

    def fsdp_second(self):
        ins = [value for pair in zip(self.hold, self.came) for value in pair]
        dims = [value.shape[1:] for value in self.hold for _ in range(2)]
        return functools.partial(split_second, order=tuple(self.order)), ins, dims, self.split(True)

    def dp(self, hop):
        ins = [value for pair in zip(self.hold, self.came) for value in pair]
        dims = [(sum(value.shape[0] for value in self.hold), self.hold[0].shape[1])]

        def then(outs):
            value = outs[0]
            self.hold = [value]
            if not self.chain:
                self.came = [lax.psum(value, "dp") if hop == 0 else jnp.zeros_like(value)]
                if hop == 0:
                    self.hold = [jnp.zeros_like(value)]
            elif self.pairs:
                self.came = [exchange(value, "dp", 1 + hop)] if hop < 2 else []
            else:
                pairs = ([(0, 1), (3, 2)], [(1, 2), (2, 1)], [(1, 0), (2, 3)])[hop]
                self.came = [lax.ppermute(value, "dp", pairs)]

        return stack_sums, ins, dims, then

    def finish(self):
        def then(outs):
            self.hold, self.came = list(outs), []

        if not self.chain or self.pairs:
            return self.dp(2)[:3] + (then,)
        return from_middle, self.hold + self.came, [self.hold[0].shape], then


def choose(line, ff1, ff0, ff0_came, at1, at0, at0_came, ff_own, ff_send, at_own, at_send, *, chain):
    z = line[line.shape[0] - 1]
    inner = (z == 1) | (z == 2)
    for sec in range(2):
        targets = (ff_own, at_own, ff_send, at_send) if sec == 0 else (ff_send, at_send, ff_own, at_own)

        @pl.when(line[0] == sec)
        def _(targets=targets):
            if chain:

                @pl.when(inner)
                def _():
                    targets[0][...] = ff0[...]

                @pl.when(jnp.logical_not(inner))
                def _():
                    targets[0][...] = ff0_came[...]
            else:
                targets[0][...] = total(ff0[...], ff0_came[...])
            targets[1][...] = total(at0[...], at0_came[...])
            targets[2][...] = ff1[...]
            targets[3][...] = at1[...]


def run_choose(line, ff1, ff0, at1, at0):
    ff, at = shape(ff1.shape, BF16), shape(at1.shape, BF16)
    return pl.pallas_call(
        functools.partial(choose, chain=ff0.chain),
        out_shape=(ff, ff, at, at),
        in_specs=[SM] + [VM] * 6,
        out_specs=(VM,) * 4,
        compiler_params=params(24),
        name="choose",
    )(line, ff1, ff0.hold[0], ff0.came[0], at1, at0.hold[0], at0.came[0])


def unpack(place, ff_own, ff_given, at_own, at_given, gate, up, down, wq, wk, wv, wo, gain_attn, gain_ffn):
    rows = gate.shape[0]
    narrow = down.shape[1]

    def emit(half, part, value):
        wide = (gate, up)[half]
        for i in range(2):
            wide[:, 2 * i * narrow:(2 * i + 2) * narrow] = part[i * rows:(i + 1) * rows, :].astype(F32)
        top = 2 * half * rows
        down[top:top + rows, :] = part[2 * rows:, :narrow].astype(F32)
        down[top + rows:top + 2 * rows, :] = part[2 * rows:, narrow:].astype(F32)
        left, right = ((wq, wk), (wo, wv))[half]
        left[...] = value[:rows, :WIDTH].astype(F32)
        right[...] = value[:rows, WIDTH:].astype(F32)
        if half == 0:
            gains = value[rows:, :rows].astype(F32)
            gain_attn[...] = gains[:1]
            gain_ffn[...] = gains[1:2]

    for sec in range(2):

        @pl.when(place[0] == sec)
        def _(sec=sec):
            emit(sec, ff_own, at_own)
            emit(1 - sec, ff_given, at_given)


def run_unpack(place, ff_own, ff_given, at_own, at_given):
    rows, cols = ff_own.shape[0] // 3, ff_own.shape[1]
    return pl.pallas_call(
        unpack,
        out_shape=(
            shape((rows, 2 * cols), F32),
            shape((rows, 2 * cols), F32),
            shape((4 * rows, cols // 2), F32),
            shape((rows, WIDTH), F32),
            shape((rows, KVW), F32),
            shape((rows, KVW), F32),
            shape((rows, WIDTH), F32),
            shape((1, rows), F32),
            shape((1, rows), F32),
        ),
        in_specs=[SM] + [VM] * 4,
        out_specs=(VM,) * 9,
        compiler_params=params(32),
        name="unpack",
    )(place, ff_own, ff_given, at_own, at_given)


def local(
    tokens,
    cotangent,
    doc_lengths,
    w_query,
    w_key,
    w_value,
    w_out,
    w_gate,
    w_up,
    w_down,
    gain_attn,
    gain_ffn,
):
    sec = lax.axis_index("section")
    first_section = sec == 0
    count = tokens.shape[2]
    place = jnp.stack([jnp.asarray(i, jnp.int32) for i in [sec] + piece_places()])
    line = jnp.concatenate([place, lax.axis_index("dp").astype(jnp.int32)[None]])
    rows, cols = w_query.shape[1], w_query.shape[2] + w_key.shape[2]
    own_at, rest_at = run_pack(
        pack_first, "pack_first", (2 * rows + EXTRA, cols),
        w_query[0], w_key[0], w_value[0], w_out[0], gain_attn, gain_ffn, w_down[0].T,
    )
    w_gate, own_at, rest_at = tie(w_gate, own_at, rest_at)
    own_ff, rest_ff = run_pack(pack_second, "pack_second", (2 * rows, cols), w_gate[0], w_up[0])

    def own_pieces(own, rest):
        came_own, came_rest = swap(rest), swap(own)
        home = [own, came_own, rest, came_rest]
        return home, jnp.where(first_section, own, came_own), jnp.where(first_section, came_own, own)

    at_home, at_zero, at_one = own_pieces(own_at, rest_at)
    ff_home, ff_zero, ff_one = own_pieces(own_ff, rest_ff)
    tables = make_tables(pick(doc_lengths[0], sec, 0), count)
    at_zero, tokens, cotangent = tie(at_zero, tokens, cotangent)
    x0 = jnp.swapaxes(pick(tokens[0], sec, 0), 0, 1)
    dy1 = jnp.swapaxes(pick(cotangent[0], sec, 0), 0, 1)

    near_at0 = first_hop(at_zero)
    near_ff0 = first_hop(ff_zero)
    near_at0, ff_one, x0, dy1, *tables = tie(near_at0, ff_one, x0, dy1, *tables)
    at0 = second_hop(near_at0)
    near_ff0, at_one, ff_one, *at0 = tie(near_ff0, at_one, ff_one, *at0)
    ff0 = second_hop(near_ff0)
    near_at1 = first_hop(at_one)
    near_ff1 = first_hop(ff_one)
    at0 = shared(at0)
    mid0, *saved0, gains0 = run_attention_forward(0, place, tables, x0, at_home + at0)
    mid0, near_at1, *ff0 = tie(mid0, near_at1, *ff0)

    ff0 = shared(ff0)
    at1 = second_hop(near_at1)
    y0, gate0, up0 = run_feed_forward(0, place, mid0, gains0, at_home + at0 + ff_home + ff0)
    y0, near_ff1, *at1 = tie(y0, near_ff1, *at1)

    at1 = shared(at1)
    ff1 = second_hop(near_ff1)
    mid1, *saved1, gains1 = run_attention_forward(1, place, tables, y0, at_home + at1)
    mid1, *ff1 = tie(mid1, *ff1)
    ff1 = shared(ff1)
    hidden1, d_mid1, g_ffn1, ff_keep1, ff_send1 = run_feed_forward(
        1, place, mid1, gains1, at_home + at1 + ff_home + ff1, dy_t=dy1
    )

    sums = []

    def after(waited, *others):
        cells = [(one.came, i) for one, i in waited]
        for one in sums:
            cells += [(one.hold, i) for i in range(len(one.hold))]
        held = list(tie(*others, *[array[i] for array, i in cells]))
        for (array, i), value in zip(cells, held[len(others):]):
            array[i] = value
        return held[:len(others)]

    def both_rows(own0, own1):
        back = swap(jnp.where(first_section, own1, own0))
        both = jnp.where(first_section, jnp.stack([own0, back]), jnp.stack([back, own1]))
        return jnp.swapaxes(both, 1, 2)[None, None]

    ff_cut, at_cut = ff_keep1.shape[1] // 32 * 16, (rows + EXTRA) // 32 * 16
    f1 = Sum(ff_keep1, ff_send1, ff_cut)
    sums.append(f1)
    dx1, dy0, at_keep1, at_send1 = run_attention_backward(
        1, place, tables, y0, gains1, d_mid1, g_ffn1, saved1, at_home + at1
    )
    dy0, at_keep1, at_send1 = after([(f1, 0)], dy0, at_keep1, at_send1)

    f1.fsdp_first_large(place)
    a1 = Sum(at_keep1, at_send1, at_cut)
    sums.append(a1)
    (dy0,) = after([], dy0)
    d_mid0, g_ffn0, ff_keep0, ff_send0 = run_feed_forward(
        0, place, mid0, gains0, at_home + at0 + ff_home + ff0, dy_t=dy0, kept=(gate0, up0)
    )
    d_mid0, ff_keep0, ff_send0 = after([(f1, 0), (f1, 1), (a1, 0)], d_mid0, ff_keep0, ff_send0)

    f0 = Sum(ff_keep0, ff_send0, ff_cut)
    sums.append(f0)
    run_work(line, [f1.fsdp_second(), a1.fsdp_first()])
    (d_mid0,) = after([], d_mid0)
    d_qk0, d_v0 = run_attention_scores_backward(0, place, tables, d_mid0, saved0, at_home + at0)
    d_qk0, d_v0 = after([(f0, 0), (f1, 0), (f1, 1), (a1, 0), (a1, 1)], d_qk0, d_v0)

    f0.fsdp_first_large(place)
    after([])
    run_work(line, [f1.dp(0), a1.fsdp_second()])
    (d_qk0,) = after([], d_qk0)
    dx0, _, at_keep0, at_send0 = run_attention_weights_backward(
        0, place, x0, gains0, d_mid0, g_ffn0, saved0, d_qk0, d_v0, at_home + at0
    )
    at_send0, at_keep0 = after([(f0, 0), (f0, 1), (f1, 0), (a1, 0), (a1, 1)], at_send0, at_keep0)

    a0 = Sum(at_keep0, at_send0, at_cut, True)
    sums.append(a0)
    run_work(line, [f0.fsdp_second(), f1.dp(1)])
    after([(a0, 0)])
    run_work(line, [a0.fsdp_first(), a1.dp(0)])
    dx0, dx1, hidden1 = after([(f0, 0), (f0, 1), (f1, 0), (a1, 0), (a0, 0), (a0, 1)], dx0, dx1, hidden1)

    run_work(line, [f0.dp(0), f1.dp(2), a1.dp(1), a0.fsdp_second()])
    y1 = run_feed_forward_result(1, place, mid1, hidden1, at_home + at1)
    dx0, dx1, y1 = after([(f0, 0), (f1, 0), (a1, 0), (a0, 0), (a0, 1)], dx0, dx1, y1)

    run_work(line, [f0.dp(1), a1.dp(2), a0.dp(0), f1.finish()])
    dx0, dx1 = after([], dx0, dx1)
    grad = both_rows(dx0, dx1)
    (grad,) = after([(f0, 0), (a1, 0), (a0, 0)], grad)

    run_work(line, [f0.dp(2), a0.dp(1), a1.finish()])
    y0, y1 = after([], y0, y1)
    out = both_rows(y0, y1)
    (out,) = after([(f0, 0), (a0, 0)], out)

    ff_own, ff_send, at_own, at_send = run_choose(line, f1.hold[0], f0, a1.hold[0], a0)
    gate, up, down, wq, wk, wv, wo, gain_attn, gain_ffn = run_unpack(place, ff_own, swap(ff_send), at_own, swap(at_send))

    return (
        out,
        grad,
        wq[None],
        wk[None],
        wv[None],
        wo[None],
        gate[None],
        up[None],
        down.T[None],
        gain_attn,
        gain_ffn,
    )


def solution(mesh):
    whole = P(("fsdp", "dp"), None, None, None)
    weight = P("section", "fsdp", None)
    gain = P("section", "fsdp")
    rows = P("section", ("fsdp", "dp"), None, None, None)
    in_specs = (whole, whole, P(("fsdp", "dp"), None, None)) + (weight,) * 7 + (gain,) * 2
    out_specs = (rows, rows) + (weight,) * 7 + (gain,) * 2
    return jax.shard_map(local, mesh=mesh, in_specs=in_specs, out_specs=out_specs, check_vma=False)
```

```python
import functools
import jax
import jax.numpy as jnp
from jax import lax
from jax.experimental import pallas as pl
from jax.experimental.pallas import tpu as pltpu
from jax.sharding import PartitionSpec as P

HEADS = 9
KV_HEADS = 3
GROUP = HEADS // KV_HEADS
HEAD = 64
HALF = HEAD // 2
WIDTH = HEADS * HEAD
KVW = KV_HEADS * HEAD

epsilon = 1e-05
rope_base = 100000.0
masked_score = -1e30
SCALE = HEAD ** (-0.5)
EXTRA = 16
F32 = jnp.float32
BF16 = jnp.bfloat16


def nn(left, right):
    return lax.dot_general(left, right, (((1,), (0,)), ((), ())), preferred_element_type=F32)


def nt(left, right):
    return lax.dot_general(left, right, (((1,), (1,)), ((), ())), preferred_element_type=F32)


def inverse_root(values):
    return lax.rsqrt(jnp.mean(values * values, axis=-1, keepdims=True) + epsilon)


def norm_back(values, inv_root, gain, upstream):
    gain_grad = jnp.sum(upstream * values * inv_root, axis=0, keepdims=True)
    scaled = upstream * gain
    dot = jnp.mean(scaled * values, axis=-1, keepdims=True)
    return inv_root * scaled - values * (inv_root * inv_root * inv_root * dot), gain_grad


def sigmoid(values):
    return 0.5 * jnp.tanh(0.5 * values) + 0.5


def pack_first(wq, wk, wv, wo, gain_attn, gain_ffn, down, own, rest):
    rows, cols = wq.shape[0], own.shape[1]
    down_cols = down.shape[1]
    half_down = down.shape[0] // 2
    top = rows + EXTRA

    def write(target, half):
        left, right = ((wq, wk), (wo, wv))[half]
        target[:rows, :] = jnp.concatenate([left[...], right[...]], axis=1)
        target[rows:top, :] = jnp.zeros((EXTRA, cols), BF16)
        target[rows:top, :rows] = jnp.concatenate(
            [gain_attn[...].astype(F32), gain_ffn[...].astype(F32), jnp.zeros((EXTRA - 2, rows), F32)], axis=0
        ).astype(BF16)
        for i in range(2):
            at = half * half_down + i * rows
            target[top:, i * down_cols:(i + 1) * down_cols] = down[at:at + rows, :]

    for number in range(2):

        @pl.when(lax.axis_index("section") == number)
        def _(number=number):
            write(own, number)
            write(rest, 1 - number)


def pack_second(gate, up, own, rest):
    rows, cols = gate.shape[0], own.shape[1]

    def write(target, half):
        wide = (gate, up)[half]
        target[:rows, :] = wide[:, :cols]
        target[rows:, :] = wide[:, cols:]

    for number in range(2):

        @pl.when(lax.axis_index("section") == number)
        def _(number=number):
            write(own, number)
            write(rest, 1 - number)


def either(condition, first, second, target, sem):
    first, second = ((first, target), (second, target)) if target is not None else (first, second)

    @pl.when(condition)
    def _():
        pltpu.make_async_copy(*first, sem).start()

    @pl.when(jnp.logical_not(condition))
    def _():
        pltpu.make_async_copy(*second, sem).start()

    return pltpu.make_async_copy(*first, sem)


def start(source, target, sem):
    one = pltpu.make_async_copy(source, target, sem)
    one.start()
    return one


def sides(place, layer, pieces):
    sec = place[0]
    slots = place.shape[0] - 1
    found = []
    for number, (half, rest) in enumerate(((sec, pieces[4:3 + slots]), (1 - sec, pieces[3 + slots:]))):
        found.append((half, place[1], pieces[2 * number], pieces[2 * number + 1]))
        for slot, piece in enumerate(rest):
            found.append((half, place[2 + slot], piece, None))
    return found


def load_attention(place, layer, pieces, weights, gains, sems):
    rows = (pieces[0].shape[0] - EXTRA) // 2
    home = place[0] == layer
    waits = []
    slots = place.shape[0] - 1
    for number, (half, owner, source, other) in enumerate(sides(place, layer, pieces)):
        target = weights.at[half, pl.ds(pl.multiple_of(owner * rows, 16), rows), :]
        window = slice(0, rows)
        if other is None:
            waits.append(start(source.at[window], target, sems.at[number]))
        else:
            waits.append(either(home, source.at[window], other.at[window], target, sems.at[number]))
        if number < slots and gains is not None:
            window, target, sem = slice(rows, rows + EXTRA), gains.at[owner], sems.at[2 * slots + number]
            if other is None:
                waits.append(start(source.at[window], target, sem))
            else:
                waits.append(either(home, source.at[window], other.at[window], target, sem))
    return waits


def load_gate_up(place, layer, pieces, gate_up, sems):
    rows, cols = pieces[0].shape[0] // 2, pieces[0].shape[1]
    home = place[0] == layer
    waits = []
    for part in range(2):
        waits.append([])
        for number, (half, owner, source, other) in enumerate(sides(place, layer, pieces)):
            window = slice(part * rows, (part + 1) * rows)
            target = gate_up.at[half, pl.ds(pl.multiple_of(owner * rows, 16), rows), part * cols:(part + 1) * cols]
            sem = sems.at[4 * number + part]
            if other is None:
                waits[part].append(start(source.at[window], target, sem))
            else:
                waits[part].append(either(home, source.at[window], other.at[window], target, sem))
    return waits


def load_down(place, layer, pieces, down, sems, first_sem):
    rows, narrow = (pieces[0].shape[0] - EXTRA) // 2, pieces[0].shape[1] // 2
    home = place[0] == layer
    waits = []
    for number, (half, owner, source, other) in enumerate(sides(place, layer, pieces)):
        for i in range(2):
            window = (slice(rows + EXTRA, 2 * rows + EXTRA), slice(i * narrow, (i + 1) * narrow))
            top = pl.multiple_of(half * (2 * rows) + i * rows, 16)
            target = down.at[pl.ds(top, rows), pl.ds(pl.multiple_of(owner * narrow, 128), narrow)]
            sem = sems.at[4 * number + first_sem + i]
            if other is None:
                waits.append(start(source.at[window], target, sem))
            else:
                waits.append(either(home, source.at[window], other.at[window], target, sem))
    return waits


def fill_bias(first, bias):
    count = bias.shape[0]
    key = lax.broadcasted_iota(jnp.int32, (count, count), 0)
    query = lax.broadcasted_iota(jnp.int32, (count, count), 1)
    allowed = (key >= first[...]) & (key <= query)
    bias[...] = jnp.where(allowed, 0.0, masked_score).astype(F32)


def attention_forward(place, first, cos, sin, x_t, *rest, layer, tile, count_pieces):
    pieces = rest[:count_pieces]
    mid, q_out, k_out, v_out, o_out, lse_out, gain_out, weights, gain_parts, bias, sems = rest[count_pieces:]
    owners = gain_parts.shape[0]
    rows = weights.shape[1] // owners
    waits = load_attention(place, layer, pieces, weights, gain_parts, sems)
    count = x_t.shape[1]
    values = x_t[...].T.astype(F32)
    scaled = values * inverse_root(values)
    fill_bias(first, bias)
    for one in waits:
        one.wait()
    gain = jnp.concatenate([gain_parts[f][:2, :rows].astype(F32) for f in range(owners)], axis=1)
    gain_out[...] = gain
    normed = (scaled * gain[:1]).astype(BF16)
    qk = nt(weights[0].T, normed)
    v_out[...] = nt(weights[1, :, WIDTH:].T, normed).astype(BF16)
    c, s = cos[...], sin[...]

    def turned(part):
        low, high = part[:HALF], part[HALF:]
        return jnp.concatenate([low * c - high * s, high * c + low * s], axis=0)

    for head in range(HEADS):
        span = slice(head * HEAD, (head + 1) * HEAD)
        q_out[span, :] = (turned(qk[span]) * SCALE).astype(BF16)
    for j in range(KV_HEADS):
        at = WIDTH + j * HEAD
        k_out[j * HEAD:(j + 1) * HEAD, :] = turned(qk[at:at + HEAD]).astype(BF16)
    for j in range(KV_HEADS):
        keys = k_out[j * HEAD:(j + 1) * HEAD, :].T
        vals = v_out[j * HEAD:(j + 1) * HEAD, :]
        for g in range(GROUP):
            head = j * GROUP + g
            span = slice(head * HEAD, (head + 1) * HEAD)
            for at in range(0, count, tile):
                end = at + tile
                scores = nn(keys[:end], q_out[span, at:end]) + bias[:end, at:end]
                top = jnp.max(scores, axis=0, keepdims=True)
                power = jnp.exp(scores - top)
                total = jnp.sum(power, axis=0, keepdims=True)
                mixed = nn(vals[:, :end], power.astype(BF16))
                o_out[span, at:end] = (mixed / total).astype(BF16)
                lse_out[head:head + 1, at:end] = top + jnp.log(total)
    mid[...] = values + nn(o_out[...].T, weights[1, :, :WIDTH])


def attention_backward(place, first, cos, sin, x_t, gain, d_mid, g_ffn, q, k, v, o, lse, *rest, layer, tile, count_pieces):
    pieces = rest[:count_pieces]
    dx, dx_low, keep, send, weights, grads, bias, g_out, d_q, d_k, d_v, sems, sems_out = rest[count_pieces:]
    owners = grads.shape[1]
    rows = weights.shape[1] // owners
    sec = place[0]
    waits = load_attention(place, layer, pieces, weights, None, sems)
    count = x_t.shape[1]
    g_mid = d_mid[...].astype(BF16)
    fill_bias(first, bias)
    for one in waits:
        one.wait()
    g_out[...] = nt(weights[1, :, :WIDTH], g_mid).astype(BF16)

    def store(side, columns, value):
        for owner in range(owners):
            grads[side, owner, :rows, columns] = value[owner * rows:(owner + 1) * rows].astype(BF16)

    store(1, slice(0, WIDTH), nn(o[...], g_mid))
    c, s = cos[...], sin[...]

    def turned_back(part):
        low, high = part[:HALF], part[HALF:]
        return jnp.concatenate([low * c + high * s, high * c - low * s], axis=0)

    for j in range(KV_HEADS):
        own = slice(j * HEAD, (j + 1) * HEAD)
        keys_t = k[own, :]
        keys = keys_t.T
        vals = v[own, :].T
        k_sum = [jnp.zeros((HEAD, tile), F32) for _ in range(count // tile)]
        v_sum = [jnp.zeros((HEAD, tile), F32) for _ in range(count // tile)]
        for g in range(GROUP):
            head = j * GROUP + g
            span = slice(head * HEAD, (head + 1) * HEAD)
            for at in range(0, count, tile):
                end = at + tile
                q_part = q[span, at:end]
                g_part = g_out[span, at:end]
                power = jnp.exp(nn(keys[:end], q_part) + bias[:end, at:end] - lse[head:head + 1, at:end])
                d_prob = nn(vals[:end], g_part)
                delta = jnp.sum(power * d_prob, axis=0, keepdims=True)
                d_score = (power * (d_prob - delta)).astype(BF16)
                power = power.astype(BF16)
                v_add = nt(g_part, power)
                k_add = nt(q_part, d_score)
                for i in range(end // tile):
                    v_sum[i] = v_sum[i] + v_add[:, i * tile:(i + 1) * tile]
                    k_sum[i] = k_sum[i] + k_add[:, i * tile:(i + 1) * tile]
                d_q[span, at:end] = nn(keys_t[:, :end], d_score) * SCALE
        d_k[own, :] = jnp.concatenate(k_sum, axis=1)
        d_v[own, :] = jnp.concatenate(v_sum, axis=1).astype(BF16)
    turned = [turned_back(d_q[h * HEAD:(h + 1) * HEAD, :]).astype(BF16) for h in range(HEADS)]
    turned += [turned_back(d_k[h * HEAD:(h + 1) * HEAD, :]).astype(BF16) for h in range(KV_HEADS)]
    d_qk = jnp.concatenate(turned, axis=0)
    values = x_t[...].T.astype(F32)
    inv = inverse_root(values)
    attn_gain = gain[:1, :]
    normed_t = (values * inv * attn_gain).astype(BF16).T
    store(0, slice(None), nt(normed_t, d_qk))
    store(1, slice(WIDTH, None), nt(normed_t, d_v[...]))
    d_normed = (nn(weights[0], d_qk) + nn(weights[1, :, WIDTH:], d_v[...])).T
    back, gain_grad = norm_back(values, inv, attn_gain, d_normed)
    for owner in range(owners):
        span = slice(owner * rows, (owner + 1) * rows)
        both = jnp.concatenate([gain_grad[:, span], g_ffn[:, span]], axis=0)
        grads[:, owner, rows:, :] = jnp.zeros((2, EXTRA, grads.shape[3]), BF16)
        padded = jnp.concatenate([both, jnp.zeros((EXTRA - 2, rows), F32)], axis=0)
        grads[0, owner, rows:, :rows] = padded.astype(BF16)
    out = [start(grads.at[1 - sec], send, sems_out.at[0]), start(grads.at[sec], keep, sems_out.at[1])]
    total = (d_mid[...] + back).T
    dx[...] = total
    dx_low[...] = total.astype(BF16)
    for one in out:
        one.wait()


def attention_scores_backward(place, first, cos, sin, d_mid, q, k, v, lse, *rest, layer, tile, count_pieces):
    pieces = rest[:count_pieces]
    d_qk, d_v, weights, bias, g_out, d_q, d_k, sems = rest[count_pieces:]
    waits = load_attention(place, layer, pieces, weights, None, sems)
    count = d_mid.shape[0]
    g_mid = d_mid[...].astype(BF16)
    fill_bias(first, bias)
    for one in waits:
        one.wait()
    g_out[...] = nt(weights[1, :, :WIDTH], g_mid).astype(BF16)
    c, s = cos[...], sin[...]

    def turned_back(part):
        low, high = part[:HALF], part[HALF:]
        return jnp.concatenate([low * c + high * s, high * c - low * s], axis=0)

    for j in range(KV_HEADS):
        own = slice(j * HEAD, (j + 1) * HEAD)
        keys_t = k[own, :]
        keys = keys_t.T
        vals = v[own, :].T
        k_sum = [jnp.zeros((HEAD, tile), F32) for _ in range(count // tile)]
        v_sum = [jnp.zeros((HEAD, tile), F32) for _ in range(count // tile)]
        for g in range(GROUP):
            head = j * GROUP + g
            span = slice(head * HEAD, (head + 1) * HEAD)
            for at in range(0, count, tile):
                end = at + tile
                q_part = q[span, at:end]
                g_part = g_out[span, at:end]
                power = jnp.exp(nn(keys[:end], q_part) + bias[:end, at:end] - lse[head:head + 1, at:end])
                d_prob = nn(vals[:end], g_part)
                delta = jnp.sum(power * d_prob, axis=0, keepdims=True)
                d_score = (power * (d_prob - delta)).astype(BF16)
                power = power.astype(BF16)
                v_add = nt(g_part, power)
                k_add = nt(q_part, d_score)
                for i in range(end // tile):
                    v_sum[i] = v_sum[i] + v_add[:, i * tile:(i + 1) * tile]
                    k_sum[i] = k_sum[i] + k_add[:, i * tile:(i + 1) * tile]
                d_q[span, at:end] = nn(keys_t[:, :end], d_score) * SCALE
        d_k[own, :] = jnp.concatenate(k_sum, axis=1)
        d_v[own, :] = jnp.concatenate(v_sum, axis=1).astype(BF16)
    for h in range(HEADS):
        d_qk[h * HEAD:(h + 1) * HEAD, :] = turned_back(d_q[h * HEAD:(h + 1) * HEAD, :]).astype(BF16)
    for h in range(KV_HEADS):
        d_qk[WIDTH + h * HEAD:WIDTH + (h + 1) * HEAD, :] = turned_back(d_k[h * HEAD:(h + 1) * HEAD, :]).astype(BF16)


def attention_weights_backward(place, x_t, gain, d_mid, g_ffn, o, d_qk, d_v, *rest, layer, count_pieces):
    pieces = rest[:count_pieces]
    dx, dx_low, keep, send, weights, grads, sems, sems_out = rest[count_pieces:]
    owners = grads.shape[1]
    rows = weights.shape[1] // owners
    sec = place[0]
    waits = load_attention(place, layer, pieces, weights, None, sems)

    def store(side, columns, value):
        for owner in range(owners):
            grads[side, owner, :rows, columns] = value[owner * rows:(owner + 1) * rows].astype(BF16)

    store(1, slice(0, WIDTH), nn(o[...], d_mid[...].astype(BF16)))
    values = x_t[...].T.astype(F32)
    inv = inverse_root(values)
    attn_gain = gain[:1, :]
    normed_t = (values * inv * attn_gain).astype(BF16).T
    store(0, slice(None), nt(normed_t, d_qk[...]))
    store(1, slice(WIDTH, None), nt(normed_t, d_v[...]))
    for one in waits:
        one.wait()
    d_normed = (nn(weights[0], d_qk[...]) + nn(weights[1, :, WIDTH:], d_v[...])).T
    back, gain_grad = norm_back(values, inv, attn_gain, d_normed)
    for owner in range(owners):
        span = slice(owner * rows, (owner + 1) * rows)
        both = jnp.concatenate([gain_grad[:, span], g_ffn[:, span]], axis=0)
        grads[:, owner, rows:, :] = jnp.zeros((2, EXTRA, grads.shape[3]), BF16)
        padded = jnp.concatenate([both, jnp.zeros((EXTRA - 2, rows), F32)], axis=0)
        grads[0, owner, rows:, :rows] = padded.astype(BF16)
    out = [start(grads.at[1 - sec], send, sems_out.at[0]), start(grads.at[sec], keep, sems_out.at[1])]
    total = (d_mid[...] + back).T
    dx[...] = total
    dx_low[...] = total.astype(BF16)
    for one in out:
        one.wait()


def feed_forward(place, mid, gain, *rest, layer, forward, backward, block, count_pieces):
    pieces = rest[:count_pieces]
    rest = list(rest[count_pieces:])
    take = lambda: rest.pop(0)
    dy_t = take() if backward else None
    kept = (take(), take()) if backward and not forward else None
    y_t = take() if forward and not backward else None
    hidden_out = take() if forward and backward else None
    keeping = (take(), take()) if forward and not backward else None
    if backward:
        d_mid, d_gain, keep, send = take(), take(), take(), take()
    gate_up, down, sems = take(), take(), take()
    middle = take()
    if backward:
        grads, sems_out, gate_back, up_back = take(), take(), take(), take()
    sec = place[0]
    first_count = len(pieces) // 2
    if kept is None:
        early = load_gate_up(place, layer, pieces[first_count:], gate_up, sems)
        late = load_down(place, layer, pieces[:first_count], down, sems, 2)
    else:
        late = load_down(place, layer, pieces[:first_count], down, sems, 2)
        kept_here, kept_sems = take(), take()
        kept_waits = []
        for number, at in enumerate(range(0, down.shape[1], block)):
            for i in range(2):
                span = slice(at, at + block)
                kept_waits.append(start(kept[i].at[:, span], kept_here.at[i, :, span], kept_sems.at[2 * number + i]))
        early = load_gate_up(place, layer, pieces[first_count:], gate_up, sems)
    values = mid[...]
    inv = inverse_root(values)
    ffn_gain = gain[1:, :]
    normed = (values * inv * ffn_gain).astype(BF16)
    if backward:
        normed_t = normed.T
        dy = dy_t[...].T
        rows = grads.shape[2] // 3
        owners = grads.shape[1]
    if kept is not None:
        for one in late:
            one.wait()
    units = down.shape[1]
    result, d_normed = None, None
    out = []
    for number, at in enumerate(range(0, units, block)):
        span = slice(at, at + block)
        if kept is None:
            for one in early[number]:
                one.wait()
            gate, up = nn(normed, gate_up[0, :, span]), nn(normed, gate_up[1, :, span])
        else:
            for one in kept_waits[2 * number:2 * number + 2]:
                one.wait()
            gate, up = kept_here[0, :, span], kept_here[1, :, span]
        if keeping is not None:
            keeping[0][:, span] = gate.astype(BF16)
            keeping[1][:, span] = up.astype(BF16)
        if number == 0 and kept is None:
            for one in late:
                one.wait()
        if backward:
            d_hidden = nn(dy, down[:, span])
        for at_column in range(0, block, 128):
            strip = slice(at_column, at_column + 128)
            g, u = gate[:, strip].astype(F32), up[:, strip].astype(F32)
            sg = sigmoid(g)
            swish = g * sg
            if hidden_out is None:
                middle[:, strip] = (swish * u).astype(BF16)
            else:
                hidden_out[:, at + at_column:at + at_column + 128] = (swish * u).astype(BF16)
            if backward:
                d = d_hidden[:, strip]
                gate_back[:, strip] = (d * u * (sg * (1.0 + g * (1.0 - sg)))).astype(BF16)
                up_back[:, strip] = (d * swish).astype(BF16)
        hidden = middle[...] if hidden_out is None else hidden_out[:, span]
        if y_t is not None:
            part = nt(hidden, down[:, span])
            result = part if result is None else result + part
        if backward:
            g_gate, g_up = gate_back[...], up_back[...]
            for half, grad in ((0, g_gate), (1, g_up)):
                value = nn(normed_t, grad).astype(BF16)
                for owner in range(owners):
                    grads[half, owner, number * rows:(number + 1) * rows, :] = value[owner * rows:(owner + 1) * rows]
            value = nn(dy_t[...], hidden).astype(BF16)
            narrow = block // 2
            for i in range(2):
                for half in range(2):
                    for k in range(2):
                        top = (2 * half + k) * rows
                        grads[half, 2 * number + i, 2 * rows:, k * narrow:(k + 1) * narrow] = value[
                            top:top + rows, i * narrow:(i + 1) * narrow
                        ]
            for side, target in ((1 - sec, send), (sec, keep)):
                for window in (
                    (slice(None), slice(number * rows, (number + 1) * rows)),
                    (slice(2 * number, 2 * number + 2), slice(2 * rows, 3 * rows)),
                ):
                    out.append(start(grads.at[(side,) + window], target.at[window], sems_out.at[len(out)]))
            if kept is not None:
                for one in early[number]:
                    one.wait()
            part = nt(g_gate, gate_up[0, :, span]) + nt(g_up, gate_up[1, :, span])
            d_normed = part if d_normed is None else d_normed + part
    if y_t is not None:
        y_t[...] = (values + result).astype(BF16).T
    if backward:
        back, gain_grad = norm_back(values, inv, ffn_gain, d_normed)
        d_gain[...] = gain_grad
        d_mid[...] = dy.astype(F32) + back
        for one in out:
            one.wait()


def feed_forward_result(place, mid, hidden, *rest, layer, count_pieces):
    pieces = rest[:count_pieces]
    y_t, down, sems = rest[count_pieces:]
    waits = load_down(place, layer, pieces, down, sems, 0)
    for one in waits:
        one.wait()
    y_t[...] = (mid[...] + nt(hidden[...], down[...])).astype(BF16).T


VM = pl.BlockSpec(memory_space=pltpu.VMEM)
SM = pl.BlockSpec(memory_space=pltpu.SMEM)
AN = pl.BlockSpec(memory_space=pl.ANY)


def params(mib):
    return pltpu.CompilerParams(vmem_limit_bytes=mib * 1024 * 1024)


def shape(dims, kind):
    return jax.ShapeDtypeStruct(dims, kind)


def cost(gigaflops):
    return pl.CostEstimate(flops=int(gigaflops * 10**6), bytes_accessed=10**4, transcendentals=0)


def run_pack(kernel, name, dims, *arrays):
    return pl.pallas_call(
        kernel,
        out_shape=(shape(dims, BF16),) * 2,
        in_specs=[VM] * len(arrays),
        out_specs=(VM,) * 2,
        compiler_params=params(56),
        name=name,
    )(*arrays)


def run_attention_forward(layer, place, tables, x_t, pieces, tile=256):
    first, cos, sin = tables
    wide, count = x_t.shape
    cols = pieces[0].shape[1]
    owners = place.shape[0] - 1
    return pl.pallas_call(
        functools.partial(attention_forward, layer=layer, tile=tile, count_pieces=len(pieces)),
        out_shape=(
            shape((count, wide), F32),
            shape((WIDTH, count), BF16),
            shape((KVW, count), BF16),
            shape((KVW, count), BF16),
            shape((WIDTH, count), BF16),
            shape((HEADS, count), F32),
            shape((2, wide), F32),
        ),
        in_specs=[SM] + [VM] * 4 + [AN] * len(pieces),
        out_specs=(VM,) * 7,
        scratch_shapes=[
            pltpu.VMEM((2, wide, cols), BF16),
            pltpu.VMEM((owners, EXTRA, cols), BF16),
            pltpu.VMEM((count, count), F32),
            pltpu.SemaphoreType.DMA((3 * owners,)),
        ],
        compiler_params=params(62),
        cost_estimate=cost(6),
        name="attention_forward",
    )(place, first, cos, sin, x_t, *pieces)


def run_attention_backward(layer, place, tables, x_t, gain, d_mid, g_ffn, saved, pieces, tile=256):
    first, cos, sin = tables
    wide, count = x_t.shape
    cols = pieces[0].shape[1]
    owners = place.shape[0] - 1
    padded = wide // owners + EXTRA
    return pl.pallas_call(
        functools.partial(attention_backward, layer=layer, tile=tile, count_pieces=len(pieces)),
        out_shape=(
            shape((wide, count), F32),
            shape((wide, count), BF16),
            shape((owners, padded, cols), BF16),
            shape((owners, padded, cols), BF16),
        ),
        in_specs=[SM] + [VM] * 12 + [AN] * len(pieces),
        out_specs=(VM, VM, AN, AN),
        scratch_shapes=[
            pltpu.VMEM((2, wide, cols), BF16),
            pltpu.VMEM((2, owners, padded, cols), BF16),
            pltpu.VMEM((count, count), F32),
            pltpu.VMEM((WIDTH, count), BF16),
            pltpu.VMEM((WIDTH, count), F32),
            pltpu.VMEM((KVW, count), F32),
            pltpu.VMEM((KVW, count), BF16),
            pltpu.SemaphoreType.DMA((2 * owners,)),
            pltpu.SemaphoreType.DMA((2,)),
        ],
        compiler_params=params(62),
        cost_estimate=cost(10),
        name="attention_backward",
    )(place, first, cos, sin, x_t, gain, d_mid, g_ffn, *saved, *pieces)


def run_attention_scores_backward(layer, place, tables, d_mid, saved, pieces, tile=256):
    first, cos, sin = tables
    count, wide = d_mid.shape
    cols = pieces[0].shape[1]
    owners = place.shape[0] - 1
    q, k, v, o, lse = saved
    return pl.pallas_call(
        functools.partial(attention_scores_backward, layer=layer, tile=tile, count_pieces=len(pieces)),
        out_shape=(shape((WIDTH + KVW, count), BF16), shape((KVW, count), BF16)),
        in_specs=[SM] + [VM] * 8 + [AN] * len(pieces),
        out_specs=(VM, VM),
        scratch_shapes=[
            pltpu.VMEM((2, wide, cols), BF16),
            pltpu.VMEM((count, count), F32),
            pltpu.VMEM((WIDTH, count), BF16),
            pltpu.VMEM((WIDTH, count), F32),
            pltpu.VMEM((KVW, count), F32),
            pltpu.SemaphoreType.DMA((2 * owners,)),
        ],
        compiler_params=params(56),
        cost_estimate=cost(7),
        name="attention_scores_backward",
    )(place, first, cos, sin, d_mid, q, k, v, lse, *pieces)


def run_attention_weights_backward(layer, place, x_t, gain, d_mid, g_ffn, saved, d_qk, d_v, pieces):
    wide, count = x_t.shape
    cols = pieces[0].shape[1]
    owners = place.shape[0] - 1
    padded = wide // owners + EXTRA
    return pl.pallas_call(
        functools.partial(attention_weights_backward, layer=layer, count_pieces=len(pieces)),
        out_shape=(
            shape((wide, count), F32),
            shape((wide, count), BF16),
            shape((owners, padded, cols), BF16),
            shape((owners, padded, cols), BF16),
        ),
        in_specs=[SM] + [VM] * 7 + [AN] * len(pieces),
        out_specs=(VM, VM, AN, AN),
        scratch_shapes=[
            pltpu.VMEM((2, wide, cols), BF16),
            pltpu.VMEM((2, owners, padded, cols), BF16),
            pltpu.SemaphoreType.DMA((2 * owners,)),
            pltpu.SemaphoreType.DMA((2,)),
        ],
        compiler_params=params(56),
        cost_estimate=cost(3),
        name="attention_weights_backward",
    )(place, x_t, gain, d_mid, g_ffn, saved[3], d_qk, d_v, *pieces)


def run_feed_forward(layer, place, mid, gain, pieces, dy_t=None, kept=(), block=768):
    backward = dy_t is not None
    forward = not kept
    count, wide = mid.shape
    owners = place.shape[0] - 1
    rows, cols = (pieces[0].shape[0] - EXTRA) // 2, pieces[0].shape[1]
    out_shape, out_specs = [], []
    scratch = [
        pltpu.VMEM((2, wide, 2 * cols), BF16),
        pltpu.VMEM((wide, 2 * cols), BF16),
        pltpu.SemaphoreType.DMA((8 * owners,)),
    ]
    if forward and backward:
        out_shape.append(shape((count, 2 * cols), BF16))
        out_specs.append(VM)
    elif forward:
        out_shape += [shape((wide, count), BF16)] + [shape((count, 2 * cols), BF16)] * 2
        out_specs += [VM] * 3
    scratch.append(pltpu.VMEM((count, block), BF16))
    if backward:
        out_shape += [
            shape((count, wide), F32),
            shape((1, wide), F32),
            shape((owners, 3 * rows, cols), BF16),
            shape((owners, 3 * rows, cols), BF16),
        ]
        out_specs += [VM, VM, AN, AN]
        scratch += [
            pltpu.VMEM((2, owners, 3 * rows, cols), BF16),
            pltpu.SemaphoreType.DMA((8,)),
            pltpu.VMEM((count, block), BF16),
            pltpu.VMEM((count, block), BF16),
        ]
    if kept:
        scratch += [pltpu.VMEM((2, count, 2 * cols), BF16), pltpu.SemaphoreType.DMA((4 * cols // block,))]
    flops = (7 if forward else 0) + (14 if backward else 0)
    extra = ([dy_t] if backward else []) + list(kept)
    return pl.pallas_call(
        functools.partial(
            feed_forward, layer=layer, forward=forward, backward=backward, block=block, count_pieces=len(pieces)
        ),
        out_shape=tuple(out_shape),
        in_specs=[SM, VM, VM] + [AN] * len(pieces) + [VM] * (len(extra) - len(kept)) + [AN] * len(kept),
        out_specs=tuple(out_specs),
        scratch_shapes=scratch,
        compiler_params=params(56 if kept else 62),
        cost_estimate=cost(flops),
        name="feed_forward",
    )(place, mid, gain, *pieces, *extra)


def run_feed_forward_result(layer, place, mid, hidden, pieces):
    count, wide = mid.shape
    owners = place.shape[0] - 1
    return pl.pallas_call(
        functools.partial(feed_forward_result, layer=layer, count_pieces=len(pieces)),
        out_shape=shape((wide, count), BF16),
        in_specs=[SM, VM, VM] + [AN] * len(pieces),
        out_specs=VM,
        scratch_shapes=[pltpu.VMEM((wide, hidden.shape[1]), BF16), pltpu.SemaphoreType.DMA((8 * owners,))],
        compiler_params=params(24),
        cost_estimate=cost(2),
        name="feed_forward_result",
    )(place, mid, hidden, *pieces)


def make_tables(lengths, count):
    ends = jnp.cumsum(lengths)
    starts = ends - lengths
    places = jnp.arange(count, dtype=jnp.int32)
    document = jnp.sum((places[:, None] >= ends[None, :]).astype(jnp.int32), axis=1)
    inside = document[:, None] == jnp.arange(lengths.shape[0], dtype=jnp.int32)[None, :]
    first = jnp.sum(jnp.where(inside, starts[None, :], 0), axis=1)
    position = (places - first).astype(F32)
    frequency = rope_base ** (-(jnp.arange(HALF, dtype=F32) * 2.0 / HEAD))
    angles = frequency[:, None] * position[None, :]
    return first[None, :], jnp.cos(angles), jnp.sin(angles)


def swap(value):
    return lax.ppermute(value, "section", [(0, 1), (1, 0)])


def give(value, target):
    return lax.ppermute(value, "section", [(1 - target, target)])


def exchange(value, axis, bit):
    count = lax.axis_size(axis)
    return lax.ppermute(value, axis, [(i, i ^ bit) for i in range(count)])


def mixed_exchange(value, even_bit, odd_bit):
    owners, replicas = lax.axis_size("fsdp"), lax.axis_size("dp")
    pairs = []
    for i in range(owners):
        for z in range(replicas):
            partner = i ^ (odd_bit if z % 2 else even_bit)
            pairs.append((i * replicas + z, partner * replicas + z))
    return lax.ppermute(value, ("fsdp", "dp"), pairs)


def paired():
    return lax.axis_size("fsdp") == 4 and lax.axis_size("dp") % 2 == 0


def piece_places():
    own = lax.axis_index("fsdp")
    if not paired():
        count = lax.axis_size("fsdp")
        return [own] + [(own + i) % count for i in range(1, count)]
    odd = lax.axis_index("dp") % 2
    near, far = jnp.where(odd == 1, own ^ 2, own ^ 1), jnp.where(odd == 1, own ^ 1, own ^ 2)
    return [own, near, own ^ 3, far]


def first_hop(value):
    if not paired():
        return lax.all_gather(value, "fsdp")
    return mixed_exchange(value, 1, 2)


def second_hop(near):
    if not paired():
        count = lax.axis_size("fsdp")
        own = lax.axis_index("fsdp")
        return [pick(near, (own + i) % count, 0) for i in range(1, count)]
    return [near, mixed_exchange(near, 2, 1), exchange(near, "dp", 1)]


def shared(pieces):
    return pieces + [swap(piece) for piece in pieces]


def tie(*values):
    return lax.optimization_barrier(values)


def pick(value, index, axis):
    return lax.dynamic_index_in_dim(value, index, axis, keepdims=False)


def total(left, right):
    return left + right


def split_first(place, ins, outs, cut):
    (keep, came), outs = ins, list(outs)
    y, x = place[1] // 2, place[1] % 2
    for by_x, low, high in ((True, 0, cut), (False, cut, keep.shape[1])):
        if low == high:
            continue
        hold, away = outs.pop(0), outs.pop(0)
        for i in range(2):
            for target, mine in ((hold, True), (away, False)):
                bit_x, bit_y = (x, y) if mine else (1 - x, 1 - y)
                block = 2 * i + bit_x if by_x else 2 * bit_y + i
                target[i] = total(keep[block, low:high], came[block, low:high])


def split_second(place, ins, outs, order):
    y, x = place[1] // 2, place[1] % 2
    for i, by_x in enumerate(order):
        hold, came, stay, away = ins[2 * i], ins[2 * i + 1], outs[2 * i], outs[2 * i + 1]
        bit = y if by_x else x
        stay[...] = total(hold[bit], came[bit])
        away[...] = total(hold[1 - bit], came[1 - bit])


def stack_sums(place, ins, outs):
    at = 0
    for i in range(0, len(ins), 2):
        rows = ins[i].shape[0]
        outs[0][at:at + rows, :] = total(ins[i][...], ins[i + 1][...])
        at += rows


def from_middle(place, ins, outs):
    z = place[place.shape[0] - 1]
    inner = (z == 1) | (z == 2)

    @pl.when(inner)
    def _():
        outs[0][...] = ins[0][...]

    @pl.when(jnp.logical_not(inner))
    def _():
        outs[0][...] = ins[1][...]


def work(place, *refs, steps):
    ins, outs = [], list(refs)
    for _, count_in, _ in steps:
        ins.append(outs[:count_in])
        outs = outs[count_in:]
    for (body, _, count_out), taken in zip(steps, ins):
        body(place, taken, outs[:count_out])
        outs = outs[count_out:]


def run_work(place, jobs, mib=24):
    ins = [value for job in jobs for value in job[1]]
    out = [shape(dims, BF16) for job in jobs for dims in job[2]]
    done = list(pl.pallas_call(
        functools.partial(work, steps=tuple((job[0], len(job[1]), len(job[2])) for job in jobs)),
        out_shape=tuple(out),
        in_specs=[SM] + [VM] * len(ins),
        out_specs=(VM,) * len(out),
        compiler_params=params(mib),
        name="work",
    )(place, *ins))
    for job in jobs:
        job[3](done[:len(job[2])])
        done = done[len(job[2]):]


def split_large(place, keep, came, hold_x, away_x, hold_y, away_y, left, right, sems_in, sems_out, *, cut):
    owners = keep.shape[0]
    y, x = place[1] // 2, place[1] % 2
    loads = [
        (start(keep.at[f], left.at[f], sems_in.at[2 * f]), start(came.at[f], right.at[f], sems_in.at[2 * f + 1]))
        for f in range(owners)
    ]
    stores = []
    for f in range(owners):
        for one in loads[f]:
            one.wait()
        left[f] = total(left[f], right[f])
        low, high = left.at[f, :cut], left.at[f, cut:]
        stores.append(either(x == f % 2, (low, hold_x.at[f // 2]), (low, away_x.at[f // 2]), None, sems_out.at[2 * f]))
        stores.append(
            either(y == f // 2, (high, hold_y.at[f % 2]), (high, away_y.at[f % 2]), None, sems_out.at[2 * f + 1])
        )
    for one in stores:
        one.wait()


def run_split_large(place, keep, came, cut):
    owners, rows, cols = keep.shape
    low, high = shape((2, cut, cols), BF16), shape((2, rows - cut, cols), BF16)
    return pl.pallas_call(
        functools.partial(split_large, cut=cut),
        out_shape=(low, low, high, high),
        in_specs=[SM, AN, AN],
        out_specs=(AN,) * 4,
        scratch_shapes=[
            pltpu.VMEM(keep.shape, BF16),
            pltpu.VMEM(keep.shape, BF16),
            pltpu.SemaphoreType.DMA((2 * owners,)),
            pltpu.SemaphoreType.DMA((2 * owners,)),
        ],
        compiler_params=params(56),
        name="split_large",
    )(place, keep, came)


def split_side(place, keep, came, out_x, out_y, left_x, right_x, left_y, right_y, sems_in, sems_out, *, cut, away):
    y, x = place[1] // 2, place[1] % 2
    if away:
        y, x = 1 - y, 1 - x
    jobs = []
    for i in range(2):
        for block, window, left, right, out in (
            (2 * i + x, slice(0, cut), left_x, right_x, out_x),
            (2 * y + i, slice(cut, keep.shape[1]), left_y, right_y, out_y),
        ):
            number = len(jobs)
            loads = (
                start(keep.at[block, window], left.at[i], sems_in.at[2 * number]),
                start(came.at[block, window], right.at[i], sems_in.at[2 * number + 1]),
            )
            jobs.append((loads, left, right, out, i))
    stores = []
    for number, (loads, left, right, out, i) in enumerate(jobs):
        for one in loads:
            one.wait()
        left[i] = total(left[i], right[i])
        stores.append(start(left.at[i], out.at[i], sems_out.at[number]))
    for one in stores:
        one.wait()


def run_split_side(place, keep, came, cut, away):
    _, rows, cols = keep.shape
    low, high = (2, cut, cols), (2, rows - cut, cols)
    return pl.pallas_call(
        functools.partial(split_side, cut=cut, away=away),
        out_shape=(shape(low, BF16), shape(high, BF16)),
        in_specs=[SM, AN, AN],
        out_specs=(AN,) * 2,
        scratch_shapes=[
            pltpu.VMEM(low, BF16),
            pltpu.VMEM(low, BF16),
            pltpu.VMEM(high, BF16),
            pltpu.VMEM(high, BF16),
            pltpu.SemaphoreType.DMA((8,)),
            pltpu.SemaphoreType.DMA((4,)),
        ],
        compiler_params=params(56),
        name="split_away" if away else "split_hold",
    )(place, keep, came)


class Sum:
    def __init__(self, keep, send, cut, pairs=False):
        self.hold, self.cut, self.pairs = [keep], cut, pairs
        self.chain = lax.axis_size("dp") == 4
        self.came = [swap(send)]
        rows = keep.shape[1]
        self.order = [by_x for by_x, some in ((True, cut > 0), (False, cut < rows)) if some]

    def split(self, second):
        def then(outs):
            self.hold = list(outs[::2])
            self.came = [
                exchange(value, "fsdp", 1 if by_x != second else 2) for value, by_x in zip(outs[1::2], self.order)
            ]
        return then

    def fsdp_first(self):
        _, rows, cols = self.hold[0].shape
        dims = [(2, self.cut if by_x else rows - self.cut, cols) for by_x in self.order for _ in range(2)]
        return functools.partial(split_first, cut=self.cut), self.hold + self.came, dims, self.split(False)

    def fsdp_first_large(self, place):
        self.split(False)(run_split_large(place, self.hold[0], self.came[0], self.cut))

    def fsdp_first_away(self, place):
        outs = run_split_side(place, self.hold[0], self.came[0], self.cut, True)
        *outs, self.hold[0], self.pending = tie(*outs, self.hold[0], self.came[0])
        self.came = [exchange(value, "fsdp", 1 if by_x else 2) for value, by_x in zip(outs, self.order)]

    def fsdp_first_hold(self, place):
        self.hold = list(run_split_side(place, self.hold[0], self.pending, self.cut, False))

    def fsdp_second(self):
        ins = [value for pair in zip(self.hold, self.came) for value in pair]
        dims = [value.shape[1:] for value in self.hold for _ in range(2)]
        return functools.partial(split_second, order=tuple(self.order)), ins, dims, self.split(True)

    def dp(self, hop):
        ins = [value for pair in zip(self.hold, self.came) for value in pair]
        dims = [(sum(value.shape[0] for value in self.hold), self.hold[0].shape[1])]

        def then(outs):
            value = outs[0]
            self.hold = [value]
            if not self.chain:
                self.came = [lax.psum(value, "dp") if hop == 0 else jnp.zeros_like(value)]
                if hop == 0:
                    self.hold = [jnp.zeros_like(value)]
            elif self.pairs:
                self.came = [exchange(value, "dp", 1 + hop)] if hop < 2 else []
            else:
                pairs = ([(0, 1), (3, 2)], [(1, 2), (2, 1)], [(1, 0), (2, 3)])[hop]
                self.came = [lax.ppermute(value, "dp", pairs)]

        return stack_sums, ins, dims, then

    def finish(self):
        def then(outs):
            self.hold, self.came = list(outs), []

        if not self.chain or self.pairs:
            return self.dp(2)[:3] + (then,)
        return from_middle, self.hold + self.came, [self.hold[0].shape], then


def choose(line, ff1, ff0, ff0_came, at1, at0, at0_came, ff_own, ff_send, at_own, at_send, *, chain):
    z = line[line.shape[0] - 1]
    inner = (z == 1) | (z == 2)
    for sec in range(2):
        targets = (ff_own, at_own, ff_send, at_send) if sec == 0 else (ff_send, at_send, ff_own, at_own)

        @pl.when(line[0] == sec)
        def _(targets=targets):
            if chain:

                @pl.when(inner)
                def _():
                    targets[0][...] = ff0[...]

                @pl.when(jnp.logical_not(inner))
                def _():
                    targets[0][...] = ff0_came[...]
            else:
                targets[0][...] = total(ff0[...], ff0_came[...])
            targets[1][...] = total(at0[...], at0_came[...])
            targets[2][...] = ff1[...]
            targets[3][...] = at1[...]


def run_choose(line, ff1, ff0, at1, at0):
    ff, at = shape(ff1.shape, BF16), shape(at1.shape, BF16)
    return pl.pallas_call(
        functools.partial(choose, chain=ff0.chain),
        out_shape=(ff, ff, at, at),
        in_specs=[SM] + [VM] * 6,
        out_specs=(VM,) * 4,
        compiler_params=params(24),
        name="choose",
    )(line, ff1, ff0.hold[0], ff0.came[0], at1, at0.hold[0], at0.came[0])


def unpack(place, ff_own, ff_given, at_own, at_given, gate, up, down, wq, wk, wv, wo, gain_attn, gain_ffn):
    rows = gate.shape[0]
    narrow = down.shape[1]

    def emit(half, part, value):
        wide = (gate, up)[half]
        for i in range(2):
            wide[:, 2 * i * narrow:(2 * i + 2) * narrow] = part[i * rows:(i + 1) * rows, :].astype(F32)
        top = 2 * half * rows
        down[top:top + rows, :] = part[2 * rows:, :narrow].astype(F32)
        down[top + rows:top + 2 * rows, :] = part[2 * rows:, narrow:].astype(F32)
        left, right = ((wq, wk), (wo, wv))[half]
        left[...] = value[:rows, :WIDTH].astype(F32)
        right[...] = value[:rows, WIDTH:].astype(F32)
        if half == 0:
            gains = value[rows:, :rows].astype(F32)
            gain_attn[...] = gains[:1]
            gain_ffn[...] = gains[1:2]

    for sec in range(2):

        @pl.when(place[0] == sec)
        def _(sec=sec):
            emit(sec, ff_own, at_own)
            emit(1 - sec, ff_given, at_given)


def run_unpack(place, ff_own, ff_given, at_own, at_given):
    rows, cols = ff_own.shape[0] // 3, ff_own.shape[1]
    return pl.pallas_call(
        unpack,
        out_shape=(
            shape((rows, 2 * cols), F32),
            shape((rows, 2 * cols), F32),
            shape((4 * rows, cols // 2), F32),
            shape((rows, WIDTH), F32),
            shape((rows, KVW), F32),
            shape((rows, KVW), F32),
            shape((rows, WIDTH), F32),
            shape((1, rows), F32),
            shape((1, rows), F32),
        ),
        in_specs=[SM] + [VM] * 4,
        out_specs=(VM,) * 9,
        compiler_params=params(32),
        name="unpack",
    )(place, ff_own, ff_given, at_own, at_given)


def local(
    tokens,
    cotangent,
    doc_lengths,
    w_query,
    w_key,
    w_value,
    w_out,
    w_gate,
    w_up,
    w_down,
    gain_attn,
    gain_ffn,
):
    sec = lax.axis_index("section")
    first_section = sec == 0
    count = tokens.shape[2]
    place = jnp.stack([jnp.asarray(i, jnp.int32) for i in [sec] + piece_places()])
    line = jnp.concatenate([place, lax.axis_index("dp").astype(jnp.int32)[None]])
    rows, cols = w_query.shape[1], w_query.shape[2] + w_key.shape[2]
    own_at, rest_at = run_pack(
        pack_first, "pack_first", (2 * rows + EXTRA, cols),
        w_query[0], w_key[0], w_value[0], w_out[0], gain_attn, gain_ffn, w_down[0].T,
    )
    w_gate, own_at, rest_at = tie(w_gate, own_at, rest_at)
    own_ff, rest_ff = run_pack(pack_second, "pack_second", (2 * rows, cols), w_gate[0], w_up[0])

    def own_pieces(own, rest):
        came_own, came_rest = swap(rest), swap(own)
        home = [own, came_own, rest, came_rest]
        return home, jnp.where(first_section, own, came_own), jnp.where(first_section, came_own, own)

    at_home, at_zero, at_one = own_pieces(own_at, rest_at)
    ff_home, ff_zero, ff_one = own_pieces(own_ff, rest_ff)
    tables = make_tables(pick(doc_lengths[0], sec, 0), count)
    at_zero, tokens, cotangent = tie(at_zero, tokens, cotangent)
    x0 = jnp.swapaxes(pick(tokens[0], sec, 0), 0, 1)
    dy1 = jnp.swapaxes(pick(cotangent[0], sec, 0), 0, 1)

    near_at0 = first_hop(at_zero)
    near_ff0 = first_hop(ff_zero)
    near_at0, ff_one, x0, dy1, *tables = tie(near_at0, ff_one, x0, dy1, *tables)
    at0 = second_hop(near_at0)
    near_ff0, at_one, ff_one, *at0 = tie(near_ff0, at_one, ff_one, *at0)
    ff0 = second_hop(near_ff0)
    near_at1 = first_hop(at_one)
    near_ff1 = first_hop(ff_one)
    at0 = shared(at0)
    mid0, *saved0, gains0 = run_attention_forward(0, place, tables, x0, at_home + at0)
    mid0, near_at1, *ff0 = tie(mid0, near_at1, *ff0)

    ff0 = shared(ff0)
    at1 = second_hop(near_at1)
    y0, gate0, up0 = run_feed_forward(0, place, mid0, gains0, at_home + at0 + ff_home + ff0)
    y0, near_ff1, *at1 = tie(y0, near_ff1, *at1)

    at1 = shared(at1)
    ff1 = second_hop(near_ff1)
    mid1, *saved1, gains1 = run_attention_forward(1, place, tables, y0, at_home + at1)
    mid1, *ff1 = tie(mid1, *ff1)
    ff1 = shared(ff1)
    hidden1, d_mid1, g_ffn1, ff_keep1, ff_send1 = run_feed_forward(
        1, place, mid1, gains1, at_home + at1 + ff_home + ff1, dy_t=dy1
    )

    sums = []

    def after(waited, *others):
        cells = [(one.came, i) for one, i in waited]
        for one in sums:
            cells += [(one.hold, i) for i in range(len(one.hold))]
        held = list(tie(*others, *[array[i] for array, i in cells]))
        for (array, i), value in zip(cells, held[len(others):]):
            array[i] = value
        return held[:len(others)]

    def both_rows(own0, own1):
        back = swap(jnp.where(first_section, own1, own0))
        both = jnp.where(first_section, jnp.stack([own0, back]), jnp.stack([back, own1]))
        return jnp.swapaxes(both, 1, 2)[None, None]

    ff_cut, at_cut = ff_keep1.shape[1] // 32 * 16, (rows + EXTRA) // 32 * 16
    f1 = Sum(ff_keep1, ff_send1, ff_cut)
    sums.append(f1)
    dx1, dy0, at_keep1, at_send1 = run_attention_backward(
        1, place, tables, y0, gains1, d_mid1, g_ffn1, saved1, at_home + at1
    )
    dy0, at_keep1, at_send1 = after([(f1, 0)], dy0, at_keep1, at_send1)

    f1.fsdp_first_large(place)
    a1 = Sum(at_keep1, at_send1, at_cut)
    sums.append(a1)
    (dy0,) = after([], dy0)
    d_mid0, g_ffn0, ff_keep0, ff_send0 = run_feed_forward(
        0, place, mid0, gains0, at_home + at0 + ff_home + ff0, dy_t=dy0, kept=(gate0, up0)
    )
    d_mid0, ff_keep0, ff_send0 = after([(f1, 0), (f1, 1), (a1, 0)], d_mid0, ff_keep0, ff_send0)

    f0 = Sum(ff_keep0, ff_send0, ff_cut)
    sums.append(f0)
    run_work(line, [f1.fsdp_second(), a1.fsdp_first()])
    (d_mid0,) = after([], d_mid0)
    d_qk0, d_v0 = run_attention_scores_backward(0, place, tables, d_mid0, saved0, at_home + at0)
    d_qk0, d_v0 = after([(f0, 0), (f1, 0), (f1, 1), (a1, 0), (a1, 1)], d_qk0, d_v0)

    f0.fsdp_first_away(place)
    after([])
    run_work(line, [f1.dp(0), a1.fsdp_second()])
    (d_qk0,) = after([], d_qk0)
    dx0, _, at_keep0, at_send0 = run_attention_weights_backward(
        0, place, x0, gains0, d_mid0, g_ffn0, saved0, d_qk0, d_v0, at_home + at0
    )
    f0.fsdp_first_hold(place)
    at_send0, at_keep0 = after([(f0, 0), (f0, 1), (f1, 0), (a1, 0), (a1, 1)], at_send0, at_keep0)

    a0 = Sum(at_keep0, at_send0, at_cut, True)
    sums.append(a0)
    run_work(line, [f0.fsdp_second(), f1.dp(1)])
    after([(a0, 0)])
    run_work(line, [a0.fsdp_first(), a1.dp(0)])
    dx0, dx1, hidden1 = after([(f0, 0), (f0, 1), (f1, 0), (a1, 0), (a0, 0), (a0, 1)], dx0, dx1, hidden1)

    run_work(line, [f0.dp(0), f1.dp(2), a1.dp(1), a0.fsdp_second()])
    y1 = run_feed_forward_result(1, place, mid1, hidden1, at_home + at1)
    dx0, dx1, y1 = after([(f0, 0), (f1, 0), (a1, 0), (a0, 0), (a0, 1)], dx0, dx1, y1)

    run_work(line, [f0.dp(1), a1.dp(2), a0.dp(0), f1.finish()])
    dx0, dx1 = after([], dx0, dx1)
    grad = both_rows(dx0, dx1)
    (grad,) = after([(f0, 0), (a1, 0), (a0, 0)], grad)

    run_work(line, [f0.dp(2), a0.dp(1), a1.finish()])
    y0, y1 = after([], y0, y1)
    out = both_rows(y0, y1)
    (out,) = after([(f0, 0), (a0, 0)], out)

    ff_own, ff_send, at_own, at_send = run_choose(line, f1.hold[0], f0, a1.hold[0], a0)
    gate, up, down, wq, wk, wv, wo, gain_attn, gain_ffn = run_unpack(place, ff_own, swap(ff_send), at_own, swap(at_send))

    return (
        out,
        grad,
        wq[None],
        wk[None],
        wv[None],
        wo[None],
        gate[None],
        up[None],
        down.T[None],
        gain_attn,
        gain_ffn,
    )


def solution(mesh):
    whole = P(("fsdp", "dp"), None, None, None)
    weight = P("section", "fsdp", None)
    gain = P("section", "fsdp")
    rows = P("section", ("fsdp", "dp"), None, None, None)
    in_specs = (whole, whole, P(("fsdp", "dp"), None, None)) + (weight,) * 7 + (gain,) * 2
    out_specs = (rows, rows) + (weight,) * 7 + (gain,) * 2
    return jax.shard_map(local, mesh=mesh, in_specs=in_specs, out_specs=out_specs, check_vma=False)
```

```python
import functools
import jax
import jax.numpy as jnp
from jax import lax
from jax.experimental import pallas as pl
from jax.experimental.pallas import tpu as pltpu
from jax.sharding import PartitionSpec as P

HEADS = 9
KV_HEADS = 3
GROUP = HEADS // KV_HEADS
HEAD = 64
HALF = HEAD // 2
WIDTH = HEADS * HEAD
KVW = KV_HEADS * HEAD

epsilon = 1e-05
rope_base = 100000.0
masked_score = -1e30
SCALE = HEAD ** (-0.5)
EXTRA = 16
F32 = jnp.float32
BF16 = jnp.bfloat16


def nn(left, right):
    return lax.dot_general(left, right, (((1,), (0,)), ((), ())), preferred_element_type=F32)


def nt(left, right):
    return lax.dot_general(left, right, (((1,), (1,)), ((), ())), preferred_element_type=F32)


def inverse_root(values):
    return lax.rsqrt(jnp.mean(values * values, axis=-1, keepdims=True) + epsilon)


def norm_back(values, inv_root, gain, upstream):
    gain_grad = jnp.sum(upstream * values * inv_root, axis=0, keepdims=True)
    scaled = upstream * gain
    dot = jnp.mean(scaled * values, axis=-1, keepdims=True)
    return inv_root * scaled - values * (inv_root * inv_root * inv_root * dot), gain_grad


def sigmoid(values):
    return 0.5 * jnp.tanh(0.5 * values) + 0.5


def pack_first(wq, wk, wv, wo, gain_attn, gain_ffn, down, own, rest):
    rows, cols = wq.shape[0], own.shape[1]
    down_cols = down.shape[1]
    half_down = down.shape[0] // 2
    top = rows + EXTRA

    def write(target, half):
        left, right = ((wq, wk), (wo, wv))[half]
        target[:rows, :] = jnp.concatenate([left[...], right[...]], axis=1)
        target[rows:top, :] = jnp.zeros((EXTRA, cols), BF16)
        target[rows:top, :rows] = jnp.concatenate(
            [gain_attn[...].astype(F32), gain_ffn[...].astype(F32), jnp.zeros((EXTRA - 2, rows), F32)], axis=0
        ).astype(BF16)
        for i in range(2):
            at = half * half_down + i * rows
            target[top:, i * down_cols:(i + 1) * down_cols] = down[at:at + rows, :]

    for number in range(2):

        @pl.when(lax.axis_index("section") == number)
        def _(number=number):
            write(own, number)
            write(rest, 1 - number)


def pack_second(gate, up, own, rest):
    rows, cols = gate.shape[0], own.shape[1]

    def write(target, half):
        wide = (gate, up)[half]
        target[:rows, :] = wide[:, :cols]
        target[rows:, :] = wide[:, cols:]

    for number in range(2):

        @pl.when(lax.axis_index("section") == number)
        def _(number=number):
            write(own, number)
            write(rest, 1 - number)


def either(condition, first, second, target, sem):
    first, second = ((first, target), (second, target)) if target is not None else (first, second)

    @pl.when(condition)
    def _():
        pltpu.make_async_copy(*first, sem).start()

    @pl.when(jnp.logical_not(condition))
    def _():
        pltpu.make_async_copy(*second, sem).start()

    return pltpu.make_async_copy(*first, sem)


def start(source, target, sem):
    one = pltpu.make_async_copy(source, target, sem)
    one.start()
    return one


def sides(place, layer, pieces):
    sec = place[0]
    slots = place.shape[0] - 1
    found = []
    for number, (half, rest) in enumerate(((sec, pieces[4:3 + slots]), (1 - sec, pieces[3 + slots:]))):
        found.append((half, place[1], pieces[2 * number], pieces[2 * number + 1]))
        for slot, piece in enumerate(rest):
            found.append((half, place[2 + slot], piece, None))
    return found


def load_attention(place, layer, pieces, weights, gains, sems):
    rows = (pieces[0].shape[0] - EXTRA) // 2
    home = place[0] == layer
    waits = []
    slots = place.shape[0] - 1
    for number, (half, owner, source, other) in enumerate(sides(place, layer, pieces)):
        target = weights.at[half, pl.ds(pl.multiple_of(owner * rows, 16), rows), :]
        window = slice(0, rows)
        if other is None:
            waits.append(start(source.at[window], target, sems.at[number]))
        else:
            waits.append(either(home, source.at[window], other.at[window], target, sems.at[number]))
        if number < slots and gains is not None:
            window, target, sem = slice(rows, rows + EXTRA), gains.at[owner], sems.at[2 * slots + number]
            if other is None:
                waits.append(start(source.at[window], target, sem))
            else:
                waits.append(either(home, source.at[window], other.at[window], target, sem))
    return waits


def load_gate_up(place, layer, pieces, gate_up, sems):
    rows, cols = pieces[0].shape[0] // 2, pieces[0].shape[1]
    home = place[0] == layer
    waits = []
    for part in range(2):
        waits.append([])
        for number, (half, owner, source, other) in enumerate(sides(place, layer, pieces)):
            window = slice(part * rows, (part + 1) * rows)
            target = gate_up.at[half, pl.ds(pl.multiple_of(owner * rows, 16), rows), part * cols:(part + 1) * cols]
            sem = sems.at[4 * number + part]
            if other is None:
                waits[part].append(start(source.at[window], target, sem))
            else:
                waits[part].append(either(home, source.at[window], other.at[window], target, sem))
    return waits


def load_down(place, layer, pieces, down, sems, first_sem):
    rows, narrow = (pieces[0].shape[0] - EXTRA) // 2, pieces[0].shape[1] // 2
    home = place[0] == layer
    waits = []
    for number, (half, owner, source, other) in enumerate(sides(place, layer, pieces)):
        for i in range(2):
            window = (slice(rows + EXTRA, 2 * rows + EXTRA), slice(i * narrow, (i + 1) * narrow))
            top = pl.multiple_of(half * (2 * rows) + i * rows, 16)
            target = down.at[pl.ds(top, rows), pl.ds(pl.multiple_of(owner * narrow, 128), narrow)]
            sem = sems.at[4 * number + first_sem + i]
            if other is None:
                waits.append(start(source.at[window], target, sem))
            else:
                waits.append(either(home, source.at[window], other.at[window], target, sem))
    return waits


def fill_bias(first, bias):
    count = bias.shape[0]
    key = lax.broadcasted_iota(jnp.int32, (count, count), 0)
    query = lax.broadcasted_iota(jnp.int32, (count, count), 1)
    allowed = (key >= first[...]) & (key <= query)
    bias[...] = jnp.where(allowed, 0.0, masked_score).astype(F32)


def attention_forward(place, first, cos, sin, x_t, *rest, layer, tile, count_pieces):
    pieces = rest[:count_pieces]
    mid, q_out, k_out, v_out, o_out, lse_out, gain_out, weights, gain_parts, bias, sems = rest[count_pieces:]
    owners = gain_parts.shape[0]
    rows = weights.shape[1] // owners
    waits = load_attention(place, layer, pieces, weights, gain_parts, sems)
    count = x_t.shape[1]
    values = x_t[...].T.astype(F32)
    scaled = values * inverse_root(values)
    fill_bias(first, bias)
    for one in waits:
        one.wait()
    gain = jnp.concatenate([gain_parts[f][:2, :rows].astype(F32) for f in range(owners)], axis=1)
    gain_out[...] = gain
    normed = (scaled * gain[:1]).astype(BF16)
    qk = nt(weights[0].T, normed)
    v_out[...] = nt(weights[1, :, WIDTH:].T, normed).astype(BF16)
    c, s = cos[...], sin[...]

    def turned(part):
        low, high = part[:HALF], part[HALF:]
        return jnp.concatenate([low * c - high * s, high * c + low * s], axis=0)

    for head in range(HEADS):
        span = slice(head * HEAD, (head + 1) * HEAD)
        q_out[span, :] = (turned(qk[span]) * SCALE).astype(BF16)
    for j in range(KV_HEADS):
        at = WIDTH + j * HEAD
        k_out[j * HEAD:(j + 1) * HEAD, :] = turned(qk[at:at + HEAD]).astype(BF16)
    for j in range(KV_HEADS):
        keys = k_out[j * HEAD:(j + 1) * HEAD, :].T
        vals = v_out[j * HEAD:(j + 1) * HEAD, :]
        for g in range(GROUP):
            head = j * GROUP + g
            span = slice(head * HEAD, (head + 1) * HEAD)
            for at in range(0, count, tile):
                end = at + tile
                scores = nn(keys[:end], q_out[span, at:end]) + bias[:end, at:end]
                top = jnp.max(scores, axis=0, keepdims=True)
                power = jnp.exp(scores - top)
                total = jnp.sum(power, axis=0, keepdims=True)
                mixed = nn(vals[:, :end], power.astype(BF16))
                o_out[span, at:end] = (mixed / total).astype(BF16)
                lse_out[head:head + 1, at:end] = top + jnp.log(total)
    mid[...] = values + nn(o_out[...].T, weights[1, :, :WIDTH])


def attention_backward(place, first, cos, sin, x_t, gain, d_mid, g_ffn, q, k, v, o, lse, *rest, layer, tile, count_pieces):
    pieces = rest[:count_pieces]
    dx, dx_low, keep, send, weights, grads, bias, g_out, d_q, d_k, d_v, sems, sems_out = rest[count_pieces:]
    owners = grads.shape[1]
    rows = weights.shape[1] // owners
    sec = place[0]
    waits = load_attention(place, layer, pieces, weights, None, sems)
    count = x_t.shape[1]
    g_mid = d_mid[...].astype(BF16)
    fill_bias(first, bias)
    for one in waits:
        one.wait()
    g_out[...] = nt(weights[1, :, :WIDTH], g_mid).astype(BF16)

    def store(side, columns, value):
        for owner in range(owners):
            grads[side, owner, :rows, columns] = value[owner * rows:(owner + 1) * rows].astype(BF16)

    store(1, slice(0, WIDTH), nn(o[...], g_mid))
    c, s = cos[...], sin[...]

    def turned_back(part):
        low, high = part[:HALF], part[HALF:]
        return jnp.concatenate([low * c + high * s, high * c - low * s], axis=0)

    for j in range(KV_HEADS):
        own = slice(j * HEAD, (j + 1) * HEAD)
        keys_t = k[own, :]
        keys = keys_t.T
        vals = v[own, :].T
        k_sum = [jnp.zeros((HEAD, tile), F32) for _ in range(count // tile)]
        v_sum = [jnp.zeros((HEAD, tile), F32) for _ in range(count // tile)]
        for g in range(GROUP):
            head = j * GROUP + g
            span = slice(head * HEAD, (head + 1) * HEAD)
            for at in range(0, count, tile):
                end = at + tile
                q_part = q[span, at:end]
                g_part = g_out[span, at:end]
                power = jnp.exp(nn(keys[:end], q_part) + bias[:end, at:end] - lse[head:head + 1, at:end])
                d_prob = nn(vals[:end], g_part)
                delta = jnp.sum(power * d_prob, axis=0, keepdims=True)
                d_score = (power * (d_prob - delta)).astype(BF16)
                power = power.astype(BF16)
                v_add = nt(g_part, power)
                k_add = nt(q_part, d_score)
                for i in range(end // tile):
                    v_sum[i] = v_sum[i] + v_add[:, i * tile:(i + 1) * tile]
                    k_sum[i] = k_sum[i] + k_add[:, i * tile:(i + 1) * tile]
                d_q[span, at:end] = nn(keys_t[:, :end], d_score) * SCALE
        d_k[own, :] = jnp.concatenate(k_sum, axis=1)
        d_v[own, :] = jnp.concatenate(v_sum, axis=1).astype(BF16)
    turned = [turned_back(d_q[h * HEAD:(h + 1) * HEAD, :]).astype(BF16) for h in range(HEADS)]
    turned += [turned_back(d_k[h * HEAD:(h + 1) * HEAD, :]).astype(BF16) for h in range(KV_HEADS)]
    d_qk = jnp.concatenate(turned, axis=0)
    values = x_t[...].T.astype(F32)
    inv = inverse_root(values)
    attn_gain = gain[:1, :]
    normed_t = (values * inv * attn_gain).astype(BF16).T
    store(0, slice(None), nt(normed_t, d_qk))
    store(1, slice(WIDTH, None), nt(normed_t, d_v[...]))
    d_normed = (nn(weights[0], d_qk) + nn(weights[1, :, WIDTH:], d_v[...])).T
    back, gain_grad = norm_back(values, inv, attn_gain, d_normed)
    for owner in range(owners):
        span = slice(owner * rows, (owner + 1) * rows)
        both = jnp.concatenate([gain_grad[:, span], g_ffn[:, span]], axis=0)
        grads[:, owner, rows:, :] = jnp.zeros((2, EXTRA, grads.shape[3]), BF16)
        padded = jnp.concatenate([both, jnp.zeros((EXTRA - 2, rows), F32)], axis=0)
        grads[0, owner, rows:, :rows] = padded.astype(BF16)
    out = [start(grads.at[1 - sec], send, sems_out.at[0]), start(grads.at[sec], keep, sems_out.at[1])]
    total = (d_mid[...] + back).T
    dx[...] = total
    dx_low[...] = total.astype(BF16)
    for one in out:
        one.wait()


def attention_scores_backward(place, first, cos, sin, d_mid, q, k, v, lse, *rest, layer, tile, count_pieces):
    pieces = rest[:count_pieces]
    d_qk, d_v, weights, bias, g_out, d_q, d_k, sems = rest[count_pieces:]
    waits = load_attention(place, layer, pieces, weights, None, sems)
    count = d_mid.shape[0]
    g_mid = d_mid[...].astype(BF16)
    fill_bias(first, bias)
    for one in waits:
        one.wait()
    g_out[...] = nt(weights[1, :, :WIDTH], g_mid).astype(BF16)
    c, s = cos[...], sin[...]

    def turned_back(part):
        low, high = part[:HALF], part[HALF:]
        return jnp.concatenate([low * c + high * s, high * c - low * s], axis=0)

    for j in range(KV_HEADS):
        own = slice(j * HEAD, (j + 1) * HEAD)
        keys_t = k[own, :]
        keys = keys_t.T
        vals = v[own, :].T
        k_sum = [jnp.zeros((HEAD, tile), F32) for _ in range(count // tile)]
        v_sum = [jnp.zeros((HEAD, tile), F32) for _ in range(count // tile)]
        for g in range(GROUP):
            head = j * GROUP + g
            span = slice(head * HEAD, (head + 1) * HEAD)
            for at in range(0, count, tile):
                end = at + tile
                q_part = q[span, at:end]
                g_part = g_out[span, at:end]
                power = jnp.exp(nn(keys[:end], q_part) + bias[:end, at:end] - lse[head:head + 1, at:end])
                d_prob = nn(vals[:end], g_part)
                delta = jnp.sum(power * d_prob, axis=0, keepdims=True)
                d_score = (power * (d_prob - delta)).astype(BF16)
                power = power.astype(BF16)
                v_add = nt(g_part, power)
                k_add = nt(q_part, d_score)
                for i in range(end // tile):
                    v_sum[i] = v_sum[i] + v_add[:, i * tile:(i + 1) * tile]
                    k_sum[i] = k_sum[i] + k_add[:, i * tile:(i + 1) * tile]
                d_q[span, at:end] = nn(keys_t[:, :end], d_score) * SCALE
        d_k[own, :] = jnp.concatenate(k_sum, axis=1)
        d_v[own, :] = jnp.concatenate(v_sum, axis=1).astype(BF16)
    for h in range(HEADS):
        d_qk[h * HEAD:(h + 1) * HEAD, :] = turned_back(d_q[h * HEAD:(h + 1) * HEAD, :]).astype(BF16)
    for h in range(KV_HEADS):
        d_qk[WIDTH + h * HEAD:WIDTH + (h + 1) * HEAD, :] = turned_back(d_k[h * HEAD:(h + 1) * HEAD, :]).astype(BF16)


def attention_weights_backward(place, x_t, gain, d_mid, g_ffn, o, d_qk, d_v, *rest, layer, count_pieces):
    pieces = rest[:count_pieces]
    dx, dx_low, keep, send, weights, grads, sems, sems_out = rest[count_pieces:]
    owners = grads.shape[1]
    rows = weights.shape[1] // owners
    sec = place[0]
    waits = load_attention(place, layer, pieces, weights, None, sems)

    def store(side, columns, value):
        for owner in range(owners):
            grads[side, owner, :rows, columns] = value[owner * rows:(owner + 1) * rows].astype(BF16)

    store(1, slice(0, WIDTH), nn(o[...], d_mid[...].astype(BF16)))
    values = x_t[...].T.astype(F32)
    inv = inverse_root(values)
    attn_gain = gain[:1, :]
    normed_t = (values * inv * attn_gain).astype(BF16).T
    store(0, slice(None), nt(normed_t, d_qk[...]))
    store(1, slice(WIDTH, None), nt(normed_t, d_v[...]))
    for one in waits:
        one.wait()
    d_normed = (nn(weights[0], d_qk[...]) + nn(weights[1, :, WIDTH:], d_v[...])).T
    back, gain_grad = norm_back(values, inv, attn_gain, d_normed)
    for owner in range(owners):
        span = slice(owner * rows, (owner + 1) * rows)
        both = jnp.concatenate([gain_grad[:, span], g_ffn[:, span]], axis=0)
        grads[:, owner, rows:, :] = jnp.zeros((2, EXTRA, grads.shape[3]), BF16)
        padded = jnp.concatenate([both, jnp.zeros((EXTRA - 2, rows), F32)], axis=0)
        grads[0, owner, rows:, :rows] = padded.astype(BF16)
    out = [start(grads.at[1 - sec], send, sems_out.at[0]), start(grads.at[sec], keep, sems_out.at[1])]
    total = (d_mid[...] + back).T
    dx[...] = total
    dx_low[...] = total.astype(BF16)
    for one in out:
        one.wait()


def feed_forward(place, mid, gain, *rest, layer, forward, backward, block, count_pieces):
    pieces = rest[:count_pieces]
    rest = list(rest[count_pieces:])
    take = lambda: rest.pop(0)
    dy_t = take() if backward else None
    kept = (take(), take()) if backward and not forward else None
    y_t = take() if forward and not backward else None
    hidden_out = take() if forward and backward else None
    keeping = (take(), take()) if forward and not backward else None
    if backward:
        d_mid, d_gain, keep, send = take(), take(), take(), take()
    gate_up, down, sems = take(), take(), take()
    middle = take()
    if backward:
        grads, sems_out, gate_back, up_back = take(), take(), take(), take()
    sec = place[0]
    first_count = len(pieces) // 2
    if kept is None:
        early = load_gate_up(place, layer, pieces[first_count:], gate_up, sems)
        late = load_down(place, layer, pieces[:first_count], down, sems, 2)
    else:
        late = load_down(place, layer, pieces[:first_count], down, sems, 2)
        kept_here, kept_sems = take(), take()
        kept_waits = []
        for number, at in enumerate(range(0, down.shape[1], block)):
            for i in range(2):
                span = slice(at, at + block)
                kept_waits.append(start(kept[i].at[:, span], kept_here.at[i, :, span], kept_sems.at[2 * number + i]))
        early = load_gate_up(place, layer, pieces[first_count:], gate_up, sems)
    values = mid[...]
    inv = inverse_root(values)
    ffn_gain = gain[1:, :]
    normed = (values * inv * ffn_gain).astype(BF16)
    if backward:
        normed_t = normed.T
        dy = dy_t[...].T
        rows = grads.shape[2] // 3
        owners = grads.shape[1]
    if kept is not None:
        for one in late:
            one.wait()
    units = down.shape[1]
    result, d_normed = None, None
    out = []
    for number, at in enumerate(range(0, units, block)):
        span = slice(at, at + block)
        if kept is None:
            for one in early[number]:
                one.wait()
            gate, up = nn(normed, gate_up[0, :, span]), nn(normed, gate_up[1, :, span])
        else:
            for one in kept_waits[2 * number:2 * number + 2]:
                one.wait()
            gate, up = kept_here[0, :, span], kept_here[1, :, span]
        if keeping is not None:
            keeping[0][:, span] = gate.astype(BF16)
            keeping[1][:, span] = up.astype(BF16)
        if number == 0 and kept is None:
            for one in late:
                one.wait()
        if backward:
            d_hidden = nn(dy, down[:, span])
        for at_column in range(0, block, 128):
            strip = slice(at_column, at_column + 128)
            g, u = gate[:, strip].astype(F32), up[:, strip].astype(F32)
            sg = sigmoid(g)
            swish = g * sg
            if hidden_out is None:
                middle[:, strip] = (swish * u).astype(BF16)
            else:
                hidden_out[:, at + at_column:at + at_column + 128] = (swish * u).astype(BF16)
            if backward:
                d = d_hidden[:, strip]
                gate_back[:, strip] = (d * u * (sg * (1.0 + g * (1.0 - sg)))).astype(BF16)
                up_back[:, strip] = (d * swish).astype(BF16)
        hidden = middle[...] if hidden_out is None else hidden_out[:, span]
        if y_t is not None:
            part = nt(hidden, down[:, span])
            result = part if result is None else result + part
        if backward:
            g_gate, g_up = gate_back[...], up_back[...]
            for half, grad in ((0, g_gate), (1, g_up)):
                value = nn(normed_t, grad).astype(BF16)
                for owner in range(owners):
                    grads[half, owner, number * rows:(number + 1) * rows, :] = value[owner * rows:(owner + 1) * rows]
            value = nn(dy_t[...], hidden).astype(BF16)
            narrow = block // 2
            for i in range(2):
                for half in range(2):
                    for k in range(2):
                        top = (2 * half + k) * rows
                        grads[half, 2 * number + i, 2 * rows:, k * narrow:(k + 1) * narrow] = value[
                            top:top + rows, i * narrow:(i + 1) * narrow
                        ]
            for side, target in ((1 - sec, send), (sec, keep)):
                for window in (
                    (slice(None), slice(number * rows, (number + 1) * rows)),
                    (slice(2 * number, 2 * number + 2), slice(2 * rows, 3 * rows)),
                ):
                    out.append(start(grads.at[(side,) + window], target.at[window], sems_out.at[len(out)]))
            if kept is not None:
                for one in early[number]:
                    one.wait()
            part = nt(g_gate, gate_up[0, :, span]) + nt(g_up, gate_up[1, :, span])
            d_normed = part if d_normed is None else d_normed + part
    if y_t is not None:
        y_t[...] = (values + result).astype(BF16).T
    if backward:
        back, gain_grad = norm_back(values, inv, ffn_gain, d_normed)
        d_gain[...] = gain_grad
        d_mid[...] = dy.astype(F32) + back
        for one in out:
            one.wait()


def feed_forward_result(place, mid, hidden, *rest, layer, count_pieces):
    pieces = rest[:count_pieces]
    y_t, down, sems = rest[count_pieces:]
    waits = load_down(place, layer, pieces, down, sems, 0)
    for one in waits:
        one.wait()
    y_t[...] = (mid[...] + nt(hidden[...], down[...])).astype(BF16).T


VM = pl.BlockSpec(memory_space=pltpu.VMEM)
SM = pl.BlockSpec(memory_space=pltpu.SMEM)
AN = pl.BlockSpec(memory_space=pl.ANY)


def params(mib):
    return pltpu.CompilerParams(vmem_limit_bytes=mib * 1024 * 1024)


def shape(dims, kind):
    return jax.ShapeDtypeStruct(dims, kind)


def cost(gigaflops):
    return pl.CostEstimate(flops=int(gigaflops * 10**6), bytes_accessed=10**4, transcendentals=0)


def run_pack(kernel, name, dims, *arrays):
    return pl.pallas_call(
        kernel,
        out_shape=(shape(dims, BF16),) * 2,
        in_specs=[VM] * len(arrays),
        out_specs=(VM,) * 2,
        compiler_params=params(56),
        name=name,
    )(*arrays)


def run_attention_forward(layer, place, tables, x_t, pieces, tile=256):
    first, cos, sin = tables
    wide, count = x_t.shape
    cols = pieces[0].shape[1]
    owners = place.shape[0] - 1
    return pl.pallas_call(
        functools.partial(attention_forward, layer=layer, tile=tile, count_pieces=len(pieces)),
        out_shape=(
            shape((count, wide), F32),
            shape((WIDTH, count), BF16),
            shape((KVW, count), BF16),
            shape((KVW, count), BF16),
            shape((WIDTH, count), BF16),
            shape((HEADS, count), F32),
            shape((2, wide), F32),
        ),
        in_specs=[SM] + [VM] * 4 + [AN] * len(pieces),
        out_specs=(VM,) * 7,
        scratch_shapes=[
            pltpu.VMEM((2, wide, cols), BF16),
            pltpu.VMEM((owners, EXTRA, cols), BF16),
            pltpu.VMEM((count, count), F32),
            pltpu.SemaphoreType.DMA((3 * owners,)),
        ],
        compiler_params=params(62),
        cost_estimate=cost(6),
        name="attention_forward",
    )(place, first, cos, sin, x_t, *pieces)


def run_attention_backward(layer, place, tables, x_t, gain, d_mid, g_ffn, saved, pieces, tile=256):
    first, cos, sin = tables
    wide, count = x_t.shape
    cols = pieces[0].shape[1]
    owners = place.shape[0] - 1
    padded = wide // owners + EXTRA
    return pl.pallas_call(
        functools.partial(attention_backward, layer=layer, tile=tile, count_pieces=len(pieces)),
        out_shape=(
            shape((wide, count), F32),
            shape((wide, count), BF16),
            shape((owners, padded, cols), BF16),
            shape((owners, padded, cols), BF16),
        ),
        in_specs=[SM] + [VM] * 12 + [AN] * len(pieces),
        out_specs=(VM, VM, AN, AN),
        scratch_shapes=[
            pltpu.VMEM((2, wide, cols), BF16),
            pltpu.VMEM((2, owners, padded, cols), BF16),
            pltpu.VMEM((count, count), F32),
            pltpu.VMEM((WIDTH, count), BF16),
            pltpu.VMEM((WIDTH, count), F32),
            pltpu.VMEM((KVW, count), F32),
            pltpu.VMEM((KVW, count), BF16),
            pltpu.SemaphoreType.DMA((2 * owners,)),
            pltpu.SemaphoreType.DMA((2,)),
        ],
        compiler_params=params(62),
        cost_estimate=cost(10),
        name="attention_backward",
    )(place, first, cos, sin, x_t, gain, d_mid, g_ffn, *saved, *pieces)


def run_attention_scores_backward(layer, place, tables, d_mid, saved, pieces, tile=256):
    first, cos, sin = tables
    count, wide = d_mid.shape
    cols = pieces[0].shape[1]
    owners = place.shape[0] - 1
    q, k, v, o, lse = saved
    return pl.pallas_call(
        functools.partial(attention_scores_backward, layer=layer, tile=tile, count_pieces=len(pieces)),
        out_shape=(shape((WIDTH + KVW, count), BF16), shape((KVW, count), BF16)),
        in_specs=[SM] + [VM] * 8 + [AN] * len(pieces),
        out_specs=(VM, VM),
        scratch_shapes=[
            pltpu.VMEM((2, wide, cols), BF16),
            pltpu.VMEM((count, count), F32),
            pltpu.VMEM((WIDTH, count), BF16),
            pltpu.VMEM((WIDTH, count), F32),
            pltpu.VMEM((KVW, count), F32),
            pltpu.SemaphoreType.DMA((2 * owners,)),
        ],
        compiler_params=params(56),
        cost_estimate=cost(7),
        name="attention_scores_backward",
    )(place, first, cos, sin, d_mid, q, k, v, lse, *pieces)


def run_attention_weights_backward(layer, place, x_t, gain, d_mid, g_ffn, saved, d_qk, d_v, pieces):
    wide, count = x_t.shape
    cols = pieces[0].shape[1]
    owners = place.shape[0] - 1
    padded = wide // owners + EXTRA
    return pl.pallas_call(
        functools.partial(attention_weights_backward, layer=layer, count_pieces=len(pieces)),
        out_shape=(
            shape((wide, count), F32),
            shape((wide, count), BF16),
            shape((owners, padded, cols), BF16),
            shape((owners, padded, cols), BF16),
        ),
        in_specs=[SM] + [VM] * 7 + [AN] * len(pieces),
        out_specs=(VM, VM, AN, AN),
        scratch_shapes=[
            pltpu.VMEM((2, wide, cols), BF16),
            pltpu.VMEM((2, owners, padded, cols), BF16),
            pltpu.SemaphoreType.DMA((2 * owners,)),
            pltpu.SemaphoreType.DMA((2,)),
        ],
        compiler_params=params(56),
        cost_estimate=cost(3),
        name="attention_weights_backward",
    )(place, x_t, gain, d_mid, g_ffn, saved[3], d_qk, d_v, *pieces)


def run_feed_forward(layer, place, mid, gain, pieces, dy_t=None, kept=(), block=768):
    backward = dy_t is not None
    forward = not kept
    count, wide = mid.shape
    owners = place.shape[0] - 1
    rows, cols = (pieces[0].shape[0] - EXTRA) // 2, pieces[0].shape[1]
    out_shape, out_specs = [], []
    scratch = [
        pltpu.VMEM((2, wide, 2 * cols), BF16),
        pltpu.VMEM((wide, 2 * cols), BF16),
        pltpu.SemaphoreType.DMA((8 * owners,)),
    ]
    if forward and backward:
        out_shape.append(shape((count, 2 * cols), BF16))
        out_specs.append(VM)
    elif forward:
        out_shape += [shape((wide, count), BF16)] + [shape((count, 2 * cols), BF16)] * 2
        out_specs += [VM] * 3
    scratch.append(pltpu.VMEM((count, block), BF16))
    if backward:
        out_shape += [
            shape((count, wide), F32),
            shape((1, wide), F32),
            shape((owners, 3 * rows, cols), BF16),
            shape((owners, 3 * rows, cols), BF16),
        ]
        out_specs += [VM, VM, AN, AN]
        scratch += [
            pltpu.VMEM((2, owners, 3 * rows, cols), BF16),
            pltpu.SemaphoreType.DMA((8,)),
            pltpu.VMEM((count, block), BF16),
            pltpu.VMEM((count, block), BF16),
        ]
    if kept:
        scratch += [pltpu.VMEM((2, count, 2 * cols), BF16), pltpu.SemaphoreType.DMA((4 * cols // block,))]
    flops = (7 if forward else 0) + (14 if backward else 0)
    extra = ([dy_t] if backward else []) + list(kept)
    return pl.pallas_call(
        functools.partial(
            feed_forward, layer=layer, forward=forward, backward=backward, block=block, count_pieces=len(pieces)
        ),
        out_shape=tuple(out_shape),
        in_specs=[SM, VM, VM] + [AN] * len(pieces) + [VM] * (len(extra) - len(kept)) + [AN] * len(kept),
        out_specs=tuple(out_specs),
        scratch_shapes=scratch,
        compiler_params=params(56 if kept else 62),
        cost_estimate=cost(flops),
        name="feed_forward",
    )(place, mid, gain, *pieces, *extra)


def run_feed_forward_result(layer, place, mid, hidden, pieces):
    count, wide = mid.shape
    owners = place.shape[0] - 1
    return pl.pallas_call(
        functools.partial(feed_forward_result, layer=layer, count_pieces=len(pieces)),
        out_shape=shape((wide, count), BF16),
        in_specs=[SM, VM, VM] + [AN] * len(pieces),
        out_specs=VM,
        scratch_shapes=[pltpu.VMEM((wide, hidden.shape[1]), BF16), pltpu.SemaphoreType.DMA((8 * owners,))],
        compiler_params=params(24),
        cost_estimate=cost(2),
        name="feed_forward_result",
    )(place, mid, hidden, *pieces)


def make_tables(lengths, count):
    ends = jnp.cumsum(lengths)
    starts = ends - lengths
    places = jnp.arange(count, dtype=jnp.int32)
    document = jnp.sum((places[:, None] >= ends[None, :]).astype(jnp.int32), axis=1)
    inside = document[:, None] == jnp.arange(lengths.shape[0], dtype=jnp.int32)[None, :]
    first = jnp.sum(jnp.where(inside, starts[None, :], 0), axis=1)
    position = (places - first).astype(F32)
    frequency = rope_base ** (-(jnp.arange(HALF, dtype=F32) * 2.0 / HEAD))
    angles = frequency[:, None] * position[None, :]
    return first[None, :], jnp.cos(angles), jnp.sin(angles)


def swap(value):
    return lax.ppermute(value, "section", [(0, 1), (1, 0)])


def give(value, target):
    return lax.ppermute(value, "section", [(1 - target, target)])


def exchange(value, axis, bit):
    count = lax.axis_size(axis)
    return lax.ppermute(value, axis, [(i, i ^ bit) for i in range(count)])


def mixed_exchange(value, even_bit, odd_bit):
    owners, replicas = lax.axis_size("fsdp"), lax.axis_size("dp")
    pairs = []
    for i in range(owners):
        for z in range(replicas):
            partner = i ^ (odd_bit if z % 2 else even_bit)
            pairs.append((i * replicas + z, partner * replicas + z))
    return lax.ppermute(value, ("fsdp", "dp"), pairs)


def paired():
    return lax.axis_size("fsdp") == 4 and lax.axis_size("dp") % 2 == 0


def piece_places():
    own = lax.axis_index("fsdp")
    if not paired():
        count = lax.axis_size("fsdp")
        return [own] + [(own + i) % count for i in range(1, count)]
    odd = lax.axis_index("dp") % 2
    near, far = jnp.where(odd == 1, own ^ 2, own ^ 1), jnp.where(odd == 1, own ^ 1, own ^ 2)
    return [own, near, own ^ 3, far]


def first_hop(value):
    if not paired():
        return lax.all_gather(value, "fsdp")
    return mixed_exchange(value, 1, 2)


def second_hop(near):
    if not paired():
        count = lax.axis_size("fsdp")
        own = lax.axis_index("fsdp")
        return [pick(near, (own + i) % count, 0) for i in range(1, count)]
    return [near, mixed_exchange(near, 2, 1), exchange(near, "dp", 1)]


def shared(pieces):
    return pieces + [swap(piece) for piece in pieces]


def tie(*values):
    return lax.optimization_barrier(values)


def pick(value, index, axis):
    return lax.dynamic_index_in_dim(value, index, axis, keepdims=False)


def total(left, right):
    return left + right


def split_first(place, ins, outs, cut):
    (keep, came), outs = ins, list(outs)
    y, x = place[1] // 2, place[1] % 2
    for by_x, low, high in ((True, 0, cut), (False, cut, keep.shape[1])):
        if low == high:
            continue
        hold, away = outs.pop(0), outs.pop(0)
        for i in range(2):
            for target, mine in ((hold, True), (away, False)):
                bit_x, bit_y = (x, y) if mine else (1 - x, 1 - y)
                block = 2 * i + bit_x if by_x else 2 * bit_y + i
                target[i] = total(keep[block, low:high], came[block, low:high])


def split_second(place, ins, outs, order):
    y, x = place[1] // 2, place[1] % 2
    for i, by_x in enumerate(order):
        hold, came, stay, away = ins[2 * i], ins[2 * i + 1], outs[2 * i], outs[2 * i + 1]
        bit = y if by_x else x
        stay[...] = total(hold[bit], came[bit])
        away[...] = total(hold[1 - bit], came[1 - bit])


def stack_sums(place, ins, outs):
    at = 0
    for i in range(0, len(ins), 2):
        rows = ins[i].shape[0]
        outs[0][at:at + rows, :] = total(ins[i][...], ins[i + 1][...])
        at += rows


def from_middle(place, ins, outs):
    z = place[place.shape[0] - 1]
    inner = (z == 1) | (z == 2)

    @pl.when(inner)
    def _():
        outs[0][...] = ins[0][...]

    @pl.when(jnp.logical_not(inner))
    def _():
        outs[0][...] = ins[1][...]


def work(place, *refs, steps):
    ins, outs = [], list(refs)
    for _, count_in, _ in steps:
        ins.append(outs[:count_in])
        outs = outs[count_in:]
    for (body, _, count_out), taken in zip(steps, ins):
        body(place, taken, outs[:count_out])
        outs = outs[count_out:]


def run_work(place, jobs, mib=24):
    ins = [value for job in jobs for value in job[1]]
    out = [shape(dims, BF16) for job in jobs for dims in job[2]]
    done = list(pl.pallas_call(
        functools.partial(work, steps=tuple((job[0], len(job[1]), len(job[2])) for job in jobs)),
        out_shape=tuple(out),
        in_specs=[SM] + [VM] * len(ins),
        out_specs=(VM,) * len(out),
        compiler_params=params(mib),
        name="work",
    )(place, *ins))
    for job in jobs:
        job[3](done[:len(job[2])])
        done = done[len(job[2]):]


def split_large(place, keep, came, hold_x, away_x, hold_y, away_y, left, right, sems_in, sems_out, *, cut):
    owners = keep.shape[0]
    y, x = place[1] // 2, place[1] % 2
    loads = [
        (start(keep.at[f], left.at[f], sems_in.at[2 * f]), start(came.at[f], right.at[f], sems_in.at[2 * f + 1]))
        for f in range(owners)
    ]
    stores = []
    for f in range(owners):
        for one in loads[f]:
            one.wait()
        left[f] = total(left[f], right[f])
        low, high = left.at[f, :cut], left.at[f, cut:]
        stores.append(either(x == f % 2, (low, hold_x.at[f // 2]), (low, away_x.at[f // 2]), None, sems_out.at[2 * f]))
        stores.append(
            either(y == f // 2, (high, hold_y.at[f % 2]), (high, away_y.at[f % 2]), None, sems_out.at[2 * f + 1])
        )
    for one in stores:
        one.wait()


def run_split_large(place, keep, came, cut):
    owners, rows, cols = keep.shape
    low, high = shape((2, cut, cols), BF16), shape((2, rows - cut, cols), BF16)
    return pl.pallas_call(
        functools.partial(split_large, cut=cut),
        out_shape=(low, low, high, high),
        in_specs=[SM, AN, AN],
        out_specs=(AN,) * 4,
        scratch_shapes=[
            pltpu.VMEM(keep.shape, BF16),
            pltpu.VMEM(keep.shape, BF16),
            pltpu.SemaphoreType.DMA((2 * owners,)),
            pltpu.SemaphoreType.DMA((2 * owners,)),
        ],
        compiler_params=params(56),
        name="split_large",
    )(place, keep, came)


def split_side(place, keep, came, out_x, out_y, left_x, right_x, left_y, right_y, sems_in, sems_out, *, cut, away):
    y, x = place[1] // 2, place[1] % 2
    if away:
        y, x = 1 - y, 1 - x
    jobs = []
    for i in range(2):
        for block, window, left, right, out in (
            (2 * i + x, slice(0, cut), left_x, right_x, out_x),
            (2 * y + i, slice(cut, keep.shape[1]), left_y, right_y, out_y),
        ):
            number = len(jobs)
            loads = (
                start(keep.at[block, window], left.at[i], sems_in.at[2 * number]),
                start(came.at[block, window], right.at[i], sems_in.at[2 * number + 1]),
            )
            jobs.append((loads, left, right, out, i))
    stores = []
    for number, (loads, left, right, out, i) in enumerate(jobs):
        for one in loads:
            one.wait()
        left[i] = total(left[i], right[i])
        stores.append(start(left.at[i], out.at[i], sems_out.at[number]))
    for one in stores:
        one.wait()


def run_split_side(place, keep, came, cut, away):
    _, rows, cols = keep.shape
    low, high = (2, cut, cols), (2, rows - cut, cols)
    return pl.pallas_call(
        functools.partial(split_side, cut=cut, away=away),
        out_shape=(shape(low, BF16), shape(high, BF16)),
        in_specs=[SM, AN, AN],
        out_specs=(AN,) * 2,
        scratch_shapes=[
            pltpu.VMEM(low, BF16),
            pltpu.VMEM(low, BF16),
            pltpu.VMEM(high, BF16),
            pltpu.VMEM(high, BF16),
            pltpu.SemaphoreType.DMA((8,)),
            pltpu.SemaphoreType.DMA((4,)),
        ],
        compiler_params=params(56),
        name="split_away" if away else "split_hold",
    )(place, keep, came)


class Sum:
    def __init__(self, keep, send, cut, pairs=False):
        self.hold, self.cut, self.pairs = [keep], cut, pairs
        self.chain = lax.axis_size("dp") == 4
        self.came = [swap(send)]
        rows = keep.shape[1]
        self.order = [by_x for by_x, some in ((True, cut > 0), (False, cut < rows)) if some]

    def split(self, second):
        def then(outs):
            self.hold = list(outs[::2])
            self.came = [
                exchange(value, "fsdp", 1 if by_x != second else 2) for value, by_x in zip(outs[1::2], self.order)
            ]
        return then

    def fsdp_first(self):
        _, rows, cols = self.hold[0].shape
        dims = [(2, self.cut if by_x else rows - self.cut, cols) for by_x in self.order for _ in range(2)]
        return functools.partial(split_first, cut=self.cut), self.hold + self.came, dims, self.split(False)

    def fsdp_first_large(self, place):
        self.split(False)(run_split_large(place, self.hold[0], self.came[0], self.cut))

    def fsdp_first_away(self, place):
        outs = run_split_side(place, self.hold[0], self.came[0], self.cut, True)
        *outs, self.hold[0], self.pending = tie(*outs, self.hold[0], self.came[0])
        self.came = [exchange(value, "fsdp", 1 if by_x else 2) for value, by_x in zip(outs, self.order)]

    def fsdp_first_hold(self, place):
        self.hold = list(run_split_side(place, self.hold[0], self.pending, self.cut, False))

    def fsdp_second(self):
        ins = [value for pair in zip(self.hold, self.came) for value in pair]
        dims = [value.shape[1:] for value in self.hold for _ in range(2)]
        return functools.partial(split_second, order=tuple(self.order)), ins, dims, self.split(True)

    def dp(self, hop):
        ins = [value for pair in zip(self.hold, self.came) for value in pair]
        dims = [(sum(value.shape[0] for value in self.hold), self.hold[0].shape[1])]

        def then(outs):
            value = outs[0]
            self.hold = [value]
            if not self.chain:
                self.came = [lax.psum(value, "dp") if hop == 0 else jnp.zeros_like(value)]
                if hop == 0:
                    self.hold = [jnp.zeros_like(value)]
            elif self.pairs:
                self.came = [exchange(value, "dp", 1 + hop)] if hop < 2 else []
            else:
                pairs = ([(0, 1), (3, 2)], [(1, 2), (2, 1)], [(1, 0), (2, 3)])[hop]
                self.came = [lax.ppermute(value, "dp", pairs)]

        return stack_sums, ins, dims, then

    def finish(self):
        def then(outs):
            self.hold, self.came = list(outs), []

        if not self.chain or self.pairs:
            return self.dp(2)[:3] + (then,)
        return from_middle, self.hold + self.came, [self.hold[0].shape], then


def choose(line, ff1, ff0, ff0_came, at1, at0, at0_came, ff_own, ff_send, at_own, at_send, *, chain):
    z = line[line.shape[0] - 1]
    inner = (z == 1) | (z == 2)
    for sec in range(2):
        targets = (ff_own, at_own, ff_send, at_send) if sec == 0 else (ff_send, at_send, ff_own, at_own)

        @pl.when(line[0] == sec)
        def _(targets=targets):
            if chain:

                @pl.when(inner)
                def _():
                    targets[0][...] = ff0[...]

                @pl.when(jnp.logical_not(inner))
                def _():
                    targets[0][...] = ff0_came[...]
            else:
                targets[0][...] = total(ff0[...], ff0_came[...])
            targets[1][...] = total(at0[...], at0_came[...])
            targets[2][...] = ff1[...]
            targets[3][...] = at1[...]


def run_choose(line, ff1, ff0, at1, at0):
    ff, at = shape(ff1.shape, BF16), shape(at1.shape, BF16)
    return pl.pallas_call(
        functools.partial(choose, chain=ff0.chain),
        out_shape=(ff, ff, at, at),
        in_specs=[SM] + [VM] * 6,
        out_specs=(VM,) * 4,
        compiler_params=params(24),
        name="choose",
    )(line, ff1, ff0.hold[0], ff0.came[0], at1, at0.hold[0], at0.came[0])


def unpack(place, ff_own, ff_given, at_own, at_given, gate, up, down, wq, wk, wv, wo, gain_attn, gain_ffn):
    rows = gate.shape[0]
    narrow = down.shape[1]

    def emit(half, part, value):
        wide = (gate, up)[half]
        for i in range(2):
            wide[:, 2 * i * narrow:(2 * i + 2) * narrow] = part[i * rows:(i + 1) * rows, :].astype(F32)
        top = 2 * half * rows
        down[top:top + rows, :] = part[2 * rows:, :narrow].astype(F32)
        down[top + rows:top + 2 * rows, :] = part[2 * rows:, narrow:].astype(F32)
        left, right = ((wq, wk), (wo, wv))[half]
        left[...] = value[:rows, :WIDTH].astype(F32)
        right[...] = value[:rows, WIDTH:].astype(F32)
        if half == 0:
            gains = value[rows:, :rows].astype(F32)
            gain_attn[...] = gains[:1]
            gain_ffn[...] = gains[1:2]

    for sec in range(2):

        @pl.when(place[0] == sec)
        def _(sec=sec):
            emit(sec, ff_own, at_own)
            emit(1 - sec, ff_given, at_given)


def run_unpack(place, ff_own, ff_given, at_own, at_given):
    rows, cols = ff_own.shape[0] // 3, ff_own.shape[1]
    return pl.pallas_call(
        unpack,
        out_shape=(
            shape((rows, 2 * cols), F32),
            shape((rows, 2 * cols), F32),
            shape((4 * rows, cols // 2), F32),
            shape((rows, WIDTH), F32),
            shape((rows, KVW), F32),
            shape((rows, KVW), F32),
            shape((rows, WIDTH), F32),
            shape((1, rows), F32),
            shape((1, rows), F32),
        ),
        in_specs=[SM] + [VM] * 4,
        out_specs=(VM,) * 9,
        compiler_params=params(32),
        name="unpack",
    )(place, ff_own, ff_given, at_own, at_given)


def local(
    tokens,
    cotangent,
    doc_lengths,
    w_query,
    w_key,
    w_value,
    w_out,
    w_gate,
    w_up,
    w_down,
    gain_attn,
    gain_ffn,
):
    sec = lax.axis_index("section")
    first_section = sec == 0
    count = tokens.shape[2]
    place = jnp.stack([jnp.asarray(i, jnp.int32) for i in [sec] + piece_places()])
    line = jnp.concatenate([place, lax.axis_index("dp").astype(jnp.int32)[None]])
    rows, cols = w_query.shape[1], w_query.shape[2] + w_key.shape[2]
    own_at, rest_at = run_pack(
        pack_first, "pack_first", (2 * rows + EXTRA, cols),
        w_query[0], w_key[0], w_value[0], w_out[0], gain_attn, gain_ffn, w_down[0].T,
    )
    w_gate, own_at, rest_at = tie(w_gate, own_at, rest_at)
    own_ff, rest_ff = run_pack(pack_second, "pack_second", (2 * rows, cols), w_gate[0], w_up[0])

    def own_pieces(own, rest):
        came_own, came_rest = swap(rest), swap(own)
        home = [own, came_own, rest, came_rest]
        return home, jnp.where(first_section, own, came_own), jnp.where(first_section, came_own, own)

    at_home, at_zero, at_one = own_pieces(own_at, rest_at)
    ff_home, ff_zero, ff_one = own_pieces(own_ff, rest_ff)
    tables = make_tables(pick(doc_lengths[0], sec, 0), count)
    at_zero, tokens, cotangent = tie(at_zero, tokens, cotangent)
    x0 = jnp.swapaxes(pick(tokens[0], sec, 0), 0, 1)
    dy1 = jnp.swapaxes(pick(cotangent[0], sec, 0), 0, 1)

    near_at0 = first_hop(at_zero)
    near_ff0 = first_hop(ff_zero)
    near_at0, ff_one, x0, dy1, *tables = tie(near_at0, ff_one, x0, dy1, *tables)
    at0 = second_hop(near_at0)
    near_ff0, at_one, ff_one, *at0 = tie(near_ff0, at_one, ff_one, *at0)
    ff0 = second_hop(near_ff0)
    near_at1 = first_hop(at_one)
    near_ff1 = first_hop(ff_one)
    at0 = shared(at0)
    mid0, *saved0, gains0 = run_attention_forward(0, place, tables, x0, at_home + at0)
    mid0, near_at1, *ff0 = tie(mid0, near_at1, *ff0)

    ff0 = shared(ff0)
    at1 = second_hop(near_at1)
    y0, gate0, up0 = run_feed_forward(0, place, mid0, gains0, at_home + at0 + ff_home + ff0)
    y0, near_ff1, *at1 = tie(y0, near_ff1, *at1)

    at1 = shared(at1)
    ff1 = second_hop(near_ff1)
    mid1, *saved1, gains1 = run_attention_forward(1, place, tables, y0, at_home + at1)
    mid1, *ff1 = tie(mid1, *ff1)
    ff1 = shared(ff1)
    hidden1, d_mid1, g_ffn1, ff_keep1, ff_send1 = run_feed_forward(
        1, place, mid1, gains1, at_home + at1 + ff_home + ff1, dy_t=dy1
    )

    sums = []

    def after(waited, *others):
        cells = [(one.came, i) for one, i in waited]
        for one in sums:
            cells += [(one.hold, i) for i in range(len(one.hold))]
        held = list(tie(*others, *[array[i] for array, i in cells]))
        for (array, i), value in zip(cells, held[len(others):]):
            array[i] = value
        return held[:len(others)]

    def both_rows(own0, own1):
        back = swap(jnp.where(first_section, own1, own0))
        both = jnp.where(first_section, jnp.stack([own0, back]), jnp.stack([back, own1]))
        return jnp.swapaxes(both, 1, 2)[None, None]

    ff_cut, at_cut = ff_keep1.shape[1] // 32 * 16, (rows + EXTRA) // 32 * 16
    f1 = Sum(ff_keep1, ff_send1, ff_cut)
    sums.append(f1)
    dx1, dy0, at_keep1, at_send1 = run_attention_backward(
        1, place, tables, y0, gains1, d_mid1, g_ffn1, saved1, at_home + at1
    )
    dy0, at_keep1, at_send1 = after([(f1, 0)], dy0, at_keep1, at_send1)

    f1.fsdp_first_large(place)
    a1 = Sum(at_keep1, at_send1, at_cut)
    sums.append(a1)
    (dy0,) = after([], dy0)
    d_mid0, g_ffn0, ff_keep0, ff_send0 = run_feed_forward(
        0, place, mid0, gains0, at_home + at0 + ff_home + ff0, dy_t=dy0, kept=(gate0, up0)
    )
    d_mid0, ff_keep0, ff_send0 = after([(f1, 0), (f1, 1), (a1, 0)], d_mid0, ff_keep0, ff_send0)

    f0 = Sum(ff_keep0, ff_send0, ff_cut)
    sums.append(f0)
    run_work(line, [f1.fsdp_second(), a1.fsdp_first()])
    (d_mid0,) = after([], d_mid0)
    d_qk0, d_v0 = run_attention_scores_backward(0, place, tables, d_mid0, saved0, at_home + at0)
    d_qk0, d_v0 = after([(f0, 0), (f1, 0), (f1, 1), (a1, 0), (a1, 1)], d_qk0, d_v0)

    f0.fsdp_first_away(place)
    after([])
    run_work(line, [f1.dp(0), a1.fsdp_second()])
    (d_qk0,) = after([], d_qk0)
    dx0, _, at_keep0, at_send0 = run_attention_weights_backward(
        0, place, x0, gains0, d_mid0, g_ffn0, saved0, d_qk0, d_v0, at_home + at0
    )
    f0.fsdp_first_hold(place)
    at_send0, at_keep0 = after([(f0, 0), (f0, 1), (f1, 0), (a1, 0), (a1, 1)], at_send0, at_keep0)

    a0 = Sum(at_keep0, at_send0, at_cut, True)
    sums.append(a0)
    run_work(line, [f0.fsdp_second(), f1.dp(1)])
    after([(a0, 0)])
    run_work(line, [a0.fsdp_first(), a1.dp(0)])
    dx0, dx1, hidden1 = after([(f0, 0), (f0, 1), (f1, 0), (a1, 0), (a0, 0), (a0, 1)], dx0, dx1, hidden1)

    run_work(line, [f0.dp(0), f1.dp(2), a1.dp(1), a0.fsdp_second()])
    y1 = run_feed_forward_result(1, place, mid1, hidden1, at_home + at1)
    dx0, dx1, y1 = after([(f0, 0), (f1, 0), (a1, 0), (a0, 0), (a0, 1)], dx0, dx1, y1)

    run_work(line, [f0.dp(1), a1.dp(2), a0.dp(0), f1.finish()])
    dx0, dx1 = after([], dx0, dx1)
    grad = both_rows(dx0, dx1)
    (grad,) = after([(a0, 0)], grad)
    run_work(line, [a0.dp(1)])
    (grad,) = after([(f0, 0), (a1, 0)], grad)

    run_work(line, [f0.dp(2), a1.finish()])
    y0, y1 = after([], y0, y1)
    out = both_rows(y0, y1)
    (out,) = after([(f0, 0), (a0, 0)], out)

    ff_own, ff_send, at_own, at_send = run_choose(line, f1.hold[0], f0, a1.hold[0], a0)
    gate, up, down, wq, wk, wv, wo, gain_attn, gain_ffn = run_unpack(place, ff_own, swap(ff_send), at_own, swap(at_send))

    return (
        out,
        grad,
        wq[None],
        wk[None],
        wv[None],
        wo[None],
        gate[None],
        up[None],
        down.T[None],
        gain_attn,
        gain_ffn,
    )


def solution(mesh):
    whole = P(("fsdp", "dp"), None, None, None)
    weight = P("section", "fsdp", None)
    gain = P("section", "fsdp")
    rows = P("section", ("fsdp", "dp"), None, None, None)
    in_specs = (whole, whole, P(("fsdp", "dp"), None, None)) + (weight,) * 7 + (gain,) * 2
    out_specs = (rows, rows) + (weight,) * 7 + (gain,) * 2
    return jax.shard_map(local, mesh=mesh, in_specs=in_specs, out_specs=out_specs, check_vma=False)
```
